512 devices in a mesh: pix: 64 (over z_lo, y, core), day: 8 (over x, z_hi).
Axes of the slice: x: 4, y: 8, z: 8 (z_hi: 2, z_lo: 4; z = z_hi * 4 + z_lo), core: 2. Of those that a mesh axis runs over, the one named last changes fastest.
Arguments:
- observed: float32 [1024, 512, 256], P('day', 'pix'), may hold values from -6 to 6
- missing: int32 [1024, 512, 256], P('day', 'pix'), may hold values 0 or 1
- land: int32 [512, 256], P('pix'), may hold values 0 or 1
- basis_start: float32 [1024, 32], P('day'), may hold values from -0.1875 to 0.1875
- day_weights: float32 [1024, 7], P('day'), may hold values from 0.05 to 0.4
Outputs:
- filled: float32 [1024, 512, 256], P('day', 'pix')
- basis: float32 [1024, 32], P('day')
The draws below stay inside these ranges and needn't reach their ends.
All inputs are finite; a program needn't handle non-finite values. No bound on the sum of `missing` or of `land` on one device may be relied on, other than what follows from the above.
Results may differ from the reference program's by a relative error of at most 0.0001.
Values sent between devices are 32-bit elements; how exact they have to be, the bound alone decides.
No kernel may reach another device: no remote copies, remote signals or barrier semaphores. Data moves between devices by JAX's collectives and lax.ppermute only.
A program may use at most 64 MiB of HBM per device.

```python
import math
import jax
import jax.numpy as jnp
from jax import lax

GRID_COLS = 256
K = 32
ITERS = 2
RADIUS = 3
TAPS = 7
DAYS = 1024
GRID_ROWS = 512


def with_ends(values, key, least, top_value):
    shape = values.shape
    spot = [jax.random.randint(jax.random.fold_in(key, axis), (), 0, shape[axis]) for axis in range(len(shape))]
    values = values.at[tuple(spot)].set(least)
    longest = shape.index(max(shape))
    spot[longest] = (spot[longest] + 1) % shape[longest]
    return values.at[tuple(spot)].set(top_value)


def shard_levels(key, dims, pieces, least, high):
    level = 1.0
    for axis_at, parts in pieces:
        draws = jax.random.uniform(jax.random.fold_in(jax.random.fold_in(key, 6), axis_at), (parts,), jnp.float32, least / len(pieces), high / len(pieces))
        level = level * jnp.repeat(jnp.exp(draws), dims[axis_at] // parts).reshape((-1,) + (1,) * (len(dims) - 1 - axis_at))
    return level


def scatter_about(own_key, shape, deviation, reach, pieces=(), kind=jnp.bfloat16):
    result = deviation * jax.random.normal(own_key, shape, jnp.float32)
    if pieces:
        result = result * shard_levels(own_key, shape, pieces, -0.22, 0.18)
    return jnp.clip(result, -reach, reach).astype(kind)


def setup_inputs(seed: int = 0) -> dict:
    key_list = jax.random.split(jax.random.key(seed), 6)
    observed = scatter_about(key_list[0], (DAYS, GRID_ROWS, GRID_COLS), 1.0, 6.0, ((0, 8), (1, 64)), jnp.float32)
    missing = with_ends((jax.random.randint(key_list[1], (DAYS, GRID_ROWS, GRID_COLS), 0, 10) < 3).astype(jnp.int32), jax.random.fold_in(key_list[1], 1), 0, 1)
    land = with_ends((jax.random.randint(key_list[2], (GRID_ROWS, GRID_COLS), 0, 5) < 1).astype(jnp.int32), jax.random.fold_in(key_list[2], 1), 0, 1)
    basis_start = scatter_about(key_list[3], (DAYS, K), DAYS ** -0.5, 0.1875, ((0, 8),), jnp.float32)
    day_weights = jnp.clip(jnp.exp(math.log(0.4) - 2.0794415 * jax.random.uniform(key_list[4], (DAYS, TAPS), jnp.float32) ** shard_levels(key_list[4], (DAYS, TAPS), ((0, 8),), -0.2, 0.2)), 0.05, 0.4)
    return {"observed": observed, "missing": missing, "land": land, "basis_start": basis_start, "day_weights": day_weights}


exact = lax.Precision.HIGHEST
smoothing = 0.2

def lower_solve(factor, right):
    return lax.linalg.triangular_solve(factor, right, left_side=True, lower=True)

def reference(observed, missing, land, basis_start, day_weights):
    ocean = (1 - land).astype(jnp.float32)
    ocean_flat = ocean.reshape(-1)
    observed_flat = observed.reshape(DAYS, -1)
    absent = missing.reshape(DAYS, -1) == 1
    filled = jnp.where(absent, jnp.float32(0.0), observed_flat) * ocean_flat
    basis = basis_start
    ocean_pad = jnp.pad(ocean, 1)
    for sweep in range(ITERS):
        modes_u = jnp.dot(basis.T, filled, precision=exact)
        gram_u = jnp.dot(modes_u, modes_u.T, precision=exact)
        factor = jnp.linalg.cholesky(gram_u)
        modes_q = lower_solve(factor, modes_u)
        weights_w = jnp.dot(filled, modes_q.T, precision=exact)
        recon = jnp.dot(weights_w, modes_q, precision=exact)
        padded = jnp.pad(recon, ((RADIUS, RADIUS), (0, 0)))
        tempered = sum((day_weights[:, j:j + 1] * padded[j:j + DAYS] for j in range(TAPS)))
        surface = tempered.reshape(DAYS, GRID_ROWS, GRID_COLS)
        widened = jnp.pad(surface, ((0, 0), (1, 1), (1, 1)))
        pairs = [(widened[:, :-2, 1:-1], ocean_pad[:-2, 1:-1]), (widened[:, 2:, 1:-1], ocean_pad[2:, 1:-1]), (widened[:, 1:-1, :-2], ocean_pad[1:-1, :-2]), (widened[:, 1:-1, 2:], ocean_pad[1:-1, 2:])]
        spread_sum = sum((flag * (value - surface) for value, flag in pairs))
        smooth = surface + smoothing * spread_sum
        filled = jnp.where(absent, smooth.reshape(DAYS, -1), observed_flat) * ocean_flat
        gram_w = jnp.dot(weights_w.T, weights_w, precision=exact)
        factor_w = jnp.linalg.cholesky(gram_w)
        basis = lower_solve(factor_w, weights_w.T).T
    return (filled.reshape(DAYS, GRID_ROWS, GRID_COLS), basis)
```

```python
import jax
import jax.numpy as jnp
from jax import lax
from jax.sharding import Mesh, PartitionSpec as P

ITERS = 2
RADIUS = 3
K = 32

PIX = ("zlo", "y", "core")
DAY = ("x", "zhi")
NEAR = ("zlo", "core")

exact = lax.Precision.HIGHEST
smoothing = 0.2


def swap(blocks, axes):
    return lax.all_to_all(blocks, axes, 0, 0)


def to_all(block, axes, count):
    return swap(jnp.broadcast_to(block[None], (count,) + block.shape), axes)


def neighbours(low_edge, high_edge, axes, count):
    up = [(i, i + 1) for i in range(count - 1)]
    down = [(i + 1, i) for i in range(count - 1)]
    return lax.ppermute(high_edge, axes, up), lax.ppermute(low_edge, axes, down)


def contract(expr, a, b):
    return jnp.einsum(expr, a, b, precision=exact)


def inverse_factor(gram):
    factor = jnp.linalg.cholesky(gram)
    eye = jnp.eye(K, dtype=jnp.float32)
    return lax.linalg.triangular_solve(factor, eye, left_side=True, lower=True)


def per_device(observed, missing, land, basis_start, day_weights):
    days, rows, cols = observed.shape
    ocean = (1 - land).astype(jnp.float32)
    ocean_low, ocean_high = neighbours(ocean[:1], ocean[-1:], PIX, 64)
    zero_col = jnp.zeros((rows, 1), jnp.float32)
    flags = [
        jnp.concatenate([ocean_low, ocean[:-1]], 0),
        jnp.concatenate([ocean[1:], ocean_high], 0),
        jnp.concatenate([zero_col, ocean[:, :-1]], 1),
        jnp.concatenate([ocean[:, 1:], zero_col], 1),
    ]
    centre = 1.0 - smoothing * sum(flags)

    absent = missing == 1
    first = (jnp.where(absent, jnp.float32(0.0), observed) * ocean).transpose(1, 0, 2)
    gap = (absent.astype(jnp.float32) * ocean).transpose(1, 0, 2)

    filled = first
    weights_t = basis_start.T
    gram = None
    for sweep in range(ITERS):
        halo_low, halo_high = neighbours(
            filled[:, :RADIUS], filled[:, -RADIUS:], DAY, 8
        )
        part = contract("kd,rdc->rkc", weights_t, filled)
        if gram is None:
            modes = swap(part, DAY).sum(0)
        else:
            wide = jnp.pad(gram, ((0, 0), (0, 128 - K)))
            both = jnp.concatenate(
                [part, jnp.broadcast_to(wide[None], (8, K, 128))], axis=2
            )
            both = swap(both, DAY).sum(0)
            factor = inverse_factor(both[:, cols : cols + K])
            modes = jnp.dot(factor, both[:, :cols], precision=exact)
        modes_u = to_all(modes, DAY, 8)

        row_low, row_high = neighbours(modes_u[0], modes_u[-1], PIX, 64)
        ext = jnp.concatenate([halo_low, filled, halo_high], axis=1)
        raw = contract("rkc,rdc->kd", modes_u, ext)
        gram_u = contract("rkc,rlc->kl", modes_u, modes_u)
        joint = jnp.concatenate([gram_u, raw], axis=1).reshape(-1)
        size = joint.shape[0]
        joint = jnp.pad(joint, (0, -size % 1024)).reshape(-1, 128)
        joint = to_all(joint, NEAR, 8).sum(0)
        joint = to_all(joint, "y", 8).sum(0)
        joint = joint.reshape(-1)[:size].reshape(K, -1)

        inv_u = inverse_factor(joint[:, :K])
        wide_t = jnp.dot(inv_u, joint[:, K:], precision=exact)
        weights_t = wide_t[:, RADIUS : RADIUS + days]
        mixed = sum(
            day_weights[:, j][None] * wide_t[:, j : j + days]
            for j in range(2 * RADIUS + 1)
        )
        mixed = jnp.dot(inv_u.T, mixed, precision=exact)

        above = jnp.concatenate([row_low[None], modes_u[:-1]], 0)
        below = jnp.concatenate([modes_u[1:], row_high[None]], 0)
        left = jnp.pad(modes_u[:, :, :-1], ((0, 0), (0, 0), (1, 0)))
        right = jnp.pad(modes_u[:, :, 1:], ((0, 0), (0, 0), (0, 1)))
        smooth = centre[:, None] * modes_u + smoothing * sum(
            flag[:, None] * value
            for flag, value in zip(flags, (above, below, left, right))
        )
        gram = jnp.dot(weights_t, weights_t.T, precision=exact)
        if sweep + 1 < ITERS:
            filled = first + gap * contract("kd,rkc->rdc", mixed, smooth)
        else:
            surface = contract("kd,rkc->drc", mixed, smooth)
            filled = jnp.where(absent, surface, observed) * ocean
    gram = to_all(gram, DAY, 8).sum(0)
    basis = jnp.dot(inverse_factor(gram), weights_t, precision=exact).T
    return filled, basis


def solution(mesh):
    fine = Mesh(
        mesh.devices.reshape(4, 8, 2, 4, 2), ("zlo", "y", "core", "x", "zhi")
    )
    return jax.shard_map(
        per_device,
        mesh=fine,
        in_specs=(
            P(DAY, PIX, None),
            P(DAY, PIX, None),
            P(PIX, None),
            P(DAY, None),
            P(DAY, None),
        ),
        out_specs=(P(DAY, PIX, None), P(DAY, None)),
        check_vma=False,
    )
```

```python
import jax
import jax.numpy as jnp
from jax import lax
from jax.experimental import pallas as pl
from jax.experimental.pallas import tpu as pltpu
from jax.sharding import Mesh, PartitionSpec as P

RADIUS = 3
K = 32
LANES = 128
HALO = 8 * RADIUS

PIX = ("zlo", "y", "core")
DAY = ("x", "zhi")
NEAR = ("zlo", "core")
SIZES = (4, 8, 2, 4, 2)

exact = lax.Precision.HIGHEST
smoothing = 0.2
f32 = jnp.float32


def mul(a, b):
    return lax.dot_general(
        a, b, (((1,), (0,)), ((), ())), precision=exact, preferred_element_type=f32
    )


def mul_t(a, b):
    return lax.dot_general(
        a, b, (((1,), (1,)), ((), ())), precision=exact, preferred_element_type=f32
    )


def inverse_factor(wide):
    row = lax.broadcasted_iota(jnp.int32, (K, LANES), 0)
    lane = lax.broadcasted_iota(jnp.int32, (K, LANES), 1)
    work = jnp.where(lane < K, wide, jnp.where(lane == row + K, f32(1.0), f32(0.0)))
    below = row[:, :1]
    for k in range(K):
        pivot_row = work[k : k + 1, :]
        pivot_row = pivot_row * (1.0 / pivot_row[:, k : k + 1])
        column = jnp.where(below > k, work[:, k : k + 1], f32(0.0))
        work = work - column * pivot_row
    pivots = jnp.sum(jnp.where(lane == row, work, f32(0.0)), axis=1, keepdims=True)
    work = work * (1.0 / jnp.sqrt(pivots))
    return pltpu.roll(work, LANES - K, 1)[:, :K]


def unpack_gram(packed):
    return jnp.concatenate(
        [packed] + [pltpu.roll(packed, LANES - K * a, 1) for a in range(1, 4)], axis=0
    )


def pack_gram(weights_t):
    wide = mul_t(
        weights_t,
        jnp.concatenate([weights_t, jnp.zeros((LANES - K, LANES), f32)], axis=0),
    )
    packed = wide[:8]
    for a in range(1, 4):
        packed = packed + pltpu.roll(wide[8 * a : 8 * a + 8], K * a, 1)
    return packed


def call(body, outs, args, scratch=(), flops=1_000_000, moved=1_000_000):
    specs = [
        pl.BlockSpec(memory_space=pltpu.SMEM if a.ndim == 1 else pltpu.VMEM)
        for a in args
    ]
    many = isinstance(outs, list)
    shapes = [jax.ShapeDtypeStruct(s, f32) for s in (outs if many else [outs])]
    out_specs = [pl.BlockSpec(memory_space=pltpu.VMEM) for _ in shapes]
    return pl.pallas_call(
        body,
        out_shape=shapes if many else shapes[0],
        in_specs=specs,
        out_specs=out_specs if many else out_specs[0],
        scratch_shapes=list(scratch),
        compiler_params=pltpu.CompilerParams(vmem_limit_bytes=24 * 1024 * 1024),
        cost_estimate=pl.CostEstimate(
            flops=flops, bytes_accessed=moved, transcendentals=0
        ),
    )(*args)


def rows_of(halves, start, size):
    return jnp.concatenate(
        [half[pl.ds(start, size, stride=8), :] for half in halves], axis=1
    )


def start_body(day, observed, missing, land, basis_t, first, out, *halves):
    d = day[0]
    out[:, K:, :] = jnp.zeros((8, HALO, out.shape[2]), f32)
    ocean = 1.0 - land[...].astype(f32)
    low, high = jnp.maximum(d - 1, 0), jnp.minimum(d + 1, 7)
    days = first.shape[1]
    for c, half in enumerate(halves):
        at = slice(LANES * c, LANES * c + LANES)
        tile = jnp.where(missing[:, :, at] == 1, f32(0.0), observed[:, :, at])
        half[...] = (tile * ocean[None, :, at]).reshape(8 * days, LANES)
    for t in range(RADIUS):
        for target, source in ((low, t), (high, days - RADIUS + t)):
            tile = [half[8 * source : 8 * source + 8, :] for half in halves]
            out[target, K + 8 * t : K + 8 * t + 8, :] = jnp.concatenate(tile, axis=1)
    weights_t = basis_t[...]
    for r in range(8):
        filled = rows_of(halves, r, days)
        first[r] = filled
        out[r, :K, :] = mul(weights_t, filled)


def add_rows_body(arrived, out):
    total = arrived[0, :K, :]
    for j in range(1, arrived.shape[0]):
        total = total + arrived[j, :K, :]
    for j in range(out.shape[0]):
        out[j] = total


def add_all_body(arrived, out):
    total = arrived[0]
    for j in range(1, arrived.shape[0]):
        total = total + arrived[j]
    for j in range(out.shape[0]):
        out[j] = total


def factor_body(arrived, out):
    packed = arrived[0, K + HALO :, :LANES]
    for j in range(1, arrived.shape[0]):
        packed = packed + arrived[j, K + HALO :, :LANES]
    out[:, :K] = inverse_factor(unpack_gram(packed))
    out[:, K:] = jnp.zeros((K, LANES - K), f32)


def project_body(day, arrived, modes, filled, land, *rest):
    *factor, out, edge_low, edge_high, halo_0, halo_1 = rest
    scale = factor[0][:, :K] if factor else None
    d = day[0]
    low = arrived[jnp.maximum(d - 1, 0), K : K + HALO, :]
    high = arrived[jnp.minimum(d + 1, 7), K : K + HALO, :]
    low = jnp.where(d > 0, low, f32(0.0))
    high = jnp.where(d < 7, high, f32(0.0))
    cols = modes.shape[2]
    for c, halo in enumerate((halo_0, halo_1)):
        halo[:HALO, :] = low[:, LANES * c : LANES * c + LANES]
        halo[HALO : 2 * HALO, :] = high[:, LANES * c : LANES * c + LANES]
        halo[2 * HALO :, :] = jnp.zeros((64 - 2 * HALO, LANES), f32)
    pad = jnp.zeros((LANES - K - 8, cols), f32)
    total = jnp.zeros((K, 2 * LANES), f32)
    for r in range(8):
        modes_u = modes[r] if scale is None else mul(scale, modes[r])
        days_near = rows_of((halo_0, halo_1), r, 8)
        right = jnp.concatenate([filled[r], modes_u, days_near, pad], axis=0)
        total = total + mul_t(modes_u, right)
    extra = total[:, LANES:]
    packed = extra[:16] + pltpu.roll(extra[16:], 64, 1)
    for j in range(out.shape[0]):
        out[j, :K, :] = total[:, :LANES]
        out[j, K:, :] = packed
    ocean = 1.0 - land[...].astype(f32)
    for edge, r in ((edge_low, 0), (edge_high, 7)):
        edge[:K, :] = modes[r]
        edge[K:, :] = jnp.broadcast_to(ocean[r : r + 1], (8, cols))


def smooth_body(modes, above, below, land, out):
    cols = out.shape[2]
    lane = lax.broadcasted_iota(jnp.int32, (1, cols), 1)
    ocean = 1.0 - land[...].astype(f32)
    rows = [above[:K, :]] + [modes[r] for r in range(8)] + [below[:K, :]]
    flags = (
        [above[K : K + 1, :]]
        + [ocean[r : r + 1] for r in range(8)]
        + [below[K : K + 1, :]]
    )
    for r in range(8):
        here, flag = rows[r + 1], flags[r + 1]
        left = jnp.where(lane > 0, pltpu.roll(flag, 1, 1), f32(0.0))
        right = jnp.where(lane < cols - 1, pltpu.roll(flag, cols - 1, 1), f32(0.0))
        up, down = flags[r], flags[r + 2]
        centre = 1.0 - smoothing * (up + down + left + right)
        spread = (
            up * rows[r]
            + down * rows[r + 2]
            + left * pltpu.roll(here, 1, 1)
            + right * pltpu.roll(here, cols - 1, 1)
        )
        out[r] = centre * here + smoothing * spread


def weights_of(arrived, band, scale):
    total = arrived[0]
    for j in range(1, arrived.shape[0]):
        total = total + arrived[j]
    extra = jnp.concatenate([total[K:], pltpu.roll(total[K:], 64, 1)], axis=0)
    factor = inverse_factor(extra)
    wide = mul(factor, jnp.concatenate([total[:K], extra], axis=1))
    tempered = mul(wide, band[...])
    right = factor if scale is None else mul(factor, scale)
    return wide[:, :LANES], mul(tempered.T, right)


def refill_body(day, arrived, band, smooth, first, gap, land, filled, out):
    weights_t, mixed = weights_of(arrived, band, None)
    d = day[0]
    low, high = jnp.maximum(d - 1, 0), jnp.minimum(d + 1, 7)
    days, cols = filled.shape[1:]
    out[:, K:, :] = jnp.zeros((8, HALO + 8, cols), f32)
    packed = pack_gram(weights_t)
    for j in range(8):
        out[j, K + HALO :, :LANES] = packed
    ocean = 1.0 - land[...].astype(f32)
    for r in range(8):
        surface = mul(mixed, smooth[r])
        now = jnp.where(gap[r] == 1, surface * ocean[r : r + 1], first[r])
        filled[r] = now
        out[r, :K, :] = mul(weights_t, now)
        for t in range(RADIUS):
            at = K + 8 * t + r
            out[low, at : at + 1, :] = now[t : t + 1]
            out[high, at : at + 1, :] = now[days - RADIUS + t : days - RADIUS + t + 1]


def last_weights_body(arrived, band, scale, weights, mixed, out):
    weights_t, mix = weights_of(arrived, band, scale[:, :K])
    weights[...] = weights_t
    mixed[...] = mix
    packed = pack_gram(weights_t)
    for j in range(out.shape[0]):
        out[j] = packed


def last_fill_body(mixed, smooth, observed, missing, land, out, *halves):
    days = observed.shape[0]
    ocean = 1.0 - land[...].astype(f32)
    mix = mixed[...]
    for r in range(8):
        surface = mul(mix, smooth[r])
        for c, half in enumerate(halves):
            half[pl.ds(r, days, stride=8), :] = surface[:, LANES * c : LANES * c + LANES]
    for c, half in enumerate(halves):
        at = slice(LANES * c, LANES * c + LANES)
        surface = half[...].reshape(days, 8, LANES)
        value = jnp.where(missing[:, :, at] == 1, surface, observed[:, :, at])
        out[:, :, at] = value * ocean[None, :, at]


def basis_body(arrived, weights, out):
    packed = arrived[0]
    for j in range(1, arrived.shape[0]):
        packed = packed + arrived[j]
    factor = inverse_factor(unpack_gram(packed))
    out[...] = mul(factor, weights[...]).T


def swap(blocks, axes):
    return lax.all_to_all(blocks, axes, 0, 0)


def near_rows(edge_low, edge_high):
    count = lax.axis_size(PIX)
    up = [(i, i + 1) for i in range(count - 1)]
    down = [(i + 1, i) for i in range(count - 1)]
    return lax.ppermute(edge_high, PIX, up), lax.ppermute(edge_low, PIX, down)


def band_of(day_weights):
    days = day_weights.shape[0]
    slot = lax.broadcasted_iota(jnp.int32, (2 * LANES, days), 0)
    target = lax.broadcasted_iota(jnp.int32, (2 * LANES, days), 1)
    first = LANES + K
    source = jnp.where(slot < days, slot, 4 * days)
    source = jnp.where((slot >= first) & (slot < first + 3), slot - first - 3, source)
    source = jnp.where(
        (slot >= first + 3) & (slot < first + 6), slot - first - 3 + days, source
    )
    taps = day_weights.T
    return sum(
        jnp.where(source - target + RADIUS == j, taps[j : j + 1], f32(0.0))
        for j in range(2 * RADIUS + 1)
    )


def per_device(observed, missing, land, basis_start, day_weights):
    days, rows, cols = observed.shape
    day = lax.axis_index(DAY).reshape(1)
    near, far = lax.axis_size(NEAR), lax.axis_size("y")
    band = band_of(day_weights)

    def sum_over_pixels(joint, edges):
        joint = swap(joint, NEAR)
        joint = call(add_all_body, (far, K + 16, LANES), (joint,))
        joint, *edges = lax.optimization_barrier((joint, *edges))
        return swap(joint, "y"), near_rows(*edges)

    halo = [pltpu.VMEM((64, LANES), f32)] * 2
    halves = [pltpu.VMEM((days * rows, LANES), f32)] * 2
    edge = (K + 8, cols)
    joint_shape = (near, K + 16, LANES)
    block = (rows, K, cols)

    first, part = call(
        start_body,
        [(rows, days, cols), (rows, K + HALO, cols)],
        (day, observed, missing, land, basis_start.T),
        halves,
    )
    gap, part = lax.optimization_barrier((missing, part))
    gap = gap.transpose(1, 0, 2)
    arrived = swap(part, DAY)
    modes = swap(call(add_rows_body, block, (arrived,)), DAY)
    joint, *edges = call(
        project_body,
        [joint_shape, edge, edge],
        (day, arrived, modes, first, land),
        halo,
    )
    joint, (above, below) = sum_over_pixels(joint, edges)
    smooth = call(smooth_body, block, (modes, above, below, land))
    filled, part = call(
        refill_body,
        [(rows, days, cols), (rows, K + HALO + 8, cols)],
        (day, joint, band, smooth, first, gap, land),
    )
    arrived = swap(part, DAY)
    modes = swap(call(add_rows_body, block, (arrived,)), DAY)
    factor = call(factor_body, (K, LANES), (arrived,))
    joint, *edges = call(
        project_body,
        [joint_shape, edge, edge],
        (day, arrived, modes, filled, land, factor),
        halo,
    )
    joint, (above, below) = sum_over_pixels(joint, edges)
    smooth = call(smooth_body, block, (modes, above, below, land))
    weights, mixed, gram = call(
        last_weights_body,
        [(K, LANES), (days, K), (8, 8, LANES)],
        (joint, band, factor),
    )
    gram = swap(gram, DAY)
    filled = call(
        last_fill_body,
        (days, rows, cols),
        (mixed, smooth, observed, missing, land),
        halves,
    )
    basis = call(basis_body, (days, K), (gram, weights))
    return filled, basis


def solution(mesh):
    fine = Mesh(mesh.devices.reshape(SIZES), ("zlo", "y", "core", "x", "zhi"))
    return jax.shard_map(
        per_device,
        mesh=fine,
        in_specs=(
            P(DAY, PIX, None),
            P(DAY, PIX, None),
            P(PIX, None),
            P(DAY, None),
            P(DAY, None),
        ),
        out_specs=(P(DAY, PIX, None), P(DAY, None)),
        check_vma=False,
    )
```

```python
import jax
import jax.numpy as jnp
from jax import lax
from jax.experimental import pallas as pl
from jax.experimental.pallas import tpu as pltpu
from jax.sharding import Mesh, PartitionSpec as P

RADIUS = 3
K = 32
LANES = 128
HALO = 8 * RADIUS

PIX = ("zlo", "y", "core")
DAY = ("x", "zhi")
NEAR = ("zlo", "core")
SIZES = (4, 8, 2, 4, 2)

exact = lax.Precision.HIGHEST
smoothing = 0.2
f32 = jnp.float32


def mul(a, b):
    return lax.dot_general(
        a, b, (((1,), (0,)), ((), ())), precision=exact, preferred_element_type=f32
    )


def mul_t(a, b):
    return lax.dot_general(
        a, b, (((1,), (1,)), ((), ())), precision=exact, preferred_element_type=f32
    )


def inverse_factor(wide):
    row = lax.broadcasted_iota(jnp.int32, (K, LANES), 0)
    lane = lax.broadcasted_iota(jnp.int32, (K, LANES), 1)
    work = jnp.where(lane < K, wide, jnp.where(lane == row + K, f32(1.0), f32(0.0)))
    done = []
    for start in range(0, K, 8):
        size = K - start
        at = lax.broadcasted_iota(jnp.int32, (size, LANES), 0)
        spread = [
            jnp.broadcast_to(work[:, start + j : start + j + 1], (size, LANES))
            for j in range(8)
        ]
        for j in range(8):
            inverse = 1.0 / spread[j][j : j + 1, :]
            column = jnp.where(at > j, spread[j], f32(0.0))
            for l in range(j + 1, 8):
                spread[l] = spread[l] - column * (spread[l][j : j + 1, :] * inverse)
            work = work - column * (work[j : j + 1, :] * inverse)
        done.append(work[:8])
        work = work[8:]
    work = jnp.concatenate(done, axis=0)
    pivots = jnp.sum(jnp.where(lane == row, work, f32(0.0)), axis=1, keepdims=True)
    work = work * (1.0 / jnp.sqrt(pivots))
    return pltpu.roll(work, LANES - K, 1)[:, :K]


def unpack_gram(packed):
    return jnp.concatenate(
        [packed] + [pltpu.roll(packed, LANES - K * a, 1) for a in range(1, 4)], axis=0
    )


def pack_rows(wide):
    packed = wide[:8]
    for a in range(1, 4):
        packed = packed + pltpu.roll(wide[8 * a : 8 * a + 8], K * a, 1)
    return packed


def pack_gram(weights_t):
    rest = jnp.zeros((LANES - K, LANES), f32)
    return pack_rows(mul_t(weights_t, jnp.concatenate([weights_t, rest], axis=0)))


def total_of(arrived):
    total = arrived[0]
    for j in range(1, arrived.shape[0]):
        total = total + arrived[j]
    return total


def call(body, outs, args, scratch=(), limit=8, anywhere=(), alias=None, out_any=()):
    specs = []
    for i, a in enumerate(args):
        space = pltpu.SMEM if a.ndim == 1 else pltpu.VMEM
        specs.append(pl.BlockSpec(memory_space=pl.ANY if i in anywhere else space))
    many = isinstance(outs, list)
    shapes = [jax.ShapeDtypeStruct(s, f32) for s in (outs if many else [outs])]
    out_specs = [
        pl.BlockSpec(memory_space=pl.ANY if i in out_any else pltpu.VMEM)
        for i in range(len(shapes))
    ]
    return pl.pallas_call(
        body,
        out_shape=shapes if many else shapes[0],
        in_specs=specs,
        out_specs=out_specs if many else out_specs[0],
        scratch_shapes=list(scratch),
        input_output_aliases=alias or {},
        compiler_params=pltpu.CompilerParams(vmem_limit_bytes=limit * 1024 * 1024),
        cost_estimate=pl.CostEstimate(
            flops=1_000_000, bytes_accessed=1_000_000, transcendentals=0
        ),
    )(*args)


def rows_of(halves, start, size):
    return jnp.concatenate(
        [half[pl.ds(start, size, stride=8), :] for half in halves], axis=1
    )


def start_body(
    day,
    observed_hbm,
    missing_hbm,
    land_hbm,
    basis_hbm,
    first,
    out,
    observed,
    missing,
    land,
    basis_t,
    half_0,
    half_1,
    arrivals,
):
    pairs = (
        (missing_hbm, missing),
        (observed_hbm, observed),
        (land_hbm, land),
        (basis_hbm, basis_t),
    )
    copies = [
        pltpu.make_async_copy(source, target, arrivals.at[i])
        for i, (source, target) in enumerate(pairs)
    ]
    for copy in copies:
        copy.start()
    d = day[0]
    halves = (half_0, half_1)
    out[:, K:, :] = jnp.zeros((8, HALO, out.shape[2]), f32)
    for copy in copies:
        copy.wait()
    ocean = 1.0 - land[...].astype(f32)
    low, high = jnp.maximum(d - 1, 0), jnp.minimum(d + 1, 7)
    days = first.shape[1]
    for c, half in enumerate(halves):
        at = slice(LANES * c, LANES * c + LANES)
        tile = jnp.where(missing[:, :, at] == 1, f32(0.0), observed[:, :, at])
        half[...] = (tile * ocean[None, :, at]).reshape(8 * days, LANES)
    for t in range(RADIUS):
        for target, source in ((low, t), (high, days - RADIUS + t)):
            tile = [half[8 * source : 8 * source + 8, :] for half in halves]
            out[target, K + 8 * t : K + 8 * t + 8, :] = jnp.concatenate(tile, axis=1)
    weights_t = basis_t[...]
    for r in range(8):
        filled = rows_of(halves, r, days)
        first[r] = filled
        out[r, :K, :] = mul(weights_t, filled)


def add_rows_body(arrived, out):
    total = arrived[0, :K, :]
    for j in range(1, arrived.shape[0]):
        total = total + arrived[j, :K, :]
    for j in range(out.shape[0]):
        out[j] = total


def add_all_body(arrived, out):
    total = total_of(arrived)
    for j in range(out.shape[0]):
        out[j] = total


def add_last_body(arrived, out, extra):
    total = total_of(arrived)
    for j in range(out.shape[0]):
        out[j] = total[:K]
    extra[...] = total[K:]


def factor_body(arrived, out):
    packed = arrived[0, K:, :LANES]
    for j in range(1, arrived.shape[0]):
        packed = packed + arrived[j, K:, :LANES]
    out[:, :K] = inverse_factor(unpack_gram(packed))
    out[:, K:] = jnp.zeros((K, LANES - K), f32)


def edges_of(modes, land, edge_low, edge_high):
    ocean = 1.0 - land[...].astype(f32)
    for edge, r in ((edge_low, 0), (edge_high, 7)):
        edge[:K, :] = modes[r]
        edge[K:, :] = jnp.broadcast_to(ocean[r : r + 1], (8, ocean.shape[1]))


def project_again_body(modes, filled, land, factor, out, edge_low, edge_high):
    cols = modes.shape[2]
    scale = factor[:, :K]
    pad = jnp.zeros((LANES - K, cols), f32)
    total = jnp.zeros((K, 2 * LANES), f32)
    for r in range(8):
        modes_u = mul(scale, modes[r])
        right = jnp.concatenate([filled[r], modes_u, pad], axis=0)
        total = total + mul_t(modes_u, right)
    packed = pack_rows(total[:, LANES:])
    for j in range(out.shape[0]):
        out[j, :K, :] = total[:, :LANES]
        out[j, K:, :] = packed
    edges_of(modes, land, edge_low, edge_high)


def project_body(
    day, arrived, modes, filled, land, out, edge_low, edge_high, halo_0, halo_1
):
    d = day[0]
    low = arrived[jnp.maximum(d - 1, 0), K : K + HALO, :]
    high = arrived[jnp.minimum(d + 1, 7), K : K + HALO, :]
    low = jnp.where(d > 0, low, f32(0.0))
    high = jnp.where(d < 7, high, f32(0.0))
    cols = modes.shape[2]
    for c, halo in enumerate((halo_0, halo_1)):
        halo[:HALO, :] = low[:, LANES * c : LANES * c + LANES]
        halo[HALO : 2 * HALO, :] = high[:, LANES * c : LANES * c + LANES]
        halo[2 * HALO :, :] = jnp.zeros((64 - 2 * HALO, LANES), f32)
    pad = jnp.zeros((LANES - K - 8, cols), f32)
    total = jnp.zeros((K, 2 * LANES), f32)
    for r in range(8):
        modes_u = modes[r]
        days_near = rows_of((halo_0, halo_1), r, 8)
        right = jnp.concatenate([filled[r], modes_u, days_near, pad], axis=0)
        total = total + mul_t(modes_u, right)
    extra = total[:, LANES:]
    packed = extra[:16] + pltpu.roll(extra[16:], 64, 1)
    for j in range(out.shape[0]):
        out[j, :K, :] = total[:, :LANES]
        out[j, K:, :] = packed
    edges_of(modes, land, edge_low, edge_high)


def smooth_body(modes, above, below, land, out):
    cols = out.shape[2]
    lane = lax.broadcasted_iota(jnp.int32, (1, cols), 1)
    ocean = 1.0 - land[...].astype(f32)
    rows = [above[:K, :]] + [modes[r] for r in range(8)] + [below[:K, :]]
    flags = (
        [above[K : K + 1, :]]
        + [ocean[r : r + 1] for r in range(8)]
        + [below[K : K + 1, :]]
    )
    for r in range(8):
        here, flag = rows[r + 1], flags[r + 1]
        left = jnp.where(lane > 0, pltpu.roll(flag, 1, 1), f32(0.0))
        right = jnp.where(lane < cols - 1, pltpu.roll(flag, cols - 1, 1), f32(0.0))
        up, down = flags[r], flags[r + 2]
        centre = 1.0 - smoothing * (up + down + left + right)
        spread = (
            up * rows[r]
            + down * rows[r + 2]
            + left * pltpu.roll(here, 1, 1)
            + right * pltpu.roll(here, cols - 1, 1)
        )
        out[r] = centre * here + smoothing * spread


def refill_body(day, arrived, band, smooth, first, gap, land, filled, out):
    total = total_of(arrived)
    extra = jnp.concatenate([total[K:], pltpu.roll(total[K:], 64, 1)], axis=0)
    raw = jnp.concatenate([total[:K], extra], axis=1)
    tempered_t = mul(raw, band[...]).T
    factor = inverse_factor(extra)
    weights_t = mul(factor, total[:K])
    mixed = mul(tempered_t, mul(factor.T, factor))
    d = day[0]
    low, high = jnp.maximum(d - 1, 0), jnp.minimum(d + 1, 7)
    days, cols = filled.shape[1:]
    packed = pack_gram(weights_t)
    for j in range(8):
        out[j, K:, :LANES] = packed
        out[j, K:, LANES:] = jnp.zeros((8, cols - LANES), f32)
    ocean = 1.0 - land[...].astype(f32)
    for r in range(8):
        surface = mul(mixed, smooth[r])
        now = jnp.where(gap[r] == 1, surface * ocean[r : r + 1], first[r])
        filled[r] = now
        out[r, :K, :] = mul(weights_t, now)


def last_weights_body(raw, extra, band, scale, mixed, right, factor):
    tempered_t = mul(raw[0], band[:LANES, :]).T
    found = inverse_factor(unpack_gram(extra[...]))
    inner = mul(found.T, mul(found, scale[:, :K]))
    mixed[...] = mul(tempered_t, inner)
    right[...] = inner
    factor[...] = found


def last_fill_body(mixed, smooth, observed, missing, land, out, *halves):
    days = observed.shape[0]
    ocean = 1.0 - land[...].astype(f32)
    mix = mixed[...]
    for r in range(8):
        surface = mul(mix, smooth[r])
        for c, half in enumerate(halves):
            half[pl.ds(r, days, stride=8), :] = surface[:, LANES * c : LANES * c + LANES]
    for c, half in enumerate(halves):
        at = slice(LANES * c, LANES * c + LANES)
        surface = half[...].reshape(days, 8, LANES)
        value = jnp.where(missing[:, :, at] == 1, surface, observed[:, :, at])
        out[:, :, at] = value * ocean[None, :, at]


def finish_body(
    day,
    arrived,
    band,
    factor,
    right,
    mixed,
    smooth,
    observed_low,
    observed_high,
    missing_low,
    missing_high,
    land,
    filled_in,
    basis_t,
    filled,
    edges,
    halves,
    sent,
):
    del filled_in
    d = day[0]
    low = arrived[jnp.maximum(d - 1, 0)]
    high = arrived[jnp.minimum(d + 1, 7)]
    low = jnp.where(d > 0, low, f32(0.0))
    high = jnp.where(d < 7, high, f32(0.0))
    near = mul(jnp.concatenate([low, high], axis=1), band[2 * LANES :, :]).T
    near = mixed[...] + mul(near, right[...])
    days = near.shape[0]
    near = jnp.concatenate([near[:8], near[days - 8 :]], axis=0)
    for r in range(8):
        surface = mul(near, smooth[r])
        for c in range(2):
            halves[c, pl.ds(r, 16, stride=8), :] = surface[:, LANES * c : LANES * c + LANES]
    ocean = 1.0 - land[...].astype(f32)
    sides = ((observed_low, missing_low), (observed_high, missing_high))
    copies = []
    for e, (observed, missing) in enumerate(sides):
        for c in range(2):
            at = slice(LANES * c, LANES * c + LANES)
            surface = halves[c, 64 * e : 64 * e + 64, :].reshape(8, 8, LANES)
            value = jnp.where(missing[:, :, at] == 1, surface, observed[:, :, at])
            edges[e, :, :, at] = value * ocean[None, :, at]
        copy = pltpu.make_async_copy(
            edges.at[e], filled.at[pl.ds((days - 8) * e, 8)], sent.at[e]
        )
        copy.start()
        copies.append(copy)
    found = factor[...]
    gram = jnp.zeros((K, LANES), f32)
    rest = jnp.zeros((LANES - K, LANES), f32)
    for j in range(arrived.shape[0]):
        weights_t = mul(found, arrived[j])
        gram = gram + mul_t(weights_t, jnp.concatenate([weights_t, rest], axis=0))
    basis_t[...] = mul(inverse_factor(gram), mul(found, arrived[d]))
    for copy in copies:
        copy.wait()


def swap(blocks, axes):
    return lax.all_to_all(blocks, axes, 0, 0)


def near_rows(edge_low, edge_high):
    count = lax.axis_size(PIX)
    up = [(i, i + 1) for i in range(count - 1)]
    down = [(i + 1, i) for i in range(count - 1)]
    return lax.ppermute(edge_high, PIX, up), lax.ppermute(edge_low, PIX, down)


def band_of(day_weights):
    days = day_weights.shape[0]
    slot = lax.broadcasted_iota(jnp.int32, (4 * LANES, days), 0)
    target = lax.broadcasted_iota(jnp.int32, (4 * LANES, days), 1)
    first = LANES + K
    source = jnp.where(slot < days, slot, 4 * days)
    source = jnp.where((slot >= first) & (slot < first + 3), slot - first - 3, source)
    source = jnp.where(
        (slot >= first + 3) & (slot < first + 6), slot - first - 3 + days, source
    )
    source = jnp.where(slot >= 2 * LANES, slot - 3 * LANES, source)
    source = jnp.where(slot >= 3 * LANES, slot - 3 * LANES + days, source)
    taps = day_weights.T
    return sum(
        jnp.where(source - target + RADIUS == j, taps[j : j + 1], f32(0.0))
        for j in range(2 * RADIUS + 1)
    )


def per_device(observed, missing, land, basis_start, day_weights):
    days, rows, cols = observed.shape
    day = lax.axis_index(DAY).reshape(1)
    near, far = lax.axis_size(NEAR), lax.axis_size("y")
    band = band_of(day_weights)

    halo = [pltpu.VMEM((64, LANES), f32)] * 2
    halves = [pltpu.VMEM((days * rows, LANES), f32)] * 2
    edge = (K + 8, cols)
    block = (rows, K, cols)

    def add_near(joint, edges):
        joint = call(add_all_body, (far,) + joint.shape[1:], (swap(joint, NEAR),))
        return lax.optimization_barrier((joint, *edges))

    def smooth_beside(joint, low, high, modes):
        above, below = near_rows(low, high)
        joint = swap(joint, "y")
        smooth = call(smooth_body, block, (modes, above, below, land))
        return lax.optimization_barrier((joint, smooth))

    first, part = call(
        start_body,
        [(rows, days, cols), (rows, K + HALO, cols)],
        (day, observed, missing, land, basis_start.T),
        [
            pltpu.VMEM((days, rows, cols), f32),
            pltpu.VMEM((days, rows, cols), jnp.int32),
            pltpu.VMEM((rows, cols), jnp.int32),
            pltpu.VMEM((K, days), f32),
            *halves,
            pltpu.SemaphoreType.DMA((4,)),
        ],
        limit=56,
        anywhere=(1, 2, 3, 4),
    )
    gap, part = lax.optimization_barrier((missing, part))
    gap = gap.transpose(1, 0, 2)
    arrived = swap(part, DAY)
    modes = swap(call(add_rows_body, block, (arrived,)), DAY)
    joint, *edges = call(
        project_body,
        [(near, K + 16, LANES), edge, edge],
        (day, arrived, modes, first, land),
        halo,
    )
    joint, low, high = add_near(joint, edges)
    joint, smooth = smooth_beside(joint, low, high, modes)
    filled, part = call(
        refill_body,
        [(rows, days, cols), (rows, K + 8, cols)],
        (day, joint, band[: 2 * LANES], smooth, first, gap, land),
    )
    arrived = swap(part, DAY)
    modes = swap(call(add_rows_body, block, (arrived,)), DAY)
    factor = call(factor_body, (K, LANES), (arrived,))
    joint, *edges = call(
        project_again_body,
        [(near, K + 8, LANES), edge, edge],
        (modes, filled, land, factor),
    )
    joint, low, high = add_near(joint, edges)
    joint, smooth = smooth_beside(joint, low, high, modes)
    raw, extra = call(add_last_body, [(8, K, LANES), (8, LANES)], (joint,))
    arrived = swap(raw, DAY)
    mixed, right, found = call(
        last_weights_body,
        [(days, K), (K, K), (K, K)],
        (raw, extra, band, factor),
    )
    filled = call(
        last_fill_body,
        (days, rows, cols),
        (mixed, smooth, observed, missing, land),
        halves,
    )
    ends = (slice(0, 8), slice(days - 8, days))
    basis_t, filled = call(
        finish_body,
        [(K, days), (days, rows, cols)],
        (day, arrived, band, found, right, mixed, smooth)
        + tuple(observed[e] for e in ends)
        + tuple(missing[e] for e in ends)
        + (land, filled),
        [
            pltpu.VMEM((2, 8, rows, cols), f32),
            pltpu.VMEM((2, 128, LANES), f32),
            pltpu.SemaphoreType.DMA((2,)),
        ],
        anywhere=(12,),
        out_any=(1,),
        alias={12: 1},
    )
    return filled, basis_t.T


def solution(mesh):
    fine = Mesh(mesh.devices.reshape(SIZES), ("zlo", "y", "core", "x", "zhi"))
    return jax.shard_map(
        per_device,
        mesh=fine,
        in_specs=(
            P(DAY, PIX, None),
            P(DAY, PIX, None),
            P(PIX, None),
            P(DAY, None),
            P(DAY, None),
        ),
        out_specs=(P(DAY, PIX, None), P(DAY, None)),
        check_vma=False,
    )
```

```python
import jax
import jax.numpy as jnp
from jax import lax
from jax.experimental import pallas as pl
from jax.experimental.pallas import tpu as pltpu
from jax.sharding import Mesh, PartitionSpec as P

RADIUS = 3
K = 32
LANES = 128
HALO = 8 * RADIUS

PIX = ("zlo", "y", "core")
DAY = ("x", "zhi")
NEAR = ("zlo", "core")
SIZES = (4, 8, 2, 4, 2)

exact = lax.Precision.HIGHEST
smoothing = 0.2
f32 = jnp.float32
bf16 = jnp.bfloat16


def mul(a, b):
    return lax.dot_general(
        a, b, (((1,), (0,)), ((), ())), precision=exact, preferred_element_type=f32
    )


def mul_t(a, b):
    return lax.dot_general(
        a, b, (((1,), (1,)), ((), ())), precision=exact, preferred_element_type=f32
    )


def split(x):
    high = x.astype(bf16)
    rest = x - high.astype(f32)
    middle = rest.astype(bf16)
    return high, middle, (rest - middle.astype(f32)).astype(bf16)


def parts_of(a):
    return jnp.concatenate(split(a), axis=0)


def mul_few(stack, b, over=0):
    rows = stack.shape[0] // 3
    total = None
    for i, part in enumerate(split(b)):
        found = lax.dot_general(
            stack[: rows * (3 - i)],
            part,
            (((1,), (over,)), ((), ())),
            preferred_element_type=f32,
        )
        for j in range(3 - i):
            piece = found[rows * j : rows * j + rows]
            total = piece if total is None else total + piece
    return total


def deep_parts_of(a):
    high, middle, low = split(a)
    return jnp.concatenate([low, middle, high, middle, high, high], axis=1)


def mul_deep(stack, b):
    high, middle, low = split(b)
    right = jnp.concatenate([high, middle, low, high, middle, high], axis=0)
    return lax.dot_general(
        stack, right, (((1,), (0,)), ((), ())), preferred_element_type=f32
    )


def inverse_factor(wide):
    row = lax.broadcasted_iota(jnp.int32, (K, LANES), 0)
    lane = lax.broadcasted_iota(jnp.int32, (K, LANES), 1)
    work = jnp.where(lane < K, wide, jnp.where(lane == row + K, f32(1.0), f32(0.0)))
    done = []
    for start in range(0, K, 8):
        size = K - start
        at = lax.broadcasted_iota(jnp.int32, (size, LANES), 0)
        spread = [
            jnp.broadcast_to(work[:, start + j : start + j + 1], (size, LANES))
            for j in range(8)
        ]
        for j in range(8):
            inverse = 1.0 / spread[j][j : j + 1, :]
            column = jnp.where(at > j, spread[j], f32(0.0))
            for l in range(j + 1, 8):
                spread[l] = spread[l] - column * (spread[l][j : j + 1, :] * inverse)
            work = work - column * (work[j : j + 1, :] * inverse)
        done.append(work[:8])
        work = work[8:]
    work = jnp.concatenate(done, axis=0)
    pivots = jnp.sum(jnp.where(lane == row, work, f32(0.0)), axis=1, keepdims=True)
    work = work * (1.0 / jnp.sqrt(pivots))
    return pltpu.roll(work, LANES - K, 1)[:, :K]


def unpack_gram(packed):
    return jnp.concatenate(
        [packed] + [pltpu.roll(packed, LANES - K * a, 1) for a in range(1, 4)], axis=0
    )


def pack_rows(wide):
    packed = wide[:8]
    for a in range(1, 4):
        packed = packed + pltpu.roll(wide[8 * a : 8 * a + 8], K * a, 1)
    return packed


def pack_gram(weights_t):
    rest = jnp.zeros((LANES - K, LANES), f32)
    return pack_rows(mul_t(weights_t, jnp.concatenate([weights_t, rest], axis=0)))


def total_of(arrived):
    total = arrived[0]
    for j in range(1, arrived.shape[0]):
        total = total + arrived[j]
    return total


def call(body, outs, args, scratch=(), limit=8, anywhere=(), alias=None, out_any=()):
    specs = []
    for i, a in enumerate(args):
        space = pltpu.SMEM if a.ndim == 1 else pltpu.VMEM
        specs.append(pl.BlockSpec(memory_space=pl.ANY if i in anywhere else space))
    many = isinstance(outs, list)
    shapes = [jax.ShapeDtypeStruct(s, f32) for s in (outs if many else [outs])]
    out_specs = [
        pl.BlockSpec(memory_space=pl.ANY if i in out_any else pltpu.VMEM)
        for i in range(len(shapes))
    ]
    return pl.pallas_call(
        body,
        out_shape=shapes if many else shapes[0],
        in_specs=specs,
        out_specs=out_specs if many else out_specs[0],
        scratch_shapes=list(scratch),
        input_output_aliases=alias or {},
        compiler_params=pltpu.CompilerParams(vmem_limit_bytes=limit * 1024 * 1024),
        cost_estimate=pl.CostEstimate(
            flops=1_000_000, bytes_accessed=1_000_000, transcendentals=0
        ),
    )(*args)


def rows_of(halves, start, size):
    return jnp.concatenate(
        [half[pl.ds(start, size, stride=8), :] for half in halves], axis=1
    )


def start_body(
    day,
    observed_hbm,
    missing_hbm,
    land_hbm,
    basis_hbm,
    first_hbm,
    out_hbm,
    observed,
    missing,
    land,
    basis_t,
    half_0,
    half_1,
    first,
    out,
    arrivals,
    sent,
):
    parts = 4
    days = first.shape[1]
    size = days // parts
    small = [
        pltpu.make_async_copy(land_hbm, land, arrivals.at[2 * parts]),
        pltpu.make_async_copy(basis_hbm, basis_t, arrivals.at[2 * parts + 1]),
    ]
    for copy in small:
        copy.start()
    copies = []
    for i in range(parts):
        at = pl.ds(size * i, size)
        for c, (source, target) in enumerate(
            ((missing_hbm, missing), (observed_hbm, observed))
        ):
            copies.append(
                pltpu.make_async_copy(
                    source.at[at], target.at[at], arrivals.at[2 * i + c]
                )
            )
            copies[-1].start()
    d = day[0]
    halves = (half_0, half_1)
    out[:, K:, :] = jnp.zeros((8, HALO, out.shape[2]), f32)
    for copy in small:
        copy.wait()
    ocean = 1.0 - land[...].astype(f32)
    for i in range(parts):
        copies[2 * i].wait()
        copies[2 * i + 1].wait()
        now = slice(size * i, size * i + size)
        for c, half in enumerate(halves):
            at = slice(LANES * c, LANES * c + LANES)
            tile = jnp.where(missing[now, :, at] == 1, f32(0.0), observed[now, :, at])
            tile = tile * ocean[None, :, at]
            half[8 * size * i : 8 * size * (i + 1), :] = tile.reshape(8 * size, LANES)
    low, high = jnp.maximum(d - 1, 0), jnp.minimum(d + 1, 7)
    for t in range(RADIUS):
        for target, source in ((low, t), (high, days - RADIUS + t)):
            tile = [half[8 * source : 8 * source + 8, :] for half in halves]
            out[target, K + 8 * t : K + 8 * t + 8, :] = jnp.concatenate(tile, axis=1)
    weights = parts_of(basis_t[...])
    copies = []
    for r in range(8):
        filled = rows_of(halves, r, days)
        first[r] = filled
        out[r, :K, :] = mul_few(weights, filled)
        copies.append(pltpu.make_async_copy(out.at[r], out_hbm.at[r], sent.at[r]))
        copies[-1].start()
        copies.append(pltpu.make_async_copy(first.at[r], first_hbm.at[r], sent.at[8 + r]))
        copies[-1].start()
    for copy in copies:
        copy.wait()


def gap_body(missing_hbm, gap_hbm, missing, half_0, half_1, gap, arrivals):
    copy = pltpu.make_async_copy(missing_hbm, missing, arrivals.at[0])
    copy.start()
    copy.wait()
    days = missing.shape[0]
    for c, half in enumerate((half_0, half_1)):
        tile = missing[:, :, LANES * c : LANES * c + LANES].astype(f32)
        half[...] = tile.reshape(8 * days, LANES)
    for r in range(8):
        gap[r] = rows_of((half_0, half_1), r, days)
    copy = pltpu.make_async_copy(gap, gap_hbm, arrivals.at[1])
    copy.start()
    copy.wait()


def add_rows_body(arrived, out):
    total = arrived[0, :K, :]
    for j in range(1, arrived.shape[0]):
        total = total + arrived[j, :K, :]
    for j in range(out.shape[0]):
        out[j] = total


def add_all_body(arrived, out):
    total = total_of(arrived)
    for j in range(out.shape[0]):
        out[j] = total


def add_last_body(arrived, out, extra):
    total = total_of(arrived)
    for j in range(out.shape[0]):
        out[j] = total[:K]
    extra[...] = total[K:]


def factor_body(arrived, out):
    packed = arrived[0, K:, :LANES]
    for j in range(1, arrived.shape[0]):
        packed = packed + arrived[j, K:, :LANES]
    out[:, :K] = inverse_factor(unpack_gram(packed))
    out[:, K:] = jnp.zeros((K, LANES - K), f32)


def edges_of(modes, land, edge_low, edge_high):
    ocean = 1.0 - land[...].astype(f32)
    for edge, r in ((edge_low, 0), (edge_high, 7)):
        edge[:K, :] = modes[r]
        edge[K:, :] = jnp.broadcast_to(ocean[r : r + 1], (8, ocean.shape[1]))


def project_again_body(modes, filled, land, factor, out, edge_low, edge_high):
    cols = modes.shape[2]
    scale = factor[:, :K]
    pad = jnp.zeros((LANES - K, cols), f32)
    total = jnp.zeros((K, 2 * LANES), f32)
    for r in range(8):
        modes_u = mul(scale, modes[r])
        right = jnp.concatenate([filled[r], modes_u, pad], axis=0)
        total = total + mul_few(parts_of(modes_u), right, 1)
    packed = pack_rows(total[:, LANES:])
    for j in range(out.shape[0]):
        out[j, :K, :] = total[:, :LANES]
        out[j, K:, :] = packed
    edges_of(modes, land, edge_low, edge_high)


def project_body(
    day, arrived, modes, filled, land, out, edge_low, edge_high, halo_0, halo_1
):
    d = day[0]
    low = arrived[jnp.maximum(d - 1, 0), K : K + HALO, :]
    high = arrived[jnp.minimum(d + 1, 7), K : K + HALO, :]
    low = jnp.where(d > 0, low, f32(0.0))
    high = jnp.where(d < 7, high, f32(0.0))
    cols = modes.shape[2]
    for c, halo in enumerate((halo_0, halo_1)):
        halo[:HALO, :] = low[:, LANES * c : LANES * c + LANES]
        halo[HALO : 2 * HALO, :] = high[:, LANES * c : LANES * c + LANES]
        halo[2 * HALO :, :] = jnp.zeros((64 - 2 * HALO, LANES), f32)
    pad = jnp.zeros((LANES - K - 8, cols), f32)
    total = jnp.zeros((K, 2 * LANES), f32)
    for r in range(8):
        modes_u = modes[r]
        days_near = rows_of((halo_0, halo_1), r, 8)
        right = jnp.concatenate([filled[r], modes_u, days_near, pad], axis=0)
        total = total + mul_few(parts_of(modes_u), right, 1)
    extra = total[:, LANES:]
    packed = extra[:16] + pltpu.roll(extra[16:], 64, 1)
    for j in range(out.shape[0]):
        out[j, :K, :] = total[:, :LANES]
        out[j, K:, :] = packed
    edges_of(modes, land, edge_low, edge_high)


def smooth_body(modes, above, below, land, out):
    cols = out.shape[2]
    lane = lax.broadcasted_iota(jnp.int32, (1, cols), 1)
    ocean = 1.0 - land[...].astype(f32)
    rows = [above[:K, :]] + [modes[r] for r in range(8)] + [below[:K, :]]
    flags = (
        [above[K : K + 1, :]]
        + [ocean[r : r + 1] for r in range(8)]
        + [below[K : K + 1, :]]
    )
    for r in range(8):
        here, flag = rows[r + 1], flags[r + 1]
        left = jnp.where(lane > 0, pltpu.roll(flag, 1, 1), f32(0.0))
        right = jnp.where(lane < cols - 1, pltpu.roll(flag, cols - 1, 1), f32(0.0))
        up, down = flags[r], flags[r + 2]
        centre = 1.0 - smoothing * (up + down + left + right)
        spread = (
            up * rows[r]
            + down * rows[r + 2]
            + left * pltpu.roll(here, 1, 1)
            + right * pltpu.roll(here, cols - 1, 1)
        )
        out[r] = centre * here + smoothing * spread


def refill_body(
    day,
    arrived,
    band,
    smooth_hbm,
    first_hbm,
    gap_hbm,
    land,
    filled_hbm,
    out,
    smooth,
    first,
    gap,
    filled,
    arrivals,
    sent,
):
    pairs = ((smooth_hbm, smooth), (first_hbm, first), (gap_hbm, gap))
    copies = [
        pltpu.make_async_copy(source, target, arrivals.at[i])
        for i, (source, target) in enumerate(pairs)
    ]
    for copy in copies:
        copy.start()
    total = total_of(arrived)
    extra = jnp.concatenate([total[K:], pltpu.roll(total[K:], 64, 1)], axis=0)
    raw = jnp.concatenate([total[:K], extra], axis=1)
    tempered_t = mul(raw, band[...]).T
    factor = inverse_factor(extra)
    weights_t = mul(factor, total[:K])
    mixed = deep_parts_of(mul(tempered_t, mul(factor.T, factor)))
    weights = parts_of(weights_t)
    days, cols = filled.shape[1:]
    packed = pack_gram(weights_t)
    for j in range(8):
        out[j, K:, :LANES] = packed
        out[j, K:, LANES:] = jnp.zeros((8, cols - LANES), f32)
    ocean = 1.0 - land[...].astype(f32)
    for copy in copies:
        copy.wait()
    copies = []
    for r in range(8):
        surface = mul_deep(mixed, smooth[r])
        now = jnp.where(gap[r] == 1, surface * ocean[r : r + 1], first[r])
        filled[r] = now
        copies.append(pltpu.make_async_copy(filled.at[r], filled_hbm.at[r], sent.at[r]))
        copies[-1].start()
        out[r, :K, :] = mul_few(weights, now)
    for copy in copies:
        copy.wait()


def last_weights_body(raw, extra, band, scale, mixed, right, factor):
    tempered_t = mul(raw[0], band[:LANES, :]).T
    found = inverse_factor(unpack_gram(extra[...]))
    inner = mul(found.T, mul(found, scale[:, :K]))
    mixed[...] = mul(tempered_t, inner)
    right[...] = inner
    factor[...] = found


def last_fill_body(mixed, smooth, observed, missing, land, out, *halves):
    days = observed.shape[0]
    ocean = 1.0 - land[...].astype(f32)
    mix = deep_parts_of(mixed[...])
    for r in range(8):
        surface = mul_deep(mix, smooth[r])
        for c, half in enumerate(halves):
            half[pl.ds(r, days, stride=8), :] = surface[:, LANES * c : LANES * c + LANES]
    for c, half in enumerate(halves):
        at = slice(LANES * c, LANES * c + LANES)
        surface = half[...].reshape(days, 8, LANES)
        value = jnp.where(missing[:, :, at] == 1, surface, observed[:, :, at])
        out[:, :, at] = value * ocean[None, :, at]


def finish_body(
    day,
    arrived,
    band,
    factor,
    right,
    mixed,
    smooth,
    observed_low,
    observed_high,
    missing_low,
    missing_high,
    land,
    filled_in,
    basis_t,
    filled,
    edges,
    halves,
    sent,
):
    del filled_in
    d = day[0]
    low = arrived[jnp.maximum(d - 1, 0)]
    high = arrived[jnp.minimum(d + 1, 7)]
    low = jnp.where(d > 0, low, f32(0.0))
    high = jnp.where(d < 7, high, f32(0.0))
    near = mul(jnp.concatenate([low, high], axis=1), band[2 * LANES :, :]).T
    near = mixed[...] + mul(near, right[...])
    days = near.shape[0]
    near = jnp.concatenate([near[:8], near[days - 8 :]], axis=0)
    for r in range(8):
        surface = mul(near, smooth[r])
        for c in range(2):
            halves[c, pl.ds(r, 16, stride=8), :] = surface[:, LANES * c : LANES * c + LANES]
    ocean = 1.0 - land[...].astype(f32)
    sides = ((observed_low, missing_low), (observed_high, missing_high))
    copies = []
    for e, (observed, missing) in enumerate(sides):
        for c in range(2):
            at = slice(LANES * c, LANES * c + LANES)
            surface = halves[c, 64 * e : 64 * e + 64, :].reshape(8, 8, LANES)
            value = jnp.where(missing[:, :, at] == 1, surface, observed[:, :, at])
            edges[e, :, :, at] = value * ocean[None, :, at]
        copy = pltpu.make_async_copy(
            edges.at[e], filled.at[pl.ds((days - 8) * e, 8)], sent.at[e]
        )
        copy.start()
        copies.append(copy)
    found = factor[...]
    gram = jnp.zeros((K, LANES), f32)
    rest = jnp.zeros((LANES - K, LANES), f32)
    for j in range(arrived.shape[0]):
        weights_t = mul(found, arrived[j])
        gram = gram + mul_t(weights_t, jnp.concatenate([weights_t, rest], axis=0))
    basis_t[...] = mul(inverse_factor(gram), mul(found, arrived[d]))
    for copy in copies:
        copy.wait()


def swap(blocks, axes):
    return lax.all_to_all(blocks, axes, 0, 0)


def near_rows(edge_low, edge_high):
    count = lax.axis_size(PIX)
    up = [(i, i + 1) for i in range(count - 1)]
    down = [(i + 1, i) for i in range(count - 1)]
    return lax.ppermute(edge_high, PIX, up), lax.ppermute(edge_low, PIX, down)


def band_of(day_weights):
    days = day_weights.shape[0]
    slot = lax.broadcasted_iota(jnp.int32, (4 * LANES, days), 0)
    target = lax.broadcasted_iota(jnp.int32, (4 * LANES, days), 1)
    first = LANES + K
    source = jnp.where(slot < days, slot, 4 * days)
    source = jnp.where((slot >= first) & (slot < first + 3), slot - first - 3, source)
    source = jnp.where(
        (slot >= first + 3) & (slot < first + 6), slot - first - 3 + days, source
    )
    source = jnp.where(slot >= 2 * LANES, slot - 3 * LANES, source)
    source = jnp.where(slot >= 3 * LANES, slot - 3 * LANES + days, source)
    taps = day_weights.T
    return sum(
        jnp.where(source - target + RADIUS == j, taps[j : j + 1], f32(0.0))
        for j in range(2 * RADIUS + 1)
    )


def per_device(observed, missing, land, basis_start, day_weights):
    days, rows, cols = observed.shape
    day = lax.axis_index(DAY).reshape(1)
    near, far = lax.axis_size(NEAR), lax.axis_size("y")
    band = band_of(day_weights)

    halo = [pltpu.VMEM((64, LANES), f32)] * 2
    halves = [pltpu.VMEM((days * rows, LANES), f32)] * 2
    edge = (K + 8, cols)
    block = (rows, K, cols)

    def add_near(joint, edges):
        joint = call(add_all_body, (far,) + joint.shape[1:], (swap(joint, NEAR),))
        return lax.optimization_barrier((joint, *edges))

    def smooth_beside(joint, low, high, modes):
        above, below = near_rows(low, high)
        joint = swap(joint, "y")
        smooth = call(smooth_body, block, (modes, above, below, land))
        return lax.optimization_barrier((joint, smooth))

    slab = pltpu.VMEM((days, rows, cols), f32)
    turned = pltpu.VMEM((rows, days, cols), f32)
    mask = pltpu.VMEM((days, rows, cols), jnp.int32)

    first, part = call(
        start_body,
        [(rows, days, cols), (rows, K + HALO, cols)],
        (day, observed, missing, land, basis_start.T),
        [
            slab,
            mask,
            pltpu.VMEM((rows, cols), jnp.int32),
            pltpu.VMEM((K, days), f32),
            *halves,
            turned,
            pltpu.VMEM((rows, K + HALO, cols), f32),
            pltpu.SemaphoreType.DMA((10,)),
            pltpu.SemaphoreType.DMA((16,)),
        ],
        limit=56,
        anywhere=(1, 2, 3, 4),
        out_any=(0, 1),
    )
    later, part = lax.optimization_barrier((missing, part))
    gap = call(
        gap_body,
        (rows, days, cols),
        (later,),
        [mask, *halves, turned, pltpu.SemaphoreType.DMA((2,))],
        limit=56,
        anywhere=(0,),
        out_any=(0,),
    )
    arrived = swap(part, DAY)
    modes = swap(call(add_rows_body, block, (arrived,)), DAY)
    joint, *edges = call(
        project_body,
        [(near, K + 16, LANES), edge, edge],
        (day, arrived, modes, first, land),
        halo,
    )
    joint, low, high = add_near(joint, edges)
    joint, smooth = smooth_beside(joint, low, high, modes)
    filled, part = call(
        refill_body,
        [(rows, days, cols), (rows, K + 8, cols)],
        (day, joint, band[: 2 * LANES], smooth, first, gap, land),
        [
            pltpu.VMEM(block, f32),
            turned,
            turned,
            turned,
            pltpu.SemaphoreType.DMA((3,)),
            pltpu.SemaphoreType.DMA((8,)),
        ],
        limit=56,
        anywhere=(3, 4, 5),
        out_any=(0,),
    )
    arrived = swap(part, DAY)
    modes = swap(call(add_rows_body, block, (arrived,)), DAY)
    factor = call(factor_body, (K, LANES), (arrived,))
    joint, *edges = call(
        project_again_body,
        [(near, K + 8, LANES), edge, edge],
        (modes, filled, land, factor),
    )
    joint, low, high = add_near(joint, edges)
    joint, smooth = smooth_beside(joint, low, high, modes)
    raw, extra = call(add_last_body, [(8, K, LANES), (8, LANES)], (joint,))
    arrived = swap(raw, DAY)
    mixed, right, found = call(
        last_weights_body,
        [(days, K), (K, K), (K, K)],
        (raw, extra, band, factor),
    )
    filled = call(
        last_fill_body,
        (days, rows, cols),
        (mixed, smooth, observed, missing, land),
        halves,
    )
    ends = (slice(0, 8), slice(days - 8, days))
    basis_t, filled = call(
        finish_body,
        [(K, days), (days, rows, cols)],
        (day, arrived, band, found, right, mixed, smooth)
        + tuple(observed[e] for e in ends)
        + tuple(missing[e] for e in ends)
        + (land, filled),
        [
            pltpu.VMEM((2, 8, rows, cols), f32),
            pltpu.VMEM((2, 128, LANES), f32),
            pltpu.SemaphoreType.DMA((2,)),
        ],
        anywhere=(12,),
        out_any=(1,),
        alias={12: 1},
    )
    return filled, basis_t.T


def solution(mesh):
    fine = Mesh(mesh.devices.reshape(SIZES), ("zlo", "y", "core", "x", "zhi"))
    return jax.shard_map(
        per_device,
        mesh=fine,
        in_specs=(
            P(DAY, PIX, None),
            P(DAY, PIX, None),
            P(PIX, None),
            P(DAY, None),
            P(DAY, None),
        ),
        out_specs=(P(DAY, PIX, None), P(DAY, None)),
        check_vma=False,
    )
```

```python
import jax
import jax.numpy as jnp
from jax import lax
from jax.experimental import pallas as pl
from jax.experimental.pallas import tpu as pltpu
from jax.sharding import Mesh, PartitionSpec as P

RADIUS = 3
K = 32
LANES = 128
HALO = 8 * RADIUS

PIX = ("zlo", "y", "core")
DAY = ("x", "zhi")
NEAR = ("zlo", "core")
SIZES = (4, 8, 2, 4, 2)

exact = lax.Precision.HIGHEST
smoothing = 0.2
f32 = jnp.float32
bf16 = jnp.bfloat16


def mul(a, b):
    return lax.dot_general(
        a, b, (((1,), (0,)), ((), ())), precision=exact, preferred_element_type=f32
    )


def mul_t(a, b):
    return lax.dot_general(
        a, b, (((1,), (1,)), ((), ())), precision=exact, preferred_element_type=f32
    )


def split(x):
    high = x.astype(bf16)
    rest = x - high.astype(f32)
    middle = rest.astype(bf16)
    return high, middle, (rest - middle.astype(f32)).astype(bf16)


def parts_of(a):
    return jnp.concatenate(split(a), axis=0)


def mul_few(stack, b, over=0):
    rows = stack.shape[0] // 3
    total = None
    for i, part in enumerate(split(b)):
        found = lax.dot_general(
            stack[: rows * (3 - i)],
            part,
            (((1,), (over,)), ((), ())),
            preferred_element_type=f32,
        )
        for j in range(3 - i):
            piece = found[rows * j : rows * j + rows]
            total = piece if total is None else total + piece
    return total


def deep_parts_of(a):
    high, middle, low = split(a)
    return jnp.concatenate([low, middle, high, middle, high, high], axis=1)


def mul_deep(stack, b):
    high, middle, low = split(b)
    right = jnp.concatenate([high, middle, low, high, middle, high], axis=0)
    return lax.dot_general(
        stack, right, (((1,), (0,)), ((), ())), preferred_element_type=f32
    )


def inverse_factor(wide):
    row = lax.broadcasted_iota(jnp.int32, (K, LANES), 0)
    lane = lax.broadcasted_iota(jnp.int32, (K, LANES), 1)
    work = jnp.where(lane < K, wide, jnp.where(lane == row + K, f32(1.0), f32(0.0)))
    done = []
    for start in range(0, K, 8):
        size = K - start
        at = lax.broadcasted_iota(jnp.int32, (size, LANES), 0)
        spread = [
            jnp.broadcast_to(work[:, start + j : start + j + 1], (size, LANES))
            for j in range(8)
        ]
        for j in range(8):
            inverse = 1.0 / spread[j][j : j + 1, :]
            column = jnp.where(at > j, spread[j], f32(0.0))
            for l in range(j + 1, 8):
                spread[l] = spread[l] - column * (spread[l][j : j + 1, :] * inverse)
            work = work - column * (work[j : j + 1, :] * inverse)
        done.append(work[:8])
        work = work[8:]
    work = jnp.concatenate(done, axis=0)
    pivots = jnp.sum(jnp.where(lane == row, work, f32(0.0)), axis=1, keepdims=True)
    work = work * (1.0 / jnp.sqrt(pivots))
    return pltpu.roll(work, LANES - K, 1)[:, :K]


def unpack_gram(packed):
    return jnp.concatenate(
        [packed] + [pltpu.roll(packed, LANES - K * a, 1) for a in range(1, 4)], axis=0
    )


def pack_rows(wide):
    packed = wide[:8]
    for a in range(1, 4):
        packed = packed + pltpu.roll(wide[8 * a : 8 * a + 8], K * a, 1)
    return packed


def pack_gram(weights_t):
    rest = jnp.zeros((LANES - K, LANES), f32)
    return pack_rows(mul_t(weights_t, jnp.concatenate([weights_t, rest], axis=0)))


def total_of(arrived):
    total = arrived[0]
    for j in range(1, arrived.shape[0]):
        total = total + arrived[j]
    return total


def call(body, outs, args, scratch=(), limit=8, anywhere=(), alias=None, out_any=()):
    specs = []
    for i, a in enumerate(args):
        space = pltpu.SMEM if a.ndim == 1 else pltpu.VMEM
        specs.append(pl.BlockSpec(memory_space=pl.ANY if i in anywhere else space))
    many = isinstance(outs, list)
    shapes = [jax.ShapeDtypeStruct(s, f32) for s in (outs if many else [outs])]
    out_specs = [
        pl.BlockSpec(memory_space=pl.ANY if i in out_any else pltpu.VMEM)
        for i in range(len(shapes))
    ]
    return pl.pallas_call(
        body,
        out_shape=shapes if many else shapes[0],
        in_specs=specs,
        out_specs=out_specs if many else out_specs[0],
        scratch_shapes=list(scratch),
        input_output_aliases=alias or {},
        compiler_params=pltpu.CompilerParams(vmem_limit_bytes=limit * 1024 * 1024),
        cost_estimate=pl.CostEstimate(
            flops=1_000_000, bytes_accessed=1_000_000, transcendentals=0
        ),
    )(*args)


def rows_of(halves, start, size):
    return jnp.concatenate(
        [half[pl.ds(start, size, stride=8), :] for half in halves], axis=1
    )


def start_body(
    day,
    observed_hbm,
    missing_hbm,
    land_hbm,
    basis_hbm,
    out_hbm,
    observed,
    missing,
    land,
    basis_t,
    half_0,
    half_1,
    out,
    arrivals,
    sent,
):
    parts = 4
    days = observed.shape[0]
    size = days // parts
    small = [
        pltpu.make_async_copy(land_hbm, land, arrivals.at[2 * parts]),
        pltpu.make_async_copy(basis_hbm, basis_t, arrivals.at[2 * parts + 1]),
    ]
    for copy in small:
        copy.start()
    copies = []
    for i in range(parts):
        at = pl.ds(size * i, size)
        for c, (source, target) in enumerate(
            ((missing_hbm, missing), (observed_hbm, observed))
        ):
            copies.append(
                pltpu.make_async_copy(
                    source.at[at], target.at[at], arrivals.at[2 * i + c]
                )
            )
            copies[-1].start()
    d = day[0]
    halves = (half_0, half_1)
    out[:, K:, :] = jnp.zeros((8, HALO, out.shape[2]), f32)
    for copy in small:
        copy.wait()
    ocean = 1.0 - land[...].astype(f32)
    for i in range(parts):
        copies[2 * i].wait()
        copies[2 * i + 1].wait()
        now = slice(size * i, size * i + size)
        for c, half in enumerate(halves):
            at = slice(LANES * c, LANES * c + LANES)
            tile = jnp.where(missing[now, :, at] == 1, f32(0.0), observed[now, :, at])
            tile = tile * ocean[None, :, at]
            half[8 * size * i : 8 * size * (i + 1), :] = tile.reshape(8 * size, LANES)
    low, high = jnp.maximum(d - 1, 0), jnp.minimum(d + 1, 7)
    for t in range(RADIUS):
        for target, source in ((low, t), (high, days - RADIUS + t)):
            tile = [half[8 * source : 8 * source + 8, :] for half in halves]
            out[target, K + 8 * t : K + 8 * t + 8, :] = jnp.concatenate(tile, axis=1)
    weights = parts_of(basis_t[...])
    copies = []
    for r in range(8):
        out[r, :K, :] = mul_few(weights, rows_of(halves, r, days))
        copies.append(pltpu.make_async_copy(out.at[r], out_hbm.at[r], sent.at[r]))
        copies[-1].start()
    for copy in copies:
        copy.wait()


def turn_body(
    observed_hbm,
    missing_hbm,
    land,
    first_hbm,
    gap_hbm,
    observed,
    missing,
    half_0,
    half_1,
    mask_0,
    mask_1,
    first,
    gap,
    arrivals,
    sent,
):
    pairs = ((missing_hbm, missing), (observed_hbm, observed))
    copies = [
        pltpu.make_async_copy(source, target, arrivals.at[i])
        for i, (source, target) in enumerate(pairs)
    ]
    for copy in copies:
        copy.start()
    for copy in copies:
        copy.wait()
    days = missing.shape[0]
    ocean = 1.0 - land[...].astype(f32)
    halves, masks = (half_0, half_1), (mask_0, mask_1)
    for c in range(2):
        at = slice(LANES * c, LANES * c + LANES)
        absent = missing[:, :, at] == 1
        tile = jnp.where(absent, f32(0.0), observed[:, :, at]) * ocean[None, :, at]
        halves[c][...] = tile.reshape(8 * days, LANES)
        masks[c][...] = absent.astype(f32).reshape(8 * days, LANES)
    for r in range(8):
        first[r] = rows_of(halves, r, days)
        gap[r] = rows_of(masks, r, days)
    copies = [
        pltpu.make_async_copy(first, first_hbm, sent.at[0]),
        pltpu.make_async_copy(gap, gap_hbm, sent.at[1]),
    ]
    for copy in copies:
        copy.start()
    for copy in copies:
        copy.wait()


def add_rows_body(arrived, out):
    total = arrived[0, :K, :]
    for j in range(1, arrived.shape[0]):
        total = total + arrived[j, :K, :]
    for j in range(out.shape[0]):
        out[j] = total


def add_all_body(arrived, out):
    total = total_of(arrived)
    for j in range(out.shape[0]):
        out[j] = total


def add_last_body(arrived, out, extra):
    total = total_of(arrived)
    for j in range(out.shape[0]):
        out[j] = total[:K]
    extra[...] = total[K:]


def factor_body(arrived, out):
    packed = arrived[0, K:, :LANES]
    for j in range(1, arrived.shape[0]):
        packed = packed + arrived[j, K:, :LANES]
    out[:, :K] = inverse_factor(unpack_gram(packed))
    out[:, K:] = jnp.zeros((K, LANES - K), f32)


def edges_of(modes, land, edge_low, edge_high):
    ocean = 1.0 - land[...].astype(f32)
    for edge, r in ((edge_low, 0), (edge_high, 7)):
        edge[:K, :] = modes[r]
        edge[K:, :] = jnp.broadcast_to(ocean[r : r + 1], (8, ocean.shape[1]))


def project_again_body(modes, filled, land, factor, out, edge_low, edge_high):
    cols = modes.shape[2]
    scale = factor[:, :K]
    pad = jnp.zeros((LANES - K, cols), f32)
    total = jnp.zeros((K, 2 * LANES), f32)
    for r in range(8):
        modes_u = mul(scale, modes[r])
        right = jnp.concatenate([filled[r], modes_u, pad], axis=0)
        total = total + mul_few(parts_of(modes_u), right, 1)
    packed = pack_rows(total[:, LANES:])
    for j in range(out.shape[0]):
        out[j, :K, :] = total[:, :LANES]
        out[j, K:, :] = packed
    edges_of(modes, land, edge_low, edge_high)


def project_body(
    day, arrived, modes, filled, land, out, edge_low, edge_high, halo_0, halo_1
):
    d = day[0]
    low = arrived[jnp.maximum(d - 1, 0), K : K + HALO, :]
    high = arrived[jnp.minimum(d + 1, 7), K : K + HALO, :]
    low = jnp.where(d > 0, low, f32(0.0))
    high = jnp.where(d < 7, high, f32(0.0))
    cols = modes.shape[2]
    for c, halo in enumerate((halo_0, halo_1)):
        halo[:HALO, :] = low[:, LANES * c : LANES * c + LANES]
        halo[HALO : 2 * HALO, :] = high[:, LANES * c : LANES * c + LANES]
        halo[2 * HALO :, :] = jnp.zeros((64 - 2 * HALO, LANES), f32)
    pad = jnp.zeros((LANES - K - 8, cols), f32)
    total = jnp.zeros((K, 2 * LANES), f32)
    for r in range(8):
        modes_u = modes[r]
        days_near = rows_of((halo_0, halo_1), r, 8)
        right = jnp.concatenate([filled[r], modes_u, days_near, pad], axis=0)
        total = total + mul_few(parts_of(modes_u), right, 1)
    extra = total[:, LANES:]
    packed = extra[:16] + pltpu.roll(extra[16:], 64, 1)
    for j in range(out.shape[0]):
        out[j, :K, :] = total[:, :LANES]
        out[j, K:, :] = packed
    edges_of(modes, land, edge_low, edge_high)


def smooth_body(modes, above, below, land, out):
    cols = out.shape[2]
    lane = lax.broadcasted_iota(jnp.int32, (1, cols), 1)
    ocean = 1.0 - land[...].astype(f32)
    rows = [above[:K, :]] + [modes[r] for r in range(8)] + [below[:K, :]]
    flags = (
        [above[K : K + 1, :]]
        + [ocean[r : r + 1] for r in range(8)]
        + [below[K : K + 1, :]]
    )
    for r in range(8):
        here, flag = rows[r + 1], flags[r + 1]
        left = jnp.where(lane > 0, pltpu.roll(flag, 1, 1), f32(0.0))
        right = jnp.where(lane < cols - 1, pltpu.roll(flag, cols - 1, 1), f32(0.0))
        up, down = flags[r], flags[r + 2]
        centre = 1.0 - smoothing * (up + down + left + right)
        spread = (
            up * rows[r]
            + down * rows[r + 2]
            + left * pltpu.roll(here, 1, 1)
            + right * pltpu.roll(here, cols - 1, 1)
        )
        out[r] = centre * here + smoothing * spread


def refill_body(
    day,
    arrived,
    band,
    smooth_hbm,
    first_hbm,
    gap_hbm,
    land,
    filled_hbm,
    out,
    smooth,
    first,
    gap,
    filled,
    arrivals,
    sent,
):
    pairs = ((smooth_hbm, smooth), (first_hbm, first), (gap_hbm, gap))
    copies = [
        pltpu.make_async_copy(source, target, arrivals.at[i])
        for i, (source, target) in enumerate(pairs)
    ]
    for copy in copies:
        copy.start()
    total = total_of(arrived)
    extra = jnp.concatenate([total[K:], pltpu.roll(total[K:], 64, 1)], axis=0)
    raw = jnp.concatenate([total[:K], extra], axis=1)
    tempered_t = mul(raw, band[: 2 * LANES, :]).T
    factor = inverse_factor(extra)
    weights_t = mul(factor, total[:K])
    mixed = deep_parts_of(mul(tempered_t, mul(factor.T, factor)))
    weights = parts_of(weights_t)
    days, cols = filled.shape[1:]
    packed = pack_gram(weights_t)
    for j in range(8):
        out[j, K:, :LANES] = packed
        out[j, K:, LANES:] = jnp.zeros((8, cols - LANES), f32)
    ocean = 1.0 - land[...].astype(f32)
    for copy in copies:
        copy.wait()
    copies = []
    for r in range(8):
        surface = mul_deep(mixed, smooth[r])
        now = jnp.where(gap[r] == 1, surface * ocean[r : r + 1], first[r])
        filled[r] = now
        copies.append(pltpu.make_async_copy(filled.at[r], filled_hbm.at[r], sent.at[r]))
        copies[-1].start()
        out[r, :K, :] = mul_few(weights, now)
    for copy in copies:
        copy.wait()


def last_weights_body(raw, extra, band, scale, mixed, right, factor):
    tempered_t = mul(raw[0], band[:LANES, :]).T
    found = inverse_factor(unpack_gram(extra[...]))
    inner = mul(found.T, mul(found, scale[:, :K]))
    mixed[...] = mul(tempered_t, inner)
    right[...] = inner
    factor[...] = found


def last_fill_body(mixed, smooth, observed, missing, land, out, *halves):
    days = observed.shape[0]
    ocean = 1.0 - land[...].astype(f32)
    mix = deep_parts_of(mixed[...])
    for r in range(8):
        surface = mul_deep(mix, smooth[r])
        for c, half in enumerate(halves):
            half[pl.ds(r, days, stride=8), :] = surface[:, LANES * c : LANES * c + LANES]
    for c, half in enumerate(halves):
        at = slice(LANES * c, LANES * c + LANES)
        surface = half[...].reshape(days, 8, LANES)
        value = jnp.where(missing[:, :, at] == 1, surface, observed[:, :, at])
        out[:, :, at] = value * ocean[None, :, at]


def finish_body(
    day,
    arrived,
    band,
    factor,
    right,
    mixed,
    smooth,
    observed_hbm,
    missing_hbm,
    land,
    filled_in,
    basis_t,
    filled,
    edges,
    halves,
    observed,
    missing,
    arrivals,
    sent,
):
    del filled_in
    fetches = []
    total_days = observed_hbm.shape[0]
    for e in range(2):
        at = pl.ds((total_days - 8) * e, 8)
        for c, (source, target) in enumerate(
            ((observed_hbm, observed), (missing_hbm, missing))
        ):
            fetches.append(
                pltpu.make_async_copy(
                    source.at[at], target.at[e], arrivals.at[2 * e + c]
                )
            )
            fetches[-1].start()
    d = day[0]
    low = arrived[jnp.maximum(d - 1, 0)]
    high = arrived[jnp.minimum(d + 1, 7)]
    low = jnp.where(d > 0, low, f32(0.0))
    high = jnp.where(d < 7, high, f32(0.0))
    near = mul(jnp.concatenate([low, high], axis=1), band[2 * LANES :, :]).T
    near = mixed[...] + mul(near, right[...])
    days = near.shape[0]
    near = jnp.concatenate([near[:8], near[days - 8 :]], axis=0)
    for r in range(8):
        surface = mul(near, smooth[r])
        for c in range(2):
            halves[c, pl.ds(r, 16, stride=8), :] = surface[:, LANES * c : LANES * c + LANES]
    ocean = 1.0 - land[...].astype(f32)
    for fetch in fetches:
        fetch.wait()
    copies = []
    for e in range(2):
        for c in range(2):
            at = slice(LANES * c, LANES * c + LANES)
            surface = halves[c, 64 * e : 64 * e + 64, :].reshape(8, 8, LANES)
            value = jnp.where(
                missing[e, :, :, at] == 1, surface, observed[e, :, :, at]
            )
            edges[e, :, :, at] = value * ocean[None, :, at]
        copy = pltpu.make_async_copy(
            edges.at[e], filled.at[pl.ds((days - 8) * e, 8)], sent.at[e]
        )
        copy.start()
        copies.append(copy)
    found = factor[...]
    raw = [arrived[j] for j in range(arrived.shape[0])]
    weights_t = mul(found, jnp.concatenate(raw, axis=1))
    rest = jnp.zeros((LANES - K, weights_t.shape[1]), f32)
    gram = mul_few(
        parts_of(weights_t), jnp.concatenate([weights_t, rest], axis=0), 1
    )
    basis_t[...] = mul(inverse_factor(gram), mul(found, arrived[d]))
    for copy in copies:
        copy.wait()


def swap(blocks, axes):
    return lax.all_to_all(blocks, axes, 0, 0)


def near_rows(edge_low, edge_high):
    count = lax.axis_size(PIX)
    up = [(i, i + 1) for i in range(count - 1)]
    down = [(i + 1, i) for i in range(count - 1)]
    return lax.ppermute(edge_high, PIX, up), lax.ppermute(edge_low, PIX, down)


def band_of(day_weights):
    days = day_weights.shape[0]
    slot = lax.broadcasted_iota(jnp.int32, (4 * LANES, days), 0)
    target = lax.broadcasted_iota(jnp.int32, (4 * LANES, days), 1)
    first = LANES + K
    source = jnp.where(slot < days, slot, 4 * days)
    source = jnp.where((slot >= first) & (slot < first + 3), slot - first - 3, source)
    source = jnp.where(
        (slot >= first + 3) & (slot < first + 6), slot - first - 3 + days, source
    )
    source = jnp.where(slot >= 2 * LANES, slot - 3 * LANES, source)
    source = jnp.where(slot >= 3 * LANES, slot - 3 * LANES + days, source)
    taps = day_weights.T
    return sum(
        jnp.where(source - target + RADIUS == j, taps[j : j + 1], f32(0.0))
        for j in range(2 * RADIUS + 1)
    )


def per_device(observed, missing, land, basis_start, day_weights):
    days, rows, cols = observed.shape
    day = lax.axis_index(DAY).reshape(1)
    near, far = lax.axis_size(NEAR), lax.axis_size("y")
    halo = [pltpu.VMEM((64, LANES), f32)] * 2
    halves = [pltpu.VMEM((days * rows, LANES), f32)] * 2
    edge = (K + 8, cols)
    block = (rows, K, cols)

    def add_near(joint, edges):
        joint = call(add_all_body, (far,) + joint.shape[1:], (swap(joint, NEAR),))
        return lax.optimization_barrier((joint, *edges))

    def smooth_beside(joint, low, high, modes):
        above, below = near_rows(low, high)
        joint = swap(joint, "y")
        smooth = call(smooth_body, block, (modes, above, below, land))
        return lax.optimization_barrier((joint, smooth))

    slab = pltpu.VMEM((days, rows, cols), f32)
    turned = pltpu.VMEM((rows, days, cols), f32)
    mask = pltpu.VMEM((days, rows, cols), jnp.int32)

    part = call(
        start_body,
        (rows, K + HALO, cols),
        (day, observed, missing, land, basis_start.T),
        [
            slab,
            mask,
            pltpu.VMEM((rows, cols), jnp.int32),
            pltpu.VMEM((K, days), f32),
            *halves,
            pltpu.VMEM((rows, K + HALO, cols), f32),
            pltpu.SemaphoreType.DMA((10,)),
            pltpu.SemaphoreType.DMA((8,)),
        ],
        limit=56,
        anywhere=(1, 2, 3, 4),
        out_any=(0,),
    )
    later, taps, part = lax.optimization_barrier((missing, day_weights, part))
    band = band_of(taps)
    first, gap = call(
        turn_body,
        [(rows, days, cols)] * 2,
        (observed, later, land),
        [slab, mask, *halves, *halves, turned, turned]
        + [pltpu.SemaphoreType.DMA((2,))] * 2,
        limit=56,
        anywhere=(0, 1),
        out_any=(0, 1),
    )
    arrived, first, gap, band = lax.optimization_barrier(
        (swap(part, DAY), first, gap, band)
    )
    modes = swap(call(add_rows_body, block, (arrived,)), DAY)
    joint, *edges = call(
        project_body,
        [(near, K + 16, LANES), edge, edge],
        (day, arrived, modes, first, land),
        halo,
    )
    joint, low, high = add_near(joint, edges)
    joint, smooth = smooth_beside(joint, low, high, modes)
    filled, part = call(
        refill_body,
        [(rows, days, cols), (rows, K + 8, cols)],
        (day, joint, band, smooth, first, gap, land),
        [
            pltpu.VMEM(block, f32),
            turned,
            turned,
            turned,
            pltpu.SemaphoreType.DMA((3,)),
            pltpu.SemaphoreType.DMA((8,)),
        ],
        limit=53,
        anywhere=(3, 4, 5),
        out_any=(0,),
    )
    arrived = swap(part, DAY)
    modes = swap(call(add_rows_body, block, (arrived,)), DAY)
    factor = call(factor_body, (K, LANES), (arrived,))
    joint, *edges = call(
        project_again_body,
        [(near, K + 8, LANES), edge, edge],
        (modes, filled, land, factor),
    )
    joint, low, high = add_near(joint, edges)
    joint, smooth = smooth_beside(joint, low, high, modes)
    raw, extra = call(add_last_body, [(8, K, LANES), (8, LANES)], (joint,))
    arrived = swap(raw, DAY)
    mixed, right, found = call(
        last_weights_body,
        [(days, K), (K, K), (K, K)],
        (raw, extra, band, factor),
    )
    filled = call(
        last_fill_body,
        (days, rows, cols),
        (mixed, smooth, observed, missing, land),
        halves,
    )
    basis_t, filled = call(
        finish_body,
        [(K, days), (days, rows, cols)],
        (day, arrived, band, found, right, mixed, smooth)
        + (observed, missing, land, filled),
        [
            pltpu.VMEM((2, 8, rows, cols), f32),
            pltpu.VMEM((2, 128, LANES), f32),
            pltpu.VMEM((2, 8, rows, cols), f32),
            pltpu.VMEM((2, 8, rows, cols), jnp.int32),
            pltpu.SemaphoreType.DMA((4,)),
            pltpu.SemaphoreType.DMA((2,)),
        ],
        anywhere=(7, 8, 10),
        out_any=(1,),
        alias={10: 1},
    )
    return filled, basis_t.T


def solution(mesh):
    fine = Mesh(mesh.devices.reshape(SIZES), ("zlo", "y", "core", "x", "zhi"))
    return jax.shard_map(
        per_device,
        mesh=fine,
        in_specs=(
            P(DAY, PIX, None),
            P(DAY, PIX, None),
            P(PIX, None),
            P(DAY, None),
            P(DAY, None),
        ),
        out_specs=(P(DAY, PIX, None), P(DAY, None)),
        check_vma=False,
    )
```

```python
import jax
import jax.numpy as jnp
from jax import lax
from jax.experimental import pallas as pl
from jax.experimental.pallas import tpu as pltpu
from jax.sharding import Mesh, PartitionSpec as P

RADIUS = 3
K = 32
LANES = 128
HALO = 8 * RADIUS

PIX = ("zlo", "y", "core")
DAY = ("x", "zhi")
NEAR = ("zlo", "core")
SIZES = (4, 8, 2, 4, 2)

exact = lax.Precision.HIGHEST
smoothing = 0.2
f32 = jnp.float32
bf16 = jnp.bfloat16


def mul(a, b):
    return lax.dot_general(
        a, b, (((1,), (0,)), ((), ())), precision=exact, preferred_element_type=f32
    )


def mul_t(a, b):
    return lax.dot_general(
        a, b, (((1,), (1,)), ((), ())), precision=exact, preferred_element_type=f32
    )


def split(x):
    high = x.astype(bf16)
    rest = x - high.astype(f32)
    middle = rest.astype(bf16)
    return high, middle, (rest - middle.astype(f32)).astype(bf16)


def parts_of(a):
    return jnp.concatenate(split(a), axis=0)


def mul_few(stack, b, over=0):
    rows = stack.shape[0] // 3
    total = None
    for i, part in enumerate(split(b)):
        found = lax.dot_general(
            stack[: rows * (3 - i)],
            part,
            (((1,), (over,)), ((), ())),
            preferred_element_type=f32,
        )
        for j in range(3 - i):
            piece = found[rows * j : rows * j + rows]
            total = piece if total is None else total + piece
    return total


def deep_parts_of(a):
    high, middle, low = split(a)
    return jnp.concatenate([low, middle, high, middle, high, high], axis=1)


def mul_deep(stack, b):
    high, middle, low = split(b)
    right = jnp.concatenate([high, middle, low, high, middle, high], axis=0)
    return lax.dot_general(
        stack, right, (((1,), (0,)), ((), ())), preferred_element_type=f32
    )


def inverse_factor(wide):
    row = lax.broadcasted_iota(jnp.int32, (K, LANES), 0)
    lane = lax.broadcasted_iota(jnp.int32, (K, LANES), 1)
    work = jnp.where(lane < K, wide, jnp.where(lane == row + K, f32(1.0), f32(0.0)))
    done = []
    for start in range(0, K, 8):
        size = K - start
        at = lax.broadcasted_iota(jnp.int32, (size, LANES), 0)
        spread = [
            jnp.broadcast_to(work[:, start + j : start + j + 1], (size, LANES))
            for j in range(8)
        ]
        for j in range(8):
            inverse = 1.0 / spread[j][j : j + 1, :]
            column = jnp.where(at > j, spread[j], f32(0.0))
            for l in range(j + 1, 8):
                spread[l] = spread[l] - column * (spread[l][j : j + 1, :] * inverse)
            work = work - column * (work[j : j + 1, :] * inverse)
        done.append(work[:8])
        work = work[8:]
    work = jnp.concatenate(done, axis=0)
    pivots = jnp.sum(jnp.where(lane == row, work, f32(0.0)), axis=1, keepdims=True)
    work = work * (1.0 / jnp.sqrt(pivots))
    return pltpu.roll(work, LANES - K, 1)[:, :K]


def unpack_gram(packed):
    return jnp.concatenate(
        [packed] + [pltpu.roll(packed, LANES - K * a, 1) for a in range(1, 4)], axis=0
    )


def pack_rows(wide):
    packed = wide[:8]
    for a in range(1, 4):
        packed = packed + pltpu.roll(wide[8 * a : 8 * a + 8], K * a, 1)
    return packed


def pack_gram(weights_t):
    rest = jnp.zeros((LANES - K, LANES), f32)
    return pack_rows(mul_t(weights_t, jnp.concatenate([weights_t, rest], axis=0)))


def total_of(arrived):
    total = arrived[0]
    for j in range(1, arrived.shape[0]):
        total = total + arrived[j]
    return total


def call(body, outs, args, scratch=(), limit=8, anywhere=(), alias=None, out_any=()):
    specs = []
    for i, a in enumerate(args):
        space = pltpu.SMEM if a.ndim == 1 else pltpu.VMEM
        specs.append(pl.BlockSpec(memory_space=pl.ANY if i in anywhere else space))
    many = isinstance(outs, list)
    shapes = [
        s if isinstance(s, jax.ShapeDtypeStruct) else jax.ShapeDtypeStruct(s, f32)
        for s in (outs if many else [outs])
    ]
    out_specs = [
        pl.BlockSpec(memory_space=pl.ANY if i in out_any else pltpu.VMEM)
        for i in range(len(shapes))
    ]
    return pl.pallas_call(
        body,
        out_shape=shapes if many else shapes[0],
        in_specs=specs,
        out_specs=out_specs if many else out_specs[0],
        scratch_shapes=list(scratch),
        input_output_aliases=alias or {},
        compiler_params=pltpu.CompilerParams(vmem_limit_bytes=limit * 1024 * 1024),
        cost_estimate=pl.CostEstimate(
            flops=1_000_000, bytes_accessed=1_000_000, transcendentals=0
        ),
    )(*args)


def rows_of(halves, start, size):
    return jnp.concatenate(
        [half[pl.ds(start, size, stride=8), :] for half in halves], axis=1
    )


def start_body(
    day,
    observed_hbm,
    missing_hbm,
    land_hbm,
    basis_hbm,
    out_hbm,
    observed,
    missing,
    land,
    basis_t,
    half_0,
    half_1,
    out,
    arrivals,
    sent,
):
    parts = 4
    days = observed.shape[0]
    size = days // parts
    small = [
        pltpu.make_async_copy(land_hbm, land, arrivals.at[2 * parts]),
        pltpu.make_async_copy(basis_hbm, basis_t, arrivals.at[2 * parts + 1]),
    ]
    for copy in small:
        copy.start()
    copies = []
    for i in range(parts):
        at = pl.ds(size * i, size)
        for c, (source, target) in enumerate(
            ((missing_hbm, missing), (observed_hbm, observed))
        ):
            copies.append(
                pltpu.make_async_copy(
                    source.at[at], target.at[at], arrivals.at[2 * i + c]
                )
            )
            copies[-1].start()
    d = day[0]
    halves = (half_0, half_1)
    out[:, K:, :] = jnp.zeros((8, HALO, out.shape[2]), f32)
    for copy in small:
        copy.wait()
    ocean = 1.0 - land[...].astype(f32)
    for i in range(parts):
        copies[2 * i].wait()
        copies[2 * i + 1].wait()
        now = slice(size * i, size * i + size)
        for c, half in enumerate(halves):
            at = slice(LANES * c, LANES * c + LANES)
            tile = jnp.where(missing[now, :, at] == 1, f32(0.0), observed[now, :, at])
            tile = tile * ocean[None, :, at]
            half[8 * size * i : 8 * size * (i + 1), :] = tile.reshape(8 * size, LANES)
    low, high = jnp.maximum(d - 1, 0), jnp.minimum(d + 1, 7)
    for t in range(RADIUS):
        for target, source in ((low, t), (high, days - RADIUS + t)):
            tile = [half[8 * source : 8 * source + 8, :] for half in halves]
            out[target, K + 8 * t : K + 8 * t + 8, :] = jnp.concatenate(tile, axis=1)
    weights = parts_of(basis_t[...])
    copies = []
    for r in range(8):
        out[r, :K, :] = mul_few(weights, rows_of(halves, r, days))
        copies.append(pltpu.make_async_copy(out.at[r], out_hbm.at[r], sent.at[r]))
        copies[-1].start()
    for copy in copies:
        copy.wait()


def turn_body(
    observed_hbm,
    missing_hbm,
    land,
    first_hbm,
    gap_hbm,
    observed,
    missing,
    half_0,
    half_1,
    mask_0,
    mask_1,
    first,
    gap,
    arrivals,
    sent,
):
    pairs = ((missing_hbm, missing), (observed_hbm, observed))
    copies = [
        pltpu.make_async_copy(source, target, arrivals.at[i])
        for i, (source, target) in enumerate(pairs)
    ]
    for copy in copies:
        copy.start()
    for copy in copies:
        copy.wait()
    days = missing.shape[0]
    ocean = 1.0 - land[...].astype(f32)
    halves, masks = (half_0, half_1), (mask_0, mask_1)
    for c in range(2):
        at = slice(LANES * c, LANES * c + LANES)
        absent = missing[:, :, at] == 1
        tile = jnp.where(absent, f32(0.0), observed[:, :, at]) * ocean[None, :, at]
        halves[c][...] = tile.reshape(8 * days, LANES)
        masks[c][...] = absent.astype(f32).reshape(8 * days, LANES)
    for r in range(8):
        first[r] = rows_of(halves, r, days)
        gap[r] = rows_of(masks, r, days).astype(bf16)
    copies = [
        pltpu.make_async_copy(first, first_hbm, sent.at[0]),
        pltpu.make_async_copy(gap, gap_hbm, sent.at[1]),
    ]
    for copy in copies:
        copy.start()
    for copy in copies:
        copy.wait()


def add_rows_body(arrived, out):
    total = arrived[0, :K, :]
    for j in range(1, arrived.shape[0]):
        total = total + arrived[j, :K, :]
    for j in range(out.shape[0]):
        out[j] = total


def add_all_body(arrived, out):
    total = total_of(arrived)
    for j in range(out.shape[0]):
        out[j] = total


def add_last_body(arrived, out, extra):
    total = total_of(arrived)
    for j in range(out.shape[0]):
        out[j] = total[:K]
    extra[...] = total[K:]


def factor_body(arrived, out):
    packed = arrived[0, K:, :LANES]
    for j in range(1, arrived.shape[0]):
        packed = packed + arrived[j, K:, :LANES]
    out[:, :K] = inverse_factor(unpack_gram(packed))
    out[:, K:] = jnp.zeros((K, LANES - K), f32)


def edges_of(day, modes, land, edge_near, edge_far):
    ocean = 1.0 - land[...].astype(f32)
    upper = day[1] == 0
    for edge, r, q in ((edge_near, 7, 0), (edge_far, 0, 7)):
        edge[:K, :] = jnp.where(upper, modes[r], modes[q])
        flag = jnp.where(upper, ocean[r : r + 1], ocean[q : q + 1])
        edge[K:, :] = jnp.broadcast_to(flag, (8, ocean.shape[1]))


def project_again_body(day, modes, filled, land, factor, out, edge_near, edge_far):
    cols = modes.shape[2]
    wide = jnp.concatenate([modes[r] for r in range(8)], axis=1)
    wide = mul_deep(deep_parts_of(factor[:, :K]), wide)
    pad = jnp.zeros((LANES - K, cols), f32)
    total = jnp.zeros((K, 2 * LANES), f32)
    for r in range(8):
        modes_u = wide[:, cols * r : cols * r + cols]
        right = jnp.concatenate([filled[r], modes_u, pad], axis=0)
        total = total + mul_few(parts_of(modes_u), right, 1)
    packed = pack_rows(total[:, LANES:])
    for j in range(out.shape[0]):
        out[j, :K, :] = total[:, :LANES]
        out[j, K:, :] = packed
    edges_of(day, modes, land, edge_near, edge_far)


def project_body(
    day, arrived, modes, filled, land, out, edge_near, edge_far, halo_0, halo_1
):
    d = day[0]
    low = arrived[jnp.maximum(d - 1, 0), K : K + HALO, :]
    high = arrived[jnp.minimum(d + 1, 7), K : K + HALO, :]
    low = jnp.where(d > 0, low, f32(0.0))
    high = jnp.where(d < 7, high, f32(0.0))
    cols = modes.shape[2]
    for c, halo in enumerate((halo_0, halo_1)):
        halo[:HALO, :] = low[:, LANES * c : LANES * c + LANES]
        halo[HALO : 2 * HALO, :] = high[:, LANES * c : LANES * c + LANES]
        halo[2 * HALO :, :] = jnp.zeros((64 - 2 * HALO, LANES), f32)
    pad = jnp.zeros((LANES - K - 8, cols), f32)
    total = jnp.zeros((K, 2 * LANES), f32)
    for r in range(8):
        modes_u = modes[r]
        days_near = rows_of((halo_0, halo_1), r, 8)
        right = jnp.concatenate([filled[r], modes_u, days_near, pad], axis=0)
        total = total + mul_few(parts_of(modes_u), right, 1)
    extra = total[:, LANES:]
    packed = extra[:16] + pltpu.roll(extra[16:], 64, 1)
    for j in range(out.shape[0]):
        out[j, :K, :] = total[:, :LANES]
        out[j, K:, :] = packed
    edges_of(day, modes, land, edge_near, edge_far)


def smooth_body(day, modes, near, far, land, out):
    upper = day[1] == 0
    above = jnp.where(upper, far[...], near[...])
    below = jnp.where(upper, near[...], far[...])
    cols = out.shape[2]
    lane = lax.broadcasted_iota(jnp.int32, (1, cols), 1)
    ocean = 1.0 - land[...].astype(f32)
    rows = [above[:K, :]] + [modes[r] for r in range(8)] + [below[:K, :]]
    flags = (
        [above[K : K + 1, :]]
        + [ocean[r : r + 1] for r in range(8)]
        + [below[K : K + 1, :]]
    )
    for r in range(8):
        here, flag = rows[r + 1], flags[r + 1]
        left = jnp.where(lane > 0, pltpu.roll(flag, 1, 1), f32(0.0))
        right = jnp.where(lane < cols - 1, pltpu.roll(flag, cols - 1, 1), f32(0.0))
        up, down = flags[r], flags[r + 2]
        centre = 1.0 - smoothing * (up + down + left + right)
        spread = (
            up * rows[r]
            + down * rows[r + 2]
            + left * pltpu.roll(here, 1, 1)
            + right * pltpu.roll(here, cols - 1, 1)
        )
        out[r] = centre * here + smoothing * spread


def refill_body(
    day,
    arrived,
    band,
    smooth_hbm,
    first_hbm,
    gap_hbm,
    land,
    filled_hbm,
    out_hbm,
    smooth,
    first,
    gap,
    filled,
    out,
    arrivals,
    sent,
):
    def start(source, target, semaphore):
        copy = pltpu.make_async_copy(source, target, semaphore)
        copy.start()
        return copy

    waits = [start(smooth_hbm, smooth, arrivals.at[16])]
    fetches = [
        (
            start(first_hbm.at[r], first.at[r], arrivals.at[2 * r]),
            start(gap_hbm.at[r], gap.at[r], arrivals.at[2 * r + 1]),
        )
        for r in range(8)
    ]
    total = total_of(arrived)
    extra = jnp.concatenate([total[K:], pltpu.roll(total[K:], 64, 1)], axis=0)
    raw = jnp.concatenate([total[:K], extra], axis=1)
    tempered_t = mul(raw, band[: 2 * LANES, :]).T
    factor = inverse_factor(extra)
    weights_t = mul(factor, total[:K])
    mixed = deep_parts_of(mul(tempered_t, mul(factor.T, factor)))
    weights = parts_of(weights_t)
    cols = filled.shape[2]
    packed = pack_gram(weights_t)
    for j in range(8):
        out[j, K:, :LANES] = packed
        out[j, K:, LANES:] = jnp.zeros((8, cols - LANES), f32)
    ocean = 1.0 - land[...].astype(f32)
    for copy in waits:
        copy.wait()
    sends = []
    for r in range(0, 8, 2):
        for copy in fetches[r] + fetches[r + 1]:
            copy.wait()
        for q in (r, r + 1):
            surface = mul_deep(mixed, smooth[q])
            absent = gap[q].astype(f32) == 1
            now = jnp.where(absent, surface * ocean[q : q + 1], first[q])
            filled[q] = now
            out[q, :K, :] = mul_few(weights, now)
        for q in (r, r + 1):
            sends.append(start(filled.at[q], filled_hbm.at[q], sent.at[2 * q]))
            sends.append(start(out.at[q], out_hbm.at[q], sent.at[2 * q + 1]))
    for copy in sends:
        copy.wait()


def last_weights_body(raw, extra, band, scale, mixed, right, factor):
    tempered_t = mul(raw[0], band[:LANES, :]).T
    found = inverse_factor(unpack_gram(extra[...]))
    inner = mul(found.T, mul(found, scale[:, :K]))
    mixed[...] = mul(tempered_t, inner)
    right[...] = inner
    factor[...] = found


def last_fill_body(mixed, smooth, observed, missing, land, out, *halves):
    days = observed.shape[0]
    ocean = 1.0 - land[...].astype(f32)
    mix = deep_parts_of(mixed[...])
    for r in range(8):
        surface = mul_deep(mix, smooth[r])
        for c, half in enumerate(halves):
            half[pl.ds(r, days, stride=8), :] = surface[:, LANES * c : LANES * c + LANES]
    for c, half in enumerate(halves):
        at = slice(LANES * c, LANES * c + LANES)
        surface = half[...].reshape(days, 8, LANES)
        value = jnp.where(missing[:, :, at] == 1, surface, observed[:, :, at])
        out[:, :, at] = value * ocean[None, :, at]


def finish_body(
    day,
    arrived,
    band,
    factor,
    right,
    mixed,
    smooth,
    observed_low,
    observed_high,
    missing_low,
    missing_high,
    land,
    filled_in,
    basis_t,
    filled,
    edges,
    halves,
    sent,
):
    del filled_in
    d = day[0]
    low = arrived[jnp.maximum(d - 1, 0)]
    high = arrived[jnp.minimum(d + 1, 7)]
    low = jnp.where(d > 0, low, f32(0.0))
    high = jnp.where(d < 7, high, f32(0.0))
    near = mul(jnp.concatenate([low, high], axis=1), band[2 * LANES :, :]).T
    near = mixed[...] + mul(near, right[...])
    days = near.shape[0]
    near = jnp.concatenate([near[:8], near[days - 8 :]], axis=0)
    near = deep_parts_of(near)
    for r in range(8):
        surface = mul_deep(near, smooth[r])
        for c in range(2):
            halves[c, pl.ds(r, 16, stride=8), :] = surface[:, LANES * c : LANES * c + LANES]
    ocean = 1.0 - land[...].astype(f32)
    sides = ((observed_low, missing_low), (observed_high, missing_high))
    copies = []
    for e, (observed, missing) in enumerate(sides):
        for c in range(2):
            at = slice(LANES * c, LANES * c + LANES)
            surface = halves[c, 64 * e : 64 * e + 64, :].reshape(8, 8, LANES)
            value = jnp.where(missing[:, :, at] == 1, surface, observed[:, :, at])
            edges[e, :, :, at] = value * ocean[None, :, at]
        copy = pltpu.make_async_copy(
            edges.at[e], filled.at[pl.ds((days - 8) * e, 8)], sent.at[e]
        )
        copy.start()
        copies.append(copy)
    found = factor[...]
    raw = [arrived[j] for j in range(arrived.shape[0])]
    weights_t = mul(found, jnp.concatenate(raw, axis=1))
    rest = jnp.zeros((LANES - K, weights_t.shape[1]), f32)
    gram = mul_few(
        parts_of(weights_t), jnp.concatenate([weights_t, rest], axis=0), 1
    )
    basis_t[...] = mul(inverse_factor(gram), mul(found, arrived[d]))
    for copy in copies:
        copy.wait()


def swap(blocks, axes):
    return lax.all_to_all(blocks, axes, 0, 0)


def near_rows(edge_near, edge_far):
    count = lax.axis_size(PIX)
    up = [(i, i + 1) for i in range(1, count - 1, 2)]
    down = [(i + 1, i) for i in range(1, count - 1, 2)]
    near = lax.ppermute(edge_near, "core", [(0, 1), (1, 0)])
    return near, lax.ppermute(edge_far, PIX, up + down)


def band_of(day_weights):
    days = day_weights.shape[0]
    slot = lax.broadcasted_iota(jnp.int32, (4 * LANES, days), 0)
    target = lax.broadcasted_iota(jnp.int32, (4 * LANES, days), 1)
    first = LANES + K
    source = jnp.where(slot < days, slot, 4 * days)
    source = jnp.where((slot >= first) & (slot < first + 3), slot - first - 3, source)
    source = jnp.where(
        (slot >= first + 3) & (slot < first + 6), slot - first - 3 + days, source
    )
    source = jnp.where(slot >= 2 * LANES, slot - 3 * LANES, source)
    source = jnp.where(slot >= 3 * LANES, slot - 3 * LANES + days, source)
    taps = day_weights.T
    return sum(
        jnp.where(source - target + RADIUS == j, taps[j : j + 1], f32(0.0))
        for j in range(2 * RADIUS + 1)
    )


def per_device(observed, missing, land, basis_start, day_weights):
    days, rows, cols = observed.shape
    day = jnp.stack([lax.axis_index(DAY), lax.axis_index("core")])
    near, far = lax.axis_size(NEAR), lax.axis_size("y")
    halo = [pltpu.VMEM((64, LANES), f32)] * 2
    halves = [pltpu.VMEM((days * rows, LANES), f32)] * 2
    edge = (K + 8, cols)
    block = (rows, K, cols)

    def add_near(joint, edges):
        joint = call(add_all_body, (far,) + joint.shape[1:], (swap(joint, NEAR),))
        return lax.optimization_barrier((joint, *edges))

    def smooth_beside(joint, low, high, modes):
        beside, beyond = near_rows(low, high)
        joint = swap(joint, "y")
        smooth = call(smooth_body, block, (day, modes, beside, beyond, land))
        return lax.optimization_barrier((joint, smooth))

    slab = pltpu.VMEM((days, rows, cols), f32)
    turned = pltpu.VMEM((rows, days, cols), f32)
    mask = pltpu.VMEM((days, rows, cols), jnp.int32)

    part = call(
        start_body,
        (rows, K + HALO, cols),
        (day, observed, missing, land, basis_start.T),
        [
            slab,
            mask,
            pltpu.VMEM((rows, cols), jnp.int32),
            pltpu.VMEM((K, days), f32),
            *halves,
            pltpu.VMEM((rows, K + HALO, cols), f32),
            pltpu.SemaphoreType.DMA((10,)),
            pltpu.SemaphoreType.DMA((8,)),
        ],
        limit=56,
        anywhere=(1, 2, 3, 4),
        out_any=(0,),
    )
    later, taps, part = lax.optimization_barrier((missing, day_weights, part))
    band = band_of(taps)
    first, gap = call(
        turn_body,
        [(rows, days, cols), jax.ShapeDtypeStruct((rows, days, cols), bf16)],
        (observed, later, land),
        [slab, mask, *halves, *halves, turned, pltpu.VMEM((rows, days, cols), bf16)]
        + [pltpu.SemaphoreType.DMA((2,))] * 2,
        limit=56,
        anywhere=(0, 1),
        out_any=(0, 1),
    )
    arrived, first, gap, band = lax.optimization_barrier(
        (swap(part, DAY), first, gap, band)
    )
    modes = swap(call(add_rows_body, block, (arrived,)), DAY)
    joint, *edges = call(
        project_body,
        [(near, K + 16, LANES), edge, edge],
        (day, arrived, modes, first, land),
        halo,
    )
    joint, low, high = add_near(joint, edges)
    joint, smooth = smooth_beside(joint, low, high, modes)
    filled, part = call(
        refill_body,
        [(rows, days, cols), (rows, K + 8, cols)],
        (day, joint, band, smooth, first, gap, land),
        [
            pltpu.VMEM(block, f32),
            turned,
            pltpu.VMEM((rows, days, cols), bf16),
            turned,
            pltpu.VMEM((rows, K + 8, cols), f32),
            pltpu.SemaphoreType.DMA((17,)),
            pltpu.SemaphoreType.DMA((16,)),
        ],
        limit=53,
        anywhere=(3, 4, 5),
        out_any=(0, 1),
    )
    arrived = swap(part, DAY)
    modes = swap(call(add_rows_body, block, (arrived,)), DAY)
    factor = call(factor_body, (K, LANES), (arrived,))
    joint, *edges = call(
        project_again_body,
        [(near, K + 8, LANES), edge, edge],
        (day, modes, filled, land, factor),
    )
    joint, low, high = add_near(joint, edges)
    joint, smooth = smooth_beside(joint, low, high, modes)
    raw, extra = call(add_last_body, [(8, K, LANES), (8, LANES)], (joint,))
    arrived = swap(raw, DAY)
    mixed, right, found = call(
        last_weights_body,
        [(days, K), (K, K), (K, K)],
        (raw, extra, band, factor),
    )
    filled = call(
        last_fill_body,
        (days, rows, cols),
        (mixed, smooth, observed, missing, land),
        halves,
    )
    ends = (slice(0, 8), slice(days - 8, days))
    basis_t, filled = call(
        finish_body,
        [(K, days), (days, rows, cols)],
        (day, arrived, band, found, right, mixed, smooth)
        + tuple(observed[e] for e in ends)
        + tuple(missing[e] for e in ends)
        + (land, filled),
        [
            pltpu.VMEM((2, 8, rows, cols), f32),
            pltpu.VMEM((2, 128, LANES), f32),
            pltpu.SemaphoreType.DMA((2,)),
        ],
        anywhere=(12,),
        out_any=(1,),
        alias={12: 1},
    )
    return filled, basis_t.T


def solution(mesh):
    fine = Mesh(mesh.devices.reshape(SIZES), ("zlo", "y", "core", "x", "zhi"))
    return jax.shard_map(
        per_device,
        mesh=fine,
        in_specs=(
            P(DAY, PIX, None),
            P(DAY, PIX, None),
            P(PIX, None),
            P(DAY, None),
            P(DAY, None),
        ),
        out_specs=(P(DAY, PIX, None), P(DAY, None)),
        check_vma=False,
    )
```

```python
import jax
import jax.numpy as jnp
from jax import lax
from jax.experimental import pallas as pl
from jax.experimental.pallas import tpu as pltpu
from jax.sharding import Mesh, PartitionSpec as P

RADIUS = 3
K = 32
LANES = 128
HALO = 8 * RADIUS

PIX = ("zlo", "y", "core")
DAY = ("x", "zhi")
NEAR = ("zlo", "core")
SIZES = (4, 8, 2, 4, 2)

exact = lax.Precision.HIGHEST
smoothing = 0.2
f32 = jnp.float32
bf16 = jnp.bfloat16


def mul(a, b):
    return lax.dot_general(
        a, b, (((1,), (0,)), ((), ())), precision=exact, preferred_element_type=f32
    )


def mul_t(a, b):
    return lax.dot_general(
        a, b, (((1,), (1,)), ((), ())), precision=exact, preferred_element_type=f32
    )


def split(x):
    high = x.astype(bf16)
    rest = x - high.astype(f32)
    middle = rest.astype(bf16)
    return high, middle, (rest - middle.astype(f32)).astype(bf16)


def parts_of(a):
    return jnp.concatenate(split(a), axis=0)


def mul_few(stack, b, over=0):
    rows = stack.shape[0] // 3
    total = None
    for i, part in enumerate(split(b)):
        found = lax.dot_general(
            stack[: rows * (3 - i)],
            part,
            (((1,), (over,)), ((), ())),
            preferred_element_type=f32,
        )
        for j in range(3 - i):
            piece = found[rows * j : rows * j + rows]
            total = piece if total is None else total + piece
    return total


def deep_parts_of(a):
    high, middle, low = split(a)
    return jnp.concatenate([low, middle, high, middle, high, high], axis=1)


def mul_deep(stack, b):
    high, middle, low = split(b)
    right = jnp.concatenate([high, middle, low, high, middle, high], axis=0)
    return lax.dot_general(
        stack, right, (((1,), (0,)), ((), ())), preferred_element_type=f32
    )


def inverse_factor(wide):
    row = lax.broadcasted_iota(jnp.int32, (K, LANES), 0)
    lane = lax.broadcasted_iota(jnp.int32, (K, LANES), 1)
    work = jnp.where(lane < K, wide, jnp.where(lane == row + K, f32(1.0), f32(0.0)))
    done = []
    for start in range(0, K, 8):
        size = K - start
        at = lax.broadcasted_iota(jnp.int32, (size, LANES), 0)
        spread = [
            jnp.broadcast_to(work[:, start + j : start + j + 1], (size, LANES))
            for j in range(8)
        ]
        for j in range(8):
            inverse = 1.0 / spread[j][j : j + 1, :]
            column = jnp.where(at > j, spread[j], f32(0.0))
            for l in range(j + 1, 8):
                spread[l] = spread[l] - column * (spread[l][j : j + 1, :] * inverse)
            work = work - column * (work[j : j + 1, :] * inverse)
        done.append(work[:8])
        work = work[8:]
    work = jnp.concatenate(done, axis=0)
    pivots = jnp.sum(jnp.where(lane == row, work, f32(0.0)), axis=1, keepdims=True)
    work = work * (1.0 / jnp.sqrt(pivots))
    return pltpu.roll(work, LANES - K, 1)[:, :K]


def unpack_gram(packed):
    return jnp.concatenate(
        [packed] + [pltpu.roll(packed, LANES - K * a, 1) for a in range(1, 4)], axis=0
    )


def pack_rows(wide):
    packed = wide[:8]
    for a in range(1, 4):
        packed = packed + pltpu.roll(wide[8 * a : 8 * a + 8], K * a, 1)
    return packed


def pack_gram(weights_t):
    rest = jnp.zeros((LANES - K, LANES), f32)
    return pack_rows(mul_t(weights_t, jnp.concatenate([weights_t, rest], axis=0)))


def total_of(arrived):
    total = arrived[0]
    for j in range(1, arrived.shape[0]):
        total = total + arrived[j]
    return total


def call(body, outs, args, scratch=(), limit=8, anywhere=(), alias=None, out_any=()):
    specs = []
    for i, a in enumerate(args):
        space = pltpu.SMEM if a.ndim == 1 else pltpu.VMEM
        specs.append(pl.BlockSpec(memory_space=pl.ANY if i in anywhere else space))
    many = isinstance(outs, list)
    shapes = [
        s if isinstance(s, jax.ShapeDtypeStruct) else jax.ShapeDtypeStruct(s, f32)
        for s in (outs if many else [outs])
    ]
    out_specs = [
        pl.BlockSpec(memory_space=pl.ANY if i in out_any else pltpu.VMEM)
        for i in range(len(shapes))
    ]
    return pl.pallas_call(
        body,
        out_shape=shapes if many else shapes[0],
        in_specs=specs,
        out_specs=out_specs if many else out_specs[0],
        scratch_shapes=list(scratch),
        input_output_aliases=alias or {},
        compiler_params=pltpu.CompilerParams(vmem_limit_bytes=limit * 1024 * 1024),
        cost_estimate=pl.CostEstimate(
            flops=1_000_000, bytes_accessed=1_000_000, transcendentals=0
        ),
    )(*args)


def rows_of(halves, start, size):
    return jnp.concatenate(
        [half[pl.ds(start, size, stride=8), :] for half in halves], axis=1
    )


def start_body(
    day,
    observed_hbm,
    missing_hbm,
    land_hbm,
    basis_hbm,
    out_hbm,
    observed,
    missing,
    land,
    basis_t,
    half_0,
    half_1,
    out,
    arrivals,
    sent,
):
    parts = 4
    days = observed.shape[0]
    size = days // parts
    small = [
        pltpu.make_async_copy(land_hbm, land, arrivals.at[2 * parts]),
        pltpu.make_async_copy(basis_hbm, basis_t, arrivals.at[2 * parts + 1]),
    ]
    for copy in small:
        copy.start()
    copies = []
    for i in range(parts):
        at = pl.ds(size * i, size)
        for c, (source, target) in enumerate(
            ((missing_hbm, missing), (observed_hbm, observed))
        ):
            copies.append(
                pltpu.make_async_copy(
                    source.at[at], target.at[at], arrivals.at[2 * i + c]
                )
            )
            copies[-1].start()
    d = day[0]
    halves = (half_0, half_1)
    out[:, K:, :] = jnp.zeros((8, HALO, out.shape[2]), f32)
    for copy in small:
        copy.wait()
    ocean = 1.0 - land[...].astype(f32)
    for i in range(parts):
        copies[2 * i].wait()
        copies[2 * i + 1].wait()
        now = slice(size * i, size * i + size)
        for c, half in enumerate(halves):
            at = slice(LANES * c, LANES * c + LANES)
            tile = jnp.where(missing[now, :, at] == 1, f32(0.0), observed[now, :, at])
            tile = tile * ocean[None, :, at]
            half[8 * size * i : 8 * size * (i + 1), :] = tile.reshape(8 * size, LANES)
    low, high = jnp.maximum(d - 1, 0), jnp.minimum(d + 1, 7)
    for t in range(RADIUS):
        for target, source in ((low, t), (high, days - RADIUS + t)):
            tile = [half[8 * source : 8 * source + 8, :] for half in halves]
            out[target, K + 8 * t : K + 8 * t + 8, :] = jnp.concatenate(tile, axis=1)
    weights = parts_of(basis_t[...])
    copies = []
    for r in range(8):
        out[r, :K, :] = mul_few(weights, rows_of(halves, r, days))
        copies.append(pltpu.make_async_copy(out.at[r], out_hbm.at[r], sent.at[r]))
        copies[-1].start()
    for copy in copies:
        copy.wait()


def turn_body(
    observed_hbm,
    missing_hbm,
    land,
    first_hbm,
    gap_hbm,
    observed,
    missing,
    half_0,
    half_1,
    mask_0,
    mask_1,
    first,
    gap,
    arrivals,
    sent,
):
    pairs = ((missing_hbm, missing), (observed_hbm, observed))
    copies = [
        pltpu.make_async_copy(source, target, arrivals.at[i])
        for i, (source, target) in enumerate(pairs)
    ]
    for copy in copies:
        copy.start()
    for copy in copies:
        copy.wait()
    days = missing.shape[0]
    ocean = 1.0 - land[...].astype(f32)
    halves, masks = (half_0, half_1), (mask_0, mask_1)
    for c in range(2):
        at = slice(LANES * c, LANES * c + LANES)
        absent = missing[:, :, at] == 1
        tile = jnp.where(absent, f32(0.0), observed[:, :, at]) * ocean[None, :, at]
        halves[c][...] = tile.reshape(8 * days, LANES)
        masks[c][...] = absent.astype(f32).reshape(8 * days, LANES)
    for r in range(8):
        first[r] = rows_of(halves, r, days)
        gap[r] = rows_of(masks, r, days).astype(bf16)
    copies = [
        pltpu.make_async_copy(first, first_hbm, sent.at[0]),
        pltpu.make_async_copy(gap, gap_hbm, sent.at[1]),
    ]
    for copy in copies:
        copy.start()
    for copy in copies:
        copy.wait()


def add_rows_body(arrived, out):
    total = arrived[0, :K, :]
    for j in range(1, arrived.shape[0]):
        total = total + arrived[j, :K, :]
    for j in range(out.shape[0]):
        out[j] = total


def add_all_body(arrived, out):
    total = total_of(arrived)
    for j in range(out.shape[0]):
        out[j] = total


def add_last_body(arrived, out, extra):
    total = total_of(arrived)
    for j in range(out.shape[0]):
        out[j] = total[:K]
    extra[...] = total[K:]


def factor_body(arrived, out):
    packed = arrived[0, K:, :LANES]
    for j in range(1, arrived.shape[0]):
        packed = packed + arrived[j, K:, :LANES]
    out[:, :K] = inverse_factor(unpack_gram(packed))
    out[:, K:] = jnp.zeros((K, LANES - K), f32)


def edges_of(modes, land, edge_low, edge_high):
    ocean = 1.0 - land[...].astype(f32)
    for edge, r in ((edge_low, 0), (edge_high, 7)):
        edge[:K, :] = modes[r]
        edge[K:, :] = jnp.broadcast_to(ocean[r : r + 1], (8, ocean.shape[1]))


class Products:
    def __init__(self, count):
        self.count = count
        self.totals = [jnp.zeros((count, K * (3 - i)), f32) for i in range(3)]

    def add(self, few, many):
        stack = parts_of(few)
        for i, part in enumerate(split(many)):
            self.totals[i] = self.totals[i] + lax.dot_general(
                part,
                stack[: K * (3 - i)],
                (((1,), (1,)), ((), ())),
                preferred_element_type=f32,
            )

    def result(self):
        found = None
        for i, total in enumerate(self.totals):
            tall = ((0, 2 * LANES - self.count), (0, LANES - total.shape[1]))
            total = jnp.pad(total, tall).T
            for j in range(3 - i):
                piece = total[K * j : K * j + K]
                found = piece if found is None else found + piece
        return found


def project_again_body(modes, filled, land, factor, out, edge_low, edge_high):
    cols = modes.shape[2]
    wide = jnp.concatenate([modes[r] for r in range(8)], axis=1)
    wide = mul_deep(deep_parts_of(factor[:, :K]), wide)
    products = Products(LANES + K)
    for r in range(8):
        modes_u = wide[:, cols * r : cols * r + cols]
        products.add(modes_u, jnp.concatenate([filled[r], modes_u], axis=0))
    total = products.result()
    packed = pack_rows(total[:, LANES:])
    for j in range(out.shape[0]):
        out[j, :K, :] = total[:, :LANES]
        out[j, K:, :] = packed
    edges_of(modes, land, edge_low, edge_high)


def project_body(
    day, arrived, modes, filled, land, out, edge_low, edge_high, halo_0, halo_1
):
    d = day[0]
    low = arrived[jnp.maximum(d - 1, 0), K : K + HALO, :]
    high = arrived[jnp.minimum(d + 1, 7), K : K + HALO, :]
    low = jnp.where(d > 0, low, f32(0.0))
    high = jnp.where(d < 7, high, f32(0.0))
    cols = modes.shape[2]
    for c, halo in enumerate((halo_0, halo_1)):
        halo[:HALO, :] = low[:, LANES * c : LANES * c + LANES]
        halo[HALO : 2 * HALO, :] = high[:, LANES * c : LANES * c + LANES]
        halo[2 * HALO :, :] = jnp.zeros((64 - 2 * HALO, LANES), f32)
    pad = jnp.zeros((8, cols), f32)
    products = Products(LANES + K + 16)
    for r in range(8):
        modes_u = modes[r]
        days_near = rows_of((halo_0, halo_1), r, 8)
        right = jnp.concatenate([filled[r], modes_u, days_near, pad], axis=0)
        products.add(modes_u, right)
    total = products.result()
    extra = total[:, LANES:]
    packed = extra[:16] + pltpu.roll(extra[16:], 64, 1)
    for j in range(out.shape[0]):
        out[j, :K, :] = total[:, :LANES]
        out[j, K:, :] = packed
    edges_of(modes, land, edge_low, edge_high)


def smooth_body(modes, above, below, land, out):
    cols = out.shape[2]
    lane = lax.broadcasted_iota(jnp.int32, (1, cols), 1)
    ocean = 1.0 - land[...].astype(f32)
    rows = [above[:K, :]] + [modes[r] for r in range(8)] + [below[:K, :]]
    flags = (
        [above[K : K + 1, :]]
        + [ocean[r : r + 1] for r in range(8)]
        + [below[K : K + 1, :]]
    )
    for r in range(8):
        here, flag = rows[r + 1], flags[r + 1]
        left = jnp.where(lane > 0, pltpu.roll(flag, 1, 1), f32(0.0))
        right = jnp.where(lane < cols - 1, pltpu.roll(flag, cols - 1, 1), f32(0.0))
        up, down = flags[r], flags[r + 2]
        centre = 1.0 - smoothing * (up + down + left + right)
        spread = (
            up * rows[r]
            + down * rows[r + 2]
            + left * pltpu.roll(here, 1, 1)
            + right * pltpu.roll(here, cols - 1, 1)
        )
        out[r] = centre * here + smoothing * spread


def refill_body(
    day,
    arrived,
    band,
    smooth_hbm,
    first_hbm,
    gap_hbm,
    land,
    filled_hbm,
    out_hbm,
    smooth,
    first,
    gap,
    filled,
    out,
    arrivals,
    sent,
):
    def start(source, target, semaphore):
        copy = pltpu.make_async_copy(source, target, semaphore)
        copy.start()
        return copy

    waits = [start(smooth_hbm, smooth, arrivals.at[16])]
    fetches = [
        (
            start(first_hbm.at[r], first.at[r], arrivals.at[2 * r]),
            start(gap_hbm.at[r], gap.at[r], arrivals.at[2 * r + 1]),
        )
        for r in range(8)
    ]
    total = total_of(arrived)
    extra = jnp.concatenate([total[K:], pltpu.roll(total[K:], 64, 1)], axis=0)
    raw = jnp.concatenate([total[:K], extra], axis=1)
    tempered_t = mul(raw, band[: 2 * LANES, :]).T
    factor = inverse_factor(extra)
    weights_t = mul(factor, total[:K])
    mixed = deep_parts_of(mul(tempered_t, mul(factor.T, factor)))
    weights = parts_of(weights_t)
    cols = filled.shape[2]
    packed = pack_gram(weights_t)
    for j in range(8):
        out[j, K:, :LANES] = packed
        out[j, K:, LANES:] = jnp.zeros((8, cols - LANES), f32)
    ocean = 1.0 - land[...].astype(f32)
    for copy in waits:
        copy.wait()
    sends = []
    for r in range(0, 8, 2):
        for copy in fetches[r] + fetches[r + 1]:
            copy.wait()
        for q in (r, r + 1):
            surface = mul_deep(mixed, smooth[q])
            absent = gap[q].astype(f32) == 1
            now = jnp.where(absent, surface * ocean[q : q + 1], first[q])
            filled[q] = now
            out[q, :K, :] = mul_few(weights, now)
        for q in (r, r + 1):
            sends.append(start(filled.at[q], filled_hbm.at[q], sent.at[2 * q]))
            sends.append(start(out.at[q], out_hbm.at[q], sent.at[2 * q + 1]))
    for copy in sends:
        copy.wait()


def last_weights_body(raw, extra, band, scale, mixed, right, factor):
    tempered_t = mul(raw[0], band[:LANES, :]).T
    found = inverse_factor(unpack_gram(extra[...]))
    inner = mul(found.T, mul(found, scale[:, :K]))
    mixed[...] = mul(tempered_t, inner)
    right[...] = inner
    factor[...] = found


def last_fill_body(mixed, smooth, observed, missing, land, out, *halves):
    days = observed.shape[0]
    ocean = 1.0 - land[...].astype(f32)
    mix = deep_parts_of(mixed[...])
    for r in range(8):
        surface = mul_deep(mix, smooth[r])
        for c, half in enumerate(halves):
            half[pl.ds(r, days, stride=8), :] = surface[:, LANES * c : LANES * c + LANES]
    for c, half in enumerate(halves):
        at = slice(LANES * c, LANES * c + LANES)
        surface = half[...].reshape(days, 8, LANES)
        value = jnp.where(missing[:, :, at] == 1, surface, observed[:, :, at])
        out[:, :, at] = value * ocean[None, :, at]


def finish_body(
    day,
    arrived,
    band,
    factor,
    right,
    mixed,
    smooth,
    observed_low,
    observed_high,
    missing_low,
    missing_high,
    land,
    filled_in,
    basis_t,
    filled,
    edges,
    halves,
    sent,
):
    del filled_in
    d = day[0]
    low = arrived[jnp.maximum(d - 1, 0)]
    high = arrived[jnp.minimum(d + 1, 7)]
    low = jnp.where(d > 0, low, f32(0.0))
    high = jnp.where(d < 7, high, f32(0.0))
    near = mul(jnp.concatenate([low, high], axis=1), band[2 * LANES :, :]).T
    near = mixed[...] + mul(near, right[...])
    days = near.shape[0]
    near = jnp.concatenate([near[:8], near[days - 8 :]], axis=0)
    near = deep_parts_of(near)
    for r in range(8):
        surface = mul_deep(near, smooth[r])
        for c in range(2):
            halves[c, pl.ds(r, 16, stride=8), :] = surface[:, LANES * c : LANES * c + LANES]
    ocean = 1.0 - land[...].astype(f32)
    sides = ((observed_low, missing_low), (observed_high, missing_high))
    copies = []
    for e, (observed, missing) in enumerate(sides):
        for c in range(2):
            at = slice(LANES * c, LANES * c + LANES)
            surface = halves[c, 64 * e : 64 * e + 64, :].reshape(8, 8, LANES)
            value = jnp.where(missing[:, :, at] == 1, surface, observed[:, :, at])
            edges[e, :, :, at] = value * ocean[None, :, at]
        copy = pltpu.make_async_copy(
            edges.at[e], filled.at[pl.ds((days - 8) * e, 8)], sent.at[e]
        )
        copy.start()
        copies.append(copy)
    found = factor[...]
    raw = [arrived[j] for j in range(arrived.shape[0])]
    weights_t = mul(found, jnp.concatenate(raw, axis=1))
    rest = jnp.zeros((LANES - K, weights_t.shape[1]), f32)
    gram = mul_few(
        parts_of(weights_t), jnp.concatenate([weights_t, rest], axis=0), 1
    )
    basis_t[...] = mul(inverse_factor(gram), mul(found, arrived[d]))
    for copy in copies:
        copy.wait()


def swap(blocks, axes):
    return lax.all_to_all(blocks, axes, 0, 0)


def near_rows(edge_low, edge_high):
    count = lax.axis_size(PIX)
    up = [(i, i + 1) for i in range(count - 1)]
    down = [(i + 1, i) for i in range(count - 1)]
    return lax.ppermute(edge_high, PIX, up), lax.ppermute(edge_low, PIX, down)


def band_of(day_weights):
    days = day_weights.shape[0]
    slot = lax.broadcasted_iota(jnp.int32, (4 * LANES, days), 0)
    target = lax.broadcasted_iota(jnp.int32, (4 * LANES, days), 1)
    first = LANES + K
    source = jnp.where(slot < days, slot, 4 * days)
    source = jnp.where((slot >= first) & (slot < first + 3), slot - first - 3, source)
    source = jnp.where(
        (slot >= first + 3) & (slot < first + 6), slot - first - 3 + days, source
    )
    source = jnp.where(slot >= 2 * LANES, slot - 3 * LANES, source)
    source = jnp.where(slot >= 3 * LANES, slot - 3 * LANES + days, source)
    taps = day_weights.T
    return sum(
        jnp.where(source - target + RADIUS == j, taps[j : j + 1], f32(0.0))
        for j in range(2 * RADIUS + 1)
    )


def per_device(observed, missing, land, basis_start, day_weights):
    days, rows, cols = observed.shape
    day = lax.axis_index(DAY).reshape(1)
    near, far = lax.axis_size(NEAR), lax.axis_size("y")
    halo = [pltpu.VMEM((64, LANES), f32)] * 2
    halves = [pltpu.VMEM((days * rows, LANES), f32)] * 2
    edge = (K + 8, cols)
    block = (rows, K, cols)

    def add_near(joint, edges):
        joint = call(add_all_body, (far,) + joint.shape[1:], (swap(joint, NEAR),))
        return lax.optimization_barrier((joint, *edges))

    def smooth_beside(joint, low, high, modes):
        above, below = near_rows(low, high)
        joint = swap(joint, "y")
        smooth = call(smooth_body, block, (modes, above, below, land))
        return lax.optimization_barrier((joint, smooth))

    slab = pltpu.VMEM((days, rows, cols), f32)
    turned = pltpu.VMEM((rows, days, cols), f32)
    mask = pltpu.VMEM((days, rows, cols), jnp.int32)

    part = call(
        start_body,
        (rows, K + HALO, cols),
        (day, observed, missing, land, basis_start.T),
        [
            slab,
            mask,
            pltpu.VMEM((rows, cols), jnp.int32),
            pltpu.VMEM((K, days), f32),
            *halves,
            pltpu.VMEM((rows, K + HALO, cols), f32),
            pltpu.SemaphoreType.DMA((10,)),
            pltpu.SemaphoreType.DMA((8,)),
        ],
        limit=56,
        anywhere=(1, 2, 3, 4),
        out_any=(0,),
    )
    later, taps, part = lax.optimization_barrier((missing, day_weights, part))
    band = band_of(taps)
    first, gap = call(
        turn_body,
        [(rows, days, cols), jax.ShapeDtypeStruct((rows, days, cols), bf16)],
        (observed, later, land),
        [slab, mask, *halves, *halves, turned, pltpu.VMEM((rows, days, cols), bf16)]
        + [pltpu.SemaphoreType.DMA((2,))] * 2,
        limit=56,
        anywhere=(0, 1),
        out_any=(0, 1),
    )
    arrived, first, gap, band = lax.optimization_barrier(
        (swap(part, DAY), first, gap, band)
    )
    modes = swap(call(add_rows_body, block, (arrived,)), DAY)
    joint, *edges = call(
        project_body,
        [(near, K + 16, LANES), edge, edge],
        (day, arrived, modes, first, land),
        halo,
    )
    joint, low, high = add_near(joint, edges)
    joint, smooth = smooth_beside(joint, low, high, modes)
    filled, part = call(
        refill_body,
        [(rows, days, cols), (rows, K + 8, cols)],
        (day, joint, band, smooth, first, gap, land),
        [
            pltpu.VMEM(block, f32),
            turned,
            pltpu.VMEM((rows, days, cols), bf16),
            turned,
            pltpu.VMEM((rows, K + 8, cols), f32),
            pltpu.SemaphoreType.DMA((17,)),
            pltpu.SemaphoreType.DMA((16,)),
        ],
        limit=53,
        anywhere=(3, 4, 5),
        out_any=(0, 1),
    )
    arrived = swap(part, DAY)
    modes = swap(call(add_rows_body, block, (arrived,)), DAY)
    factor = call(factor_body, (K, LANES), (arrived,))
    joint, *edges = call(
        project_again_body,
        [(near, K + 8, LANES), edge, edge],
        (modes, filled, land, factor),
    )
    joint, low, high = add_near(joint, edges)
    joint, smooth = smooth_beside(joint, low, high, modes)
    raw, extra = call(add_last_body, [(8, K, LANES), (8, LANES)], (joint,))
    arrived = swap(raw, DAY)
    mixed, right, found = call(
        last_weights_body,
        [(days, K), (K, K), (K, K)],
        (raw, extra, band, factor),
    )
    filled = call(
        last_fill_body,
        (days, rows, cols),
        (mixed, smooth, observed, missing, land),
        halves,
    )
    ends = (slice(0, 8), slice(days - 8, days))
    basis_t, filled = call(
        finish_body,
        [(K, days), (days, rows, cols)],
        (day, arrived, band, found, right, mixed, smooth)
        + tuple(observed[e] for e in ends)
        + tuple(missing[e] for e in ends)
        + (land, filled),
        [
            pltpu.VMEM((2, 8, rows, cols), f32),
            pltpu.VMEM((2, 128, LANES), f32),
            pltpu.SemaphoreType.DMA((2,)),
        ],
        anywhere=(12,),
        out_any=(1,),
        alias={12: 1},
    )
    return filled, basis_t.T


def solution(mesh):
    fine = Mesh(mesh.devices.reshape(SIZES), ("zlo", "y", "core", "x", "zhi"))
    return jax.shard_map(
        per_device,
        mesh=fine,
        in_specs=(
            P(DAY, PIX, None),
            P(DAY, PIX, None),
            P(PIX, None),
            P(DAY, None),
            P(DAY, None),
        ),
        out_specs=(P(DAY, PIX, None), P(DAY, None)),
        check_vma=False,
    )
```

```python
import jax
import jax.numpy as jnp
from jax import lax
from jax.experimental import pallas as pl
from jax.experimental.pallas import tpu as pltpu
from jax.sharding import Mesh, PartitionSpec as P

RADIUS = 3
K = 32
LANES = 128
HALO = 8 * RADIUS

PIX = ("zlo", "y", "core")
DAY = ("x", "zhi")
NEAR = ("zlo", "core")
SIZES = (4, 8, 2, 4, 2)

exact = lax.Precision.HIGHEST
smoothing = 0.2
f32 = jnp.float32
bf16 = jnp.bfloat16


def mul(a, b):
    return lax.dot_general(
        a, b, (((1,), (0,)), ((), ())), precision=exact, preferred_element_type=f32
    )


def mul_t(a, b):
    return lax.dot_general(
        a, b, (((1,), (1,)), ((), ())), precision=exact, preferred_element_type=f32
    )


def split(x):
    high = x.astype(bf16)
    rest = x - high.astype(f32)
    middle = rest.astype(bf16)
    return high, middle, (rest - middle.astype(f32)).astype(bf16)


def parts_of(a):
    return jnp.concatenate(split(a), axis=0)


def mul_few(stack, b, over=0):
    rows = stack.shape[0] // 3
    total = None
    for i, part in enumerate(split(b)):
        found = lax.dot_general(
            stack[: rows * (3 - i)],
            part,
            (((1,), (over,)), ((), ())),
            preferred_element_type=f32,
        )
        for j in range(3 - i):
            piece = found[rows * j : rows * j + rows]
            total = piece if total is None else total + piece
    return total


def deep_parts_of(a):
    high, middle, low = split(a)
    return jnp.concatenate([low, middle, high, middle, high, high], axis=1)


def mul_deep(stack, b):
    high, middle, low = split(b)
    right = jnp.concatenate([high, middle, low, high, middle, high], axis=0)
    return lax.dot_general(
        stack, right, (((1,), (0,)), ((), ())), preferred_element_type=f32
    )


def inverse_factor(wide):
    row = lax.broadcasted_iota(jnp.int32, (K, LANES), 0)
    lane = lax.broadcasted_iota(jnp.int32, (K, LANES), 1)
    work = jnp.where(lane < K, wide, jnp.where(lane == row + K, f32(1.0), f32(0.0)))
    done = []
    for start in range(0, K, 8):
        size = K - start
        at = lax.broadcasted_iota(jnp.int32, (size, LANES), 0)
        spread = [
            jnp.broadcast_to(work[:, start + j : start + j + 1], (size, LANES))
            for j in range(8)
        ]
        for j in range(8):
            inverse = 1.0 / spread[j][j : j + 1, :]
            column = jnp.where(at > j, spread[j], f32(0.0))
            for l in range(j + 1, 8):
                spread[l] = spread[l] - column * (spread[l][j : j + 1, :] * inverse)
            work = work - column * (work[j : j + 1, :] * inverse)
        done.append(work[:8])
        work = work[8:]
    work = jnp.concatenate(done, axis=0)
    pivots = jnp.sum(jnp.where(lane == row, work, f32(0.0)), axis=1, keepdims=True)
    work = work * (1.0 / jnp.sqrt(pivots))
    return pltpu.roll(work, LANES - K, 1)[:, :K]


def unpack_gram(packed):
    return jnp.concatenate(
        [packed] + [pltpu.roll(packed, LANES - K * a, 1) for a in range(1, 4)], axis=0
    )


def pack_rows(wide):
    packed = wide[:8]
    for a in range(1, 4):
        packed = packed + pltpu.roll(wide[8 * a : 8 * a + 8], K * a, 1)
    return packed


def pack_gram(weights_t):
    rest = jnp.zeros((LANES - K, LANES), f32)
    return pack_rows(mul_t(weights_t, jnp.concatenate([weights_t, rest], axis=0)))


def total_of(arrived):
    total = arrived[0]
    for j in range(1, arrived.shape[0]):
        total = total + arrived[j]
    return total


def call(body, outs, args, scratch=(), limit=8, anywhere=(), alias=None, out_any=()):
    specs = []
    for i, a in enumerate(args):
        space = pltpu.SMEM if a.ndim == 1 else pltpu.VMEM
        specs.append(pl.BlockSpec(memory_space=pl.ANY if i in anywhere else space))
    many = isinstance(outs, list)
    shapes = [
        jax.ShapeDtypeStruct(s, f32) if isinstance(s, tuple) else s
        for s in (outs if many else [outs])
    ]
    out_specs = [
        pl.BlockSpec(memory_space=pl.ANY if i in out_any else pltpu.VMEM)
        for i in range(len(shapes))
    ]
    return pl.pallas_call(
        body,
        out_shape=shapes if many else shapes[0],
        in_specs=specs,
        out_specs=out_specs if many else out_specs[0],
        scratch_shapes=list(scratch),
        input_output_aliases=alias or {},
        compiler_params=pltpu.CompilerParams(vmem_limit_bytes=limit * 1024 * 1024),
        cost_estimate=pl.CostEstimate(
            flops=1_000_000, bytes_accessed=1_000_000, transcendentals=0
        ),
    )(*args)


def rows_of(halves, start, size):
    return jnp.concatenate(
        [half[pl.ds(start, size, stride=8), :] for half in halves], axis=1
    )


def start_body(
    day,
    observed_hbm,
    missing_hbm,
    land_hbm,
    basis_hbm,
    out_hbm,
    observed,
    missing,
    land,
    basis_t,
    half_0,
    half_1,
    out,
    arrivals,
    sent,
):
    parts = 4
    days = observed.shape[0]
    size = days // parts
    small = [
        pltpu.make_async_copy(land_hbm, land, arrivals.at[2 * parts]),
        pltpu.make_async_copy(basis_hbm, basis_t, arrivals.at[2 * parts + 1]),
    ]
    for copy in small:
        copy.start()
    copies = []
    for i in range(parts):
        at = pl.ds(size * i, size)
        for c, (source, target) in enumerate(
            ((missing_hbm, missing), (observed_hbm, observed))
        ):
            copies.append(
                pltpu.make_async_copy(
                    source.at[at], target.at[at], arrivals.at[2 * i + c]
                )
            )
            copies[-1].start()
    d = day[0]
    halves = (half_0, half_1)
    out[:, K:, :] = jnp.zeros((8, HALO, out.shape[2]), f32)
    for copy in small:
        copy.wait()
    ocean = 1.0 - land[...].astype(f32)
    for i in range(parts):
        copies[2 * i].wait()
        copies[2 * i + 1].wait()
        now = slice(size * i, size * i + size)
        for c, half in enumerate(halves):
            at = slice(LANES * c, LANES * c + LANES)
            tile = jnp.where(missing[now, :, at] == 1, f32(0.0), observed[now, :, at])
            tile = tile * ocean[None, :, at]
            half[8 * size * i : 8 * size * (i + 1), :] = tile.reshape(8 * size, LANES)
    low, high = jnp.maximum(d - 1, 0), jnp.minimum(d + 1, 7)
    for t in range(RADIUS):
        for target, source in ((low, t), (high, days - RADIUS + t)):
            tile = [half[8 * source : 8 * source + 8, :] for half in halves]
            out[target, K + 8 * t : K + 8 * t + 8, :] = jnp.concatenate(tile, axis=1)
    weights = parts_of(basis_t[...])
    copies = []
    for r in range(8):
        out[r, :K, :] = mul_few(weights, rows_of(halves, r, days))
        copies.append(pltpu.make_async_copy(out.at[r], out_hbm.at[r], sent.at[r]))
        copies[-1].start()
    for copy in copies:
        copy.wait()


def turn_body(
    observed_hbm,
    missing_hbm,
    land,
    first_hbm,
    gap_hbm,
    observed,
    missing,
    half_0,
    half_1,
    mask_0,
    mask_1,
    first,
    gap,
    arrivals,
    sent,
):
    pairs = ((missing_hbm, missing), (observed_hbm, observed))
    copies = [
        pltpu.make_async_copy(source, target, arrivals.at[i])
        for i, (source, target) in enumerate(pairs)
    ]
    for copy in copies:
        copy.start()
    for copy in copies:
        copy.wait()
    days = missing.shape[0]
    ocean = 1.0 - land[...].astype(f32)
    halves, masks = (half_0, half_1), (mask_0, mask_1)
    for c in range(2):
        at = slice(LANES * c, LANES * c + LANES)
        absent = missing[:, :, at] == 1
        tile = jnp.where(absent, f32(0.0), observed[:, :, at]) * ocean[None, :, at]
        halves[c][...] = tile.reshape(8 * days, LANES)
        masks[c][...] = absent.astype(f32).reshape(8 * days, LANES)
    for r in range(8):
        first[r] = rows_of(halves, r, days)
        gap[r] = rows_of(masks, r, days).astype(bf16)
    copies = [
        pltpu.make_async_copy(first, first_hbm, sent.at[0]),
        pltpu.make_async_copy(gap, gap_hbm, sent.at[1]),
    ]
    for copy in copies:
        copy.start()
    for copy in copies:
        copy.wait()


def add_rows_body(arrived, out):
    total = arrived[0, :K, :]
    for j in range(1, arrived.shape[0]):
        total = total + arrived[j, :K, :]
    for j in range(out.shape[0]):
        out[j] = total


def add_all_body(arrived, out):
    total = total_of(arrived)
    for j in range(out.shape[0]):
        out[j] = total


def add_last_body(arrived, out, extra):
    total = total_of(arrived)
    for j in range(out.shape[0]):
        out[j] = total[:K]
    extra[...] = total[K:]


def factor_body(arrived, out):
    packed = arrived[0, K:, :LANES]
    for j in range(1, arrived.shape[0]):
        packed = packed + arrived[j, K:, :LANES]
    out[:, :K] = inverse_factor(unpack_gram(packed))
    out[:, K:] = jnp.zeros((K, LANES - K), f32)


def edges_of(modes, land, edge_low, edge_high):
    ocean = 1.0 - land[...].astype(f32)
    for edge, r in ((edge_low, 0), (edge_high, 7)):
        edge[:K, :] = modes[r]
        edge[K:, :] = jnp.broadcast_to(ocean[r : r + 1], (8, ocean.shape[1]))


class Products:
    def __init__(self, count):
        self.count = count
        self.totals = [jnp.zeros((count, K * (3 - i)), f32) for i in range(3)]

    def add(self, few, many):
        stack = parts_of(few)
        for i, part in enumerate(split(many)):
            self.totals[i] = self.totals[i] + lax.dot_general(
                part,
                stack[: K * (3 - i)],
                (((1,), (1,)), ((), ())),
                preferred_element_type=f32,
            )

    def result(self):
        found = None
        for i, total in enumerate(self.totals):
            tall = ((0, 2 * LANES - self.count), (0, LANES - total.shape[1]))
            total = jnp.pad(total, tall).T
            for j in range(3 - i):
                piece = total[K * j : K * j + K]
                found = piece if found is None else found + piece
        return found


def project_again_body(
    modes, filled_hbm, land, factor, out, edge_low, edge_high, filled, arrivals
):
    copies = [
        pltpu.make_async_copy(filled_hbm.at[r], filled.at[r], arrivals.at[r])
        for r in range(8)
    ]
    for copy in copies:
        copy.start()
    cols = modes.shape[2]
    wide = jnp.concatenate([modes[r] for r in range(8)], axis=1)
    wide = mul_deep(deep_parts_of(factor[:, :K]), wide)
    products = Products(LANES + K)
    for r in range(8):
        if r % 2 == 0:
            copies[r].wait()
            copies[r + 1].wait()
        modes_u = wide[:, cols * r : cols * r + cols]
        products.add(modes_u, jnp.concatenate([filled[r], modes_u], axis=0))
    total = products.result()
    packed = pack_rows(total[:, LANES:])
    for j in range(out.shape[0]):
        out[j, :K, :] = total[:, :LANES]
        out[j, K:, :] = packed
    edges_of(modes, land, edge_low, edge_high)


def project_body(
    day, arrived, modes, filled, land, out, edge_low, edge_high, halo_0, halo_1
):
    d = day[0]
    low = arrived[jnp.maximum(d - 1, 0), K : K + HALO, :]
    high = arrived[jnp.minimum(d + 1, 7), K : K + HALO, :]
    low = jnp.where(d > 0, low, f32(0.0))
    high = jnp.where(d < 7, high, f32(0.0))
    cols = modes.shape[2]
    for c, halo in enumerate((halo_0, halo_1)):
        halo[:HALO, :] = low[:, LANES * c : LANES * c + LANES]
        halo[HALO : 2 * HALO, :] = high[:, LANES * c : LANES * c + LANES]
        halo[2 * HALO :, :] = jnp.zeros((64 - 2 * HALO, LANES), f32)
    pad = jnp.zeros((8, cols), f32)
    products = Products(LANES + K + 16)
    for r in range(8):
        modes_u = modes[r]
        days_near = rows_of((halo_0, halo_1), r, 8)
        right = jnp.concatenate([filled[r], modes_u, days_near, pad], axis=0)
        products.add(modes_u, right)
    total = products.result()
    extra = total[:, LANES:]
    packed = extra[:16] + pltpu.roll(extra[16:], 64, 1)
    for j in range(out.shape[0]):
        out[j, :K, :] = total[:, :LANES]
        out[j, K:, :] = packed
    edges_of(modes, land, edge_low, edge_high)


def smooth_body(modes, above, below, land, out):
    cols = out.shape[2]
    lane = lax.broadcasted_iota(jnp.int32, (1, cols), 1)
    ocean = 1.0 - land[...].astype(f32)
    rows = [above[:K, :]] + [modes[r] for r in range(8)] + [below[:K, :]]
    flags = (
        [above[K : K + 1, :]]
        + [ocean[r : r + 1] for r in range(8)]
        + [below[K : K + 1, :]]
    )
    for r in range(8):
        here, flag = rows[r + 1], flags[r + 1]
        left = jnp.where(lane > 0, pltpu.roll(flag, 1, 1), f32(0.0))
        right = jnp.where(lane < cols - 1, pltpu.roll(flag, cols - 1, 1), f32(0.0))
        up, down = flags[r], flags[r + 2]
        centre = 1.0 - smoothing * (up + down + left + right)
        spread = (
            up * rows[r]
            + down * rows[r + 2]
            + left * pltpu.roll(here, 1, 1)
            + right * pltpu.roll(here, cols - 1, 1)
        )
        out[r] = centre * here + smoothing * spread


def refill_body(
    day,
    arrived,
    band,
    smooth_hbm,
    first_hbm,
    gap_hbm,
    land,
    filled_hbm,
    out_hbm,
    smooth,
    first,
    gap,
    filled,
    out,
    arrivals,
    sent,
):
    def start(source, target, semaphore):
        copy = pltpu.make_async_copy(source, target, semaphore)
        copy.start()
        return copy

    waits = [start(smooth_hbm, smooth, arrivals.at[16])]
    fetches = [
        (
            start(first_hbm.at[r], first.at[r], arrivals.at[2 * r]),
            start(gap_hbm.at[r], gap.at[r], arrivals.at[2 * r + 1]),
        )
        for r in range(8)
    ]
    total = total_of(arrived)
    extra = jnp.concatenate([total[K:], pltpu.roll(total[K:], 64, 1)], axis=0)
    raw = jnp.concatenate([total[:K], extra], axis=1)
    tempered_t = mul(raw, band[: 2 * LANES, :]).T
    factor = inverse_factor(extra)
    weights_t = mul(factor, total[:K])
    mixed = deep_parts_of(mul(tempered_t, mul(factor.T, factor)))
    weights = parts_of(weights_t)
    cols = filled.shape[2]
    packed = pack_gram(weights_t)
    for j in range(8):
        out[j, K:, :LANES] = packed
        out[j, K:, LANES:] = jnp.zeros((8, cols - LANES), f32)
    ocean = 1.0 - land[...].astype(f32)
    for copy in waits:
        copy.wait()
    sends = []
    for r in range(0, 8, 2):
        for copy in fetches[r] + fetches[r + 1]:
            copy.wait()
        for q in (r, r + 1):
            surface = mul_deep(mixed, smooth[q])
            absent = gap[q].astype(f32) == 1
            now = jnp.where(absent, surface * ocean[q : q + 1], first[q])
            filled[q] = now
            out[q, :K, :] = mul_few(weights, now)
        for q in (r, r + 1):
            sends.append(start(filled.at[q], filled_hbm.at[q], sent.at[2 * q]))
            sends.append(start(out.at[q], out_hbm.at[q], sent.at[2 * q + 1]))
    for copy in sends:
        copy.wait()


def last_weights_body(raw, extra, band, scale, mixed, right, factor):
    tempered_t = mul(raw[0], band[:LANES, :]).T
    found = inverse_factor(unpack_gram(extra[...]))
    inner = mul(found.T, mul(found, scale[:, :K]))
    mixed[...] = mul(tempered_t, inner)
    right[...] = inner
    factor[...] = found


def last_fill_body(mixed, smooth, observed, missing, land, out, *halves):
    days = observed.shape[0]
    ocean = 1.0 - land[...].astype(f32)
    mix = deep_parts_of(mixed[...])
    for r in range(8):
        surface = mul_deep(mix, smooth[r])
        for c, half in enumerate(halves):
            half[pl.ds(r, days, stride=8), :] = surface[:, LANES * c : LANES * c + LANES]
    for c, half in enumerate(halves):
        at = slice(LANES * c, LANES * c + LANES)
        surface = half[...].reshape(days, 8, LANES)
        value = jnp.where(missing[:, :, at] == 1, surface, observed[:, :, at])
        out[:, :, at] = value * ocean[None, :, at]


def finish_body(
    day,
    arrived,
    band,
    factor,
    right,
    mixed,
    smooth,
    observed_low,
    observed_high,
    missing_low,
    missing_high,
    land,
    filled_in,
    basis_t,
    filled,
    edges,
    halves,
    sent,
):
    del filled_in
    d = day[0]
    low = arrived[jnp.maximum(d - 1, 0)]
    high = arrived[jnp.minimum(d + 1, 7)]
    low = jnp.where(d > 0, low, f32(0.0))
    high = jnp.where(d < 7, high, f32(0.0))
    near = mul(jnp.concatenate([low, high], axis=1), band[2 * LANES :, :]).T
    near = mixed[...] + mul(near, right[...])
    days = near.shape[0]
    near = jnp.concatenate([near[:8], near[days - 8 :]], axis=0)
    near = deep_parts_of(near)
    for r in range(8):
        surface = mul_deep(near, smooth[r])
        for c in range(2):
            halves[c, pl.ds(r, 16, stride=8), :] = surface[:, LANES * c : LANES * c + LANES]
    ocean = 1.0 - land[...].astype(f32)
    sides = ((observed_low, missing_low), (observed_high, missing_high))
    copies = []
    for e, (observed, missing) in enumerate(sides):
        for c in range(2):
            at = slice(LANES * c, LANES * c + LANES)
            surface = halves[c, 64 * e : 64 * e + 64, :].reshape(8, 8, LANES)
            value = jnp.where(missing[:, :, at] == 1, surface, observed[:, :, at])
            edges[e, :, :, at] = value * ocean[None, :, at]
        copy = pltpu.make_async_copy(
            edges.at[e], filled.at[pl.ds((days - 8) * e, 8)], sent.at[e]
        )
        copy.start()
        copies.append(copy)
    found = factor[...]
    raw = [arrived[j] for j in range(arrived.shape[0])]
    weights_t = mul(found, jnp.concatenate(raw, axis=1))
    rest = jnp.zeros((LANES - K, weights_t.shape[1]), f32)
    gram = mul_few(
        parts_of(weights_t), jnp.concatenate([weights_t, rest], axis=0), 1
    )
    basis_t[...] = mul(inverse_factor(gram), mul(found, arrived[d]))
    for copy in copies:
        copy.wait()


def swap(blocks, axes):
    return lax.all_to_all(blocks, axes, 0, 0)


def near_rows(edge_low, edge_high):
    count = lax.axis_size(PIX)
    up = [(i, i + 1) for i in range(count - 1)]
    down = [(i + 1, i) for i in range(count - 1)]
    return lax.ppermute(edge_high, PIX, up), lax.ppermute(edge_low, PIX, down)


def band_of(day_weights):
    days = day_weights.shape[0]
    slot = lax.broadcasted_iota(jnp.int32, (4 * LANES, days), 0)
    target = lax.broadcasted_iota(jnp.int32, (4 * LANES, days), 1)
    first = LANES + K
    source = jnp.where(slot < days, slot, 4 * days)
    source = jnp.where((slot >= first) & (slot < first + 3), slot - first - 3, source)
    source = jnp.where(
        (slot >= first + 3) & (slot < first + 6), slot - first - 3 + days, source
    )
    source = jnp.where(slot >= 2 * LANES, slot - 3 * LANES, source)
    source = jnp.where(slot >= 3 * LANES, slot - 3 * LANES + days, source)
    taps = day_weights.T
    return sum(
        jnp.where(source - target + RADIUS == j, taps[j : j + 1], f32(0.0))
        for j in range(2 * RADIUS + 1)
    )


def per_device(observed, missing, land, basis_start, day_weights):
    days, rows, cols = observed.shape
    day = lax.axis_index(DAY).reshape(1)
    near, far = lax.axis_size(NEAR), lax.axis_size("y")
    halo = [pltpu.VMEM((64, LANES), f32)] * 2
    halves = [pltpu.VMEM((days * rows, LANES), f32)] * 2
    edge = (K + 8, cols)
    block = (rows, K, cols)

    def add_first(joint, edges):
        joint = call(add_all_body, (near,) + joint.shape[1:], (swap(joint, "y"),))
        return lax.optimization_barrier((joint, *edges))

    def smooth_beside(joint, low, high, modes):
        above, below = near_rows(low, high)
        joint = swap(joint, NEAR)
        smooth = call(smooth_body, block, (modes, above, below, land))
        return lax.optimization_barrier((joint, smooth))

    slab = pltpu.VMEM((days, rows, cols), f32)
    turned = pltpu.VMEM((rows, days, cols), f32)
    mask = pltpu.VMEM((days, rows, cols), jnp.int32)

    part = call(
        start_body,
        (rows, K + HALO, cols),
        (day, observed, missing, land, basis_start.T),
        [
            slab,
            mask,
            pltpu.VMEM((rows, cols), jnp.int32),
            pltpu.VMEM((K, days), f32),
            *halves,
            pltpu.VMEM((rows, K + HALO, cols), f32),
            pltpu.SemaphoreType.DMA((10,)),
            pltpu.SemaphoreType.DMA((8,)),
        ],
        limit=56,
        anywhere=(1, 2, 3, 4),
        out_any=(0,),
    )
    later, taps, part = lax.optimization_barrier((missing, day_weights, part))
    band = band_of(taps)
    first, gap = call(
        turn_body,
        [(rows, days, cols), jax.ShapeDtypeStruct((rows, days, cols), bf16)],
        (observed, later, land),
        [slab, mask, *halves, *halves, turned, pltpu.VMEM((rows, days, cols), bf16)]
        + [pltpu.SemaphoreType.DMA((2,))] * 2,
        limit=56,
        anywhere=(0, 1),
        out_any=(0, 1),
    )
    arrived, first, gap, band = lax.optimization_barrier(
        (swap(part, DAY), first, gap, band)
    )
    modes = swap(call(add_rows_body, block, (arrived,)), DAY)
    joint, *edges = call(
        project_body,
        [(far, K + 16, LANES), edge, edge],
        (day, arrived, modes, first, land),
        halo,
    )
    joint, low, high = add_first(joint, edges)
    joint, smooth = smooth_beside(joint, low, high, modes)
    filled, part = call(
        refill_body,
        [(rows, days, cols), (rows, K + 8, cols)],
        (day, joint, band, smooth, first, gap, land),
        [
            pltpu.VMEM(block, f32),
            turned,
            pltpu.VMEM((rows, days, cols), bf16),
            turned,
            pltpu.VMEM((rows, K + 8, cols), f32),
            pltpu.SemaphoreType.DMA((17,)),
            pltpu.SemaphoreType.DMA((16,)),
        ],
        limit=53,
        anywhere=(3, 4, 5),
        out_any=(0, 1),
    )
    arrived = swap(part, DAY)
    modes = swap(call(add_rows_body, block, (arrived,)), DAY)
    factor = call(factor_body, (K, LANES), (arrived,))
    joint, *edges = call(
        project_again_body,
        [(far, K + 8, LANES), edge, edge],
        (modes, filled, land, factor),
        [turned, pltpu.SemaphoreType.DMA((8,))],
        limit=53,
        anywhere=(1,),
    )
    joint, low, high = add_first(joint, edges)
    joint, smooth = smooth_beside(joint, low, high, modes)
    raw, extra = call(add_last_body, [(8, K, LANES), (8, LANES)], (joint,))
    arrived = swap(raw, DAY)
    mixed, right, found = call(
        last_weights_body,
        [(days, K), (K, K), (K, K)],
        (raw, extra, band, factor),
    )
    filled = call(
        last_fill_body,
        (days, rows, cols),
        (mixed, smooth, observed, missing, land),
        halves,
    )
    ends = (slice(0, 8), slice(days - 8, days))
    basis_t, filled = call(
        finish_body,
        [(K, days), (days, rows, cols)],
        (day, arrived, band, found, right, mixed, smooth)
        + tuple(observed[e] for e in ends)
        + tuple(missing[e] for e in ends)
        + (land, filled),
        [
            pltpu.VMEM((2, 8, rows, cols), f32),
            pltpu.VMEM((2, 128, LANES), f32),
            pltpu.SemaphoreType.DMA((2,)),
        ],
        anywhere=(12,),
        out_any=(1,),
        alias={12: 1},
    )
    return filled, basis_t.T


def solution(mesh):
    fine = Mesh(mesh.devices.reshape(SIZES), ("zlo", "y", "core", "x", "zhi"))
    return jax.shard_map(
        per_device,
        mesh=fine,
        in_specs=(
            P(DAY, PIX, None),
            P(DAY, PIX, None),
            P(PIX, None),
            P(DAY, None),
            P(DAY, None),
        ),
        out_specs=(P(DAY, PIX, None), P(DAY, None)),
        check_vma=False,
    )
```

```python
import jax
import jax.numpy as jnp
from jax import lax
from jax.experimental import pallas as pl
from jax.experimental.pallas import tpu as pltpu
from jax.sharding import Mesh, PartitionSpec as P

RADIUS = 3
K = 32
LANES = 128
HALO = 8 * RADIUS

PIX = ("zlo", "y", "core")
DAY = ("x", "zhi")
NEAR = ("zlo", "core")
SIZES = (4, 8, 2, 4, 2)

exact = lax.Precision.HIGHEST
smoothing = 0.2
f32 = jnp.float32
bf16 = jnp.bfloat16


def mul(a, b):
    return lax.dot_general(
        a, b, (((1,), (0,)), ((), ())), precision=exact, preferred_element_type=f32
    )


def mul_t(a, b):
    return lax.dot_general(
        a, b, (((1,), (1,)), ((), ())), precision=exact, preferred_element_type=f32
    )


def split(x):
    high = x.astype(bf16)
    rest = x - high.astype(f32)
    middle = rest.astype(bf16)
    return high, middle, (rest - middle.astype(f32)).astype(bf16)


def parts_of(a):
    return jnp.concatenate(split(a), axis=0)


def mul_few(stack, b, over=0):
    rows = stack.shape[0] // 3
    total = None
    for i, part in enumerate(split(b)):
        found = lax.dot_general(
            stack[: rows * (3 - i)],
            part,
            (((1,), (over,)), ((), ())),
            preferred_element_type=f32,
        )
        for j in range(3 - i):
            piece = found[rows * j : rows * j + rows]
            total = piece if total is None else total + piece
    return total


def deep_parts_of(a):
    high, middle, low = split(a)
    return jnp.concatenate([low, middle, high, middle, high, high], axis=1)


def mul_deep(stack, b):
    high, middle, low = split(b)
    right = jnp.concatenate([high, middle, low, high, middle, high], axis=0)
    return lax.dot_general(
        stack, right, (((1,), (0,)), ((), ())), preferred_element_type=f32
    )


def inverse_factor(wide):
    row = lax.broadcasted_iota(jnp.int32, (K, LANES), 0)
    lane = lax.broadcasted_iota(jnp.int32, (K, LANES), 1)
    work = jnp.where(lane < K, wide, jnp.where(lane == row + K, f32(1.0), f32(0.0)))
    done = []
    for start in range(0, K, 8):
        size = K - start
        at = lax.broadcasted_iota(jnp.int32, (size, LANES), 0)
        spread = [
            jnp.broadcast_to(work[:, start + j : start + j + 1], (size, LANES))
            for j in range(8)
        ]
        for j in range(8):
            inverse = 1.0 / spread[j][j : j + 1, :]
            column = jnp.where(at > j, spread[j], f32(0.0))
            for l in range(j + 1, 8):
                spread[l] = spread[l] - column * (spread[l][j : j + 1, :] * inverse)
            work = work - column * (work[j : j + 1, :] * inverse)
        done.append(work[:8])
        work = work[8:]
    work = jnp.concatenate(done, axis=0)
    pivots = jnp.sum(jnp.where(lane == row, work, f32(0.0)), axis=1, keepdims=True)
    work = work * (1.0 / jnp.sqrt(pivots))
    return pltpu.roll(work, LANES - K, 1)[:, :K]


def unpack_gram(packed):
    return jnp.concatenate(
        [packed] + [pltpu.roll(packed, LANES - K * a, 1) for a in range(1, 4)], axis=0
    )


def pack_rows(wide):
    packed = wide[:8]
    for a in range(1, 4):
        packed = packed + pltpu.roll(wide[8 * a : 8 * a + 8], K * a, 1)
    return packed


def pack_gram(weights_t):
    rest = jnp.zeros((LANES - K, LANES), f32)
    return pack_rows(mul_t(weights_t, jnp.concatenate([weights_t, rest], axis=0)))


def total_of(arrived):
    total = arrived[0]
    for j in range(1, arrived.shape[0]):
        total = total + arrived[j]
    return total


def call(body, outs, args, scratch=(), limit=8, anywhere=(), still=(), alias=None, out_any={}):
    specs = []
    for i, a in enumerate(args):
        space = pltpu.SMEM if a.ndim == 1 else pltpu.VMEM
        space = pl.ANY if i in anywhere else pltpu.HBM if i in still else space
        specs.append(pl.BlockSpec(memory_space=space))
    many = isinstance(outs, list)
    shapes = [
        jax.ShapeDtypeStruct(s, f32) if isinstance(s, tuple) else s
        for s in (outs if many else [outs])
    ]
    out_specs = [
        pl.BlockSpec(memory_space=out_any.get(i, pltpu.VMEM))
        for i in range(len(shapes))
    ]
    return pl.pallas_call(
        body,
        out_shape=shapes if many else shapes[0],
        in_specs=specs,
        out_specs=out_specs if many else out_specs[0],
        scratch_shapes=list(scratch),
        input_output_aliases=alias or {},
        compiler_params=pltpu.CompilerParams(vmem_limit_bytes=limit * 1024 * 1024),
        cost_estimate=pl.CostEstimate(
            flops=1_000_000, bytes_accessed=1_000_000, transcendentals=0
        ),
    )(*args)


def rows_of(halves, start, size):
    return jnp.concatenate(
        [half[pl.ds(start, size, stride=8), :] for half in halves], axis=1
    )


def start_body(
    day,
    observed_hbm,
    missing_hbm,
    land_hbm,
    basis_hbm,
    out_hbm,
    observed,
    missing,
    land,
    basis_t,
    half_0,
    half_1,
    out,
    arrivals,
    sent,
):
    parts = 4
    days = observed.shape[0]
    size = days // parts
    small = [
        pltpu.make_async_copy(land_hbm, land, arrivals.at[2 * parts]),
        pltpu.make_async_copy(basis_hbm, basis_t, arrivals.at[2 * parts + 1]),
    ]
    for copy in small:
        copy.start()
    copies = []
    for i in range(parts):
        at = pl.ds(size * i, size)
        for c, (source, target) in enumerate(
            ((missing_hbm, missing), (observed_hbm, observed))
        ):
            copies.append(
                pltpu.make_async_copy(
                    source.at[at], target.at[at], arrivals.at[2 * i + c]
                )
            )
            copies[-1].start()
    d = day[0]
    halves = (half_0, half_1)
    out[:, K:, :] = jnp.zeros((8, HALO, out.shape[2]), f32)
    for copy in small:
        copy.wait()
    ocean = 1.0 - land[...].astype(f32)
    for i in range(parts):
        copies[2 * i].wait()
        copies[2 * i + 1].wait()
        now = slice(size * i, size * i + size)
        for c, half in enumerate(halves):
            at = slice(LANES * c, LANES * c + LANES)
            tile = jnp.where(missing[now, :, at] == 1, f32(0.0), observed[now, :, at])
            tile = tile * ocean[None, :, at]
            half[8 * size * i : 8 * size * (i + 1), :] = tile.reshape(8 * size, LANES)
    low, high = jnp.maximum(d - 1, 0), jnp.minimum(d + 1, 7)
    for t in range(RADIUS):
        for target, source in ((low, t), (high, days - RADIUS + t)):
            tile = [half[8 * source : 8 * source + 8, :] for half in halves]
            out[target, K + 8 * t : K + 8 * t + 8, :] = jnp.concatenate(tile, axis=1)
    weights = parts_of(basis_t[...])
    copies = []
    for r in range(8):
        out[r, :K, :] = mul_few(weights, rows_of(halves, r, days))
        copies.append(pltpu.make_async_copy(out.at[r], out_hbm.at[r], sent.at[r]))
        copies[-1].start()
    for copy in copies:
        copy.wait()


def turn_body(
    observed_hbm,
    missing_hbm,
    land,
    first_hbm,
    gap_hbm,
    observed,
    missing,
    half_0,
    half_1,
    mask_0,
    mask_1,
    first,
    gap,
    arrivals,
    sent,
):
    pairs = ((missing_hbm, missing), (observed_hbm, observed))
    copies = [
        pltpu.make_async_copy(source, target, arrivals.at[i])
        for i, (source, target) in enumerate(pairs)
    ]
    for copy in copies:
        copy.start()
    for copy in copies:
        copy.wait()
    days = missing.shape[0]
    ocean = 1.0 - land[...].astype(f32)
    halves, masks = (half_0, half_1), (mask_0, mask_1)
    for c in range(2):
        at = slice(LANES * c, LANES * c + LANES)
        absent = missing[:, :, at] == 1
        tile = jnp.where(absent, f32(0.0), observed[:, :, at]) * ocean[None, :, at]
        halves[c][...] = tile.reshape(8 * days, LANES)
        masks[c][...] = absent.astype(f32).reshape(8 * days, LANES)
    for r in range(8):
        first[r] = rows_of(halves, r, days)
        gap[r] = rows_of(masks, r, days).astype(bf16)
    copies = [
        pltpu.make_async_copy(first, first_hbm, sent.at[0]),
        pltpu.make_async_copy(gap, gap_hbm, sent.at[1]),
    ]
    for copy in copies:
        copy.start()
    for copy in copies:
        copy.wait()


def add_rows_body(arrived, out):
    total = arrived[0, :K, :]
    for j in range(1, arrived.shape[0]):
        total = total + arrived[j, :K, :]
    for j in range(out.shape[0]):
        out[j] = total


def add_rows_again_body(arrived, filled, out):
    del filled
    add_rows_body(arrived, out)


def add_all_body(arrived, out):
    total = total_of(arrived)
    for j in range(out.shape[0]):
        out[j] = total


def add_last_body(arrived, out, extra):
    total = total_of(arrived)
    for j in range(out.shape[0]):
        out[j] = total[:K]
    extra[...] = total[K:]


def factor_body(arrived, out):
    packed = arrived[0, K:, :LANES]
    for j in range(1, arrived.shape[0]):
        packed = packed + arrived[j, K:, :LANES]
    out[:, :K] = inverse_factor(unpack_gram(packed))
    out[:, K:] = jnp.zeros((K, LANES - K), f32)


def edges_of(modes, land, edge_low, edge_high):
    ocean = 1.0 - land[...].astype(f32)
    for edge, r in ((edge_low, 0), (edge_high, 7)):
        edge[:K, :] = modes[r]
        edge[K:, :] = jnp.broadcast_to(ocean[r : r + 1], (8, ocean.shape[1]))


class Products:
    def __init__(self, count):
        self.count = count
        self.totals = [jnp.zeros((count, K * (3 - i)), f32) for i in range(3)]

    def add(self, few, many):
        stack = parts_of(few)
        for i, part in enumerate(split(many)):
            self.totals[i] = self.totals[i] + lax.dot_general(
                part,
                stack[: K * (3 - i)],
                (((1,), (1,)), ((), ())),
                preferred_element_type=f32,
            )

    def result(self):
        found = None
        for i, total in enumerate(self.totals):
            tall = ((0, 2 * LANES - self.count), (0, LANES - total.shape[1]))
            total = jnp.pad(total, tall).T
            for j in range(3 - i):
                piece = total[K * j : K * j + K]
                found = piece if found is None else found + piece
        return found


def project_again_body(modes, filled, land, factor, out, edge_low, edge_high):
    cols = modes.shape[2]
    wide = jnp.concatenate([modes[r] for r in range(8)], axis=1)
    wide = mul_deep(deep_parts_of(factor[:, :K]), wide)
    products = Products(LANES + K)
    for r in range(8):
        modes_u = wide[:, cols * r : cols * r + cols]
        products.add(modes_u, jnp.concatenate([filled[r], modes_u], axis=0))
    total = products.result()
    packed = pack_rows(total[:, LANES:])
    for j in range(out.shape[0]):
        out[j, :K, :] = total[:, :LANES]
        out[j, K:, :] = packed
    edges_of(modes, land, edge_low, edge_high)


def project_body(
    day, arrived, modes, filled, land, out, edge_low, edge_high, halo_0, halo_1
):
    d = day[0]
    low = arrived[jnp.maximum(d - 1, 0), K : K + HALO, :]
    high = arrived[jnp.minimum(d + 1, 7), K : K + HALO, :]
    low = jnp.where(d > 0, low, f32(0.0))
    high = jnp.where(d < 7, high, f32(0.0))
    cols = modes.shape[2]
    for c, halo in enumerate((halo_0, halo_1)):
        halo[:HALO, :] = low[:, LANES * c : LANES * c + LANES]
        halo[HALO : 2 * HALO, :] = high[:, LANES * c : LANES * c + LANES]
        halo[2 * HALO :, :] = jnp.zeros((64 - 2 * HALO, LANES), f32)
    pad = jnp.zeros((8, cols), f32)
    products = Products(LANES + K + 16)
    for r in range(8):
        modes_u = modes[r]
        days_near = rows_of((halo_0, halo_1), r, 8)
        right = jnp.concatenate([filled[r], modes_u, days_near, pad], axis=0)
        products.add(modes_u, right)
    total = products.result()
    extra = total[:, LANES:]
    packed = extra[:16] + pltpu.roll(extra[16:], 64, 1)
    for j in range(out.shape[0]):
        out[j, :K, :] = total[:, :LANES]
        out[j, K:, :] = packed
    edges_of(modes, land, edge_low, edge_high)


def smooth_body(modes, above, below, land, out):
    cols = out.shape[2]
    lane = lax.broadcasted_iota(jnp.int32, (1, cols), 1)
    ocean = 1.0 - land[...].astype(f32)
    rows = [above[:K, :]] + [modes[r] for r in range(8)] + [below[:K, :]]
    flags = (
        [above[K : K + 1, :]]
        + [ocean[r : r + 1] for r in range(8)]
        + [below[K : K + 1, :]]
    )
    for r in range(8):
        here, flag = rows[r + 1], flags[r + 1]
        left = jnp.where(lane > 0, pltpu.roll(flag, 1, 1), f32(0.0))
        right = jnp.where(lane < cols - 1, pltpu.roll(flag, cols - 1, 1), f32(0.0))
        up, down = flags[r], flags[r + 2]
        centre = 1.0 - smoothing * (up + down + left + right)
        spread = (
            up * rows[r]
            + down * rows[r + 2]
            + left * pltpu.roll(here, 1, 1)
            + right * pltpu.roll(here, cols - 1, 1)
        )
        out[r] = centre * here + smoothing * spread


def refill_body(
    day,
    arrived,
    band,
    smooth_hbm,
    first,
    gap,
    land,
    filled_hbm,
    out,
    smooth,
    filled,
    arrivals,
    sent,
):
    def start(source, target, semaphore):
        copy = pltpu.make_async_copy(source, target, semaphore)
        copy.start()
        return copy

    waits = [start(smooth_hbm, smooth, arrivals.at[0])]
    total = total_of(arrived)
    extra = jnp.concatenate([total[K:], pltpu.roll(total[K:], 64, 1)], axis=0)
    raw = jnp.concatenate([total[:K], extra], axis=1)
    tempered_t = mul(raw, band[: 2 * LANES, :]).T
    factor = inverse_factor(extra)
    weights_t = mul(factor, total[:K])
    mixed = deep_parts_of(mul(tempered_t, mul(factor.T, factor)))
    weights = parts_of(weights_t)
    cols = filled.shape[2]
    packed = pack_gram(weights_t)
    for j in range(8):
        out[j, K:, :LANES] = packed
        out[j, K:, LANES:] = jnp.zeros((8, cols - LANES), f32)
    ocean = 1.0 - land[...].astype(f32)
    for copy in waits:
        copy.wait()
    sends = []
    for r in range(0, 8, 2):
        for q in (r, r + 1):
            surface = mul_deep(mixed, smooth[q])
            absent = gap[q].astype(f32) == 1
            now = jnp.where(absent, surface * ocean[q : q + 1], first[q])
            filled[q] = now
            out[q, :K, :] = mul_few(weights, now)
        for q in (r, r + 1):
            sends.append(start(filled.at[q], filled_hbm.at[q], sent.at[q]))
    for copy in sends:
        copy.wait()


def last_weights_body(raw, extra, band, scale, mixed, right, factor):
    tempered_t = mul(raw[0], band[:LANES, :]).T
    found = inverse_factor(unpack_gram(extra[...]))
    inner = mul(found.T, mul(found, scale[:, :K]))
    mixed[...] = mul(tempered_t, inner)
    right[...] = inner
    factor[...] = found


def last_fill_body(mixed, smooth, observed, missing, land, out, *halves):
    days = observed.shape[0]
    ocean = 1.0 - land[...].astype(f32)
    mix = deep_parts_of(mixed[...])
    for r in range(8):
        surface = mul_deep(mix, smooth[r])
        for c, half in enumerate(halves):
            half[pl.ds(r, days, stride=8), :] = surface[:, LANES * c : LANES * c + LANES]
    for c, half in enumerate(halves):
        at = slice(LANES * c, LANES * c + LANES)
        surface = half[...].reshape(days, 8, LANES)
        value = jnp.where(missing[:, :, at] == 1, surface, observed[:, :, at])
        out[:, :, at] = value * ocean[None, :, at]


def finish_body(
    day,
    arrived,
    band,
    factor,
    right,
    mixed,
    smooth,
    observed_low,
    observed_high,
    missing_low,
    missing_high,
    land,
    filled_in,
    basis_t,
    filled,
    edges,
    halves,
    sent,
):
    del filled_in
    d = day[0]
    low = arrived[jnp.maximum(d - 1, 0)]
    high = arrived[jnp.minimum(d + 1, 7)]
    low = jnp.where(d > 0, low, f32(0.0))
    high = jnp.where(d < 7, high, f32(0.0))
    near = mul(jnp.concatenate([low, high], axis=1), band[2 * LANES :, :]).T
    near = mixed[...] + mul(near, right[...])
    days = near.shape[0]
    near = jnp.concatenate([near[:8], near[days - 8 :]], axis=0)
    near = deep_parts_of(near)
    for r in range(8):
        surface = mul_deep(near, smooth[r])
        for c in range(2):
            halves[c, pl.ds(r, 16, stride=8), :] = surface[:, LANES * c : LANES * c + LANES]
    ocean = 1.0 - land[...].astype(f32)
    sides = ((observed_low, missing_low), (observed_high, missing_high))
    copies = []
    for e, (observed, missing) in enumerate(sides):
        for c in range(2):
            at = slice(LANES * c, LANES * c + LANES)
            surface = halves[c, 64 * e : 64 * e + 64, :].reshape(8, 8, LANES)
            value = jnp.where(missing[:, :, at] == 1, surface, observed[:, :, at])
            edges[e, :, :, at] = value * ocean[None, :, at]
        copy = pltpu.make_async_copy(
            edges.at[e], filled.at[pl.ds((days - 8) * e, 8)], sent.at[e]
        )
        copy.start()
        copies.append(copy)
    found = factor[...]
    raw = [arrived[j] for j in range(arrived.shape[0])]
    weights_t = mul(found, jnp.concatenate(raw, axis=1))
    rest = jnp.zeros((LANES - K, weights_t.shape[1]), f32)
    gram = mul_few(
        parts_of(weights_t), jnp.concatenate([weights_t, rest], axis=0), 1
    )
    basis_t[...] = mul(inverse_factor(gram), mul(found, arrived[d]))
    for copy in copies:
        copy.wait()


def swap(blocks, axes):
    return lax.all_to_all(blocks, axes, 0, 0)


def near_rows(edge_low, edge_high):
    count = lax.axis_size(PIX)
    up = [(i, i + 1) for i in range(count - 1)]
    down = [(i + 1, i) for i in range(count - 1)]
    return lax.ppermute(edge_high, PIX, up), lax.ppermute(edge_low, PIX, down)


def band_of(day_weights):
    days = day_weights.shape[0]
    slot = lax.broadcasted_iota(jnp.int32, (4 * LANES, days), 0)
    target = lax.broadcasted_iota(jnp.int32, (4 * LANES, days), 1)
    first = LANES + K
    source = jnp.where(slot < days, slot, 4 * days)
    source = jnp.where((slot >= first) & (slot < first + 3), slot - first - 3, source)
    source = jnp.where(
        (slot >= first + 3) & (slot < first + 6), slot - first - 3 + days, source
    )
    source = jnp.where(slot >= 2 * LANES, slot - 3 * LANES, source)
    source = jnp.where(slot >= 3 * LANES, slot - 3 * LANES + days, source)
    taps = day_weights.T
    return sum(
        jnp.where(source - target + RADIUS == j, taps[j : j + 1], f32(0.0))
        for j in range(2 * RADIUS + 1)
    )


def per_device(observed, missing, land, basis_start, day_weights):
    days, rows, cols = observed.shape
    day = lax.axis_index(DAY).reshape(1)
    near, far = lax.axis_size(NEAR), lax.axis_size("y")
    halo = [pltpu.VMEM((64, LANES), f32)] * 2
    halves = [pltpu.VMEM((days * rows, LANES), f32)] * 2
    edge = (K + 8, cols)
    block = (rows, K, cols)

    def add_near(joint, edges):
        joint = call(add_all_body, (far,) + joint.shape[1:], (swap(joint, NEAR),))
        return lax.optimization_barrier((joint, *edges))

    def smooth_beside(joint, low, high, modes):
        above, below = near_rows(low, high)
        joint = swap(joint, "y")
        smooth = call(smooth_body, block, (modes, above, below, land))
        return lax.optimization_barrier((joint, smooth))

    slab = pltpu.VMEM((days, rows, cols), f32)
    turned = pltpu.VMEM((rows, days, cols), f32)
    mask = pltpu.VMEM((days, rows, cols), jnp.int32)

    part = call(
        start_body,
        (rows, K + HALO, cols),
        (day, observed, missing, land, basis_start.T),
        [
            slab,
            mask,
            pltpu.VMEM((rows, cols), jnp.int32),
            pltpu.VMEM((K, days), f32),
            *halves,
            pltpu.VMEM((rows, K + HALO, cols), f32),
            pltpu.SemaphoreType.DMA((10,)),
            pltpu.SemaphoreType.DMA((8,)),
        ],
        limit=56,
        anywhere=(1, 2, 3, 4),
        out_any={0: pl.ANY},
    )
    later, taps, part = lax.optimization_barrier((missing, day_weights, part))
    band = band_of(taps)
    first, gap = call(
        turn_body,
        [(rows, days, cols), jax.ShapeDtypeStruct((rows, days, cols), bf16)],
        (observed, later, land),
        [slab, mask, *halves, *halves, turned, pltpu.VMEM((rows, days, cols), bf16)]
        + [pltpu.SemaphoreType.DMA((2,))] * 2,
        limit=56,
        anywhere=(0, 1),
        out_any={0: pl.ANY, 1: pl.ANY},
    )
    arrived, first, gap, band = lax.optimization_barrier(
        (swap(part, DAY), first, gap, band)
    )
    modes = swap(call(add_rows_body, block, (arrived,)), DAY)
    joint, *edges = call(
        project_body,
        [(near, K + 16, LANES), edge, edge],
        (day, arrived, modes, first, land),
        halo,
    )
    joint, low, high = add_near(joint, edges)
    joint, smooth = smooth_beside(joint, low, high, modes)
    filled, part = call(
        refill_body,
        [pltpu.HBM((rows, days, cols), f32), (rows, K + 8, cols)],
        (day, joint, band, smooth, first, gap, land),
        [
            pltpu.VMEM(block, f32),
            turned,
            pltpu.SemaphoreType.DMA((1,)),
            pltpu.SemaphoreType.DMA((8,)),
        ],
        limit=12,
        anywhere=(3,),
        out_any={0: pltpu.HBM},
    )
    arrived = swap(part, DAY)
    modes = call(add_rows_again_body, block, (arrived, filled), still=(1,), limit=53)
    modes = swap(modes, DAY)
    factor = call(factor_body, (K, LANES), (arrived,))
    joint, *edges = call(
        project_again_body,
        [(near, K + 8, LANES), edge, edge],
        (modes, filled, land, factor),
    )
    joint, low, high = add_near(joint, edges)
    joint, smooth = smooth_beside(joint, low, high, modes)
    raw, extra = call(add_last_body, [(8, K, LANES), (8, LANES)], (joint,))
    arrived = swap(raw, DAY)
    mixed, right, found = call(
        last_weights_body,
        [(days, K), (K, K), (K, K)],
        (raw, extra, band, factor),
    )
    filled = call(
        last_fill_body,
        (days, rows, cols),
        (mixed, smooth, observed, missing, land),
        halves,
    )
    ends = (slice(0, 8), slice(days - 8, days))
    basis_t, filled = call(
        finish_body,
        [(K, days), (days, rows, cols)],
        (day, arrived, band, found, right, mixed, smooth)
        + tuple(observed[e] for e in ends)
        + tuple(missing[e] for e in ends)
        + (land, filled),
        [
            pltpu.VMEM((2, 8, rows, cols), f32),
            pltpu.VMEM((2, 128, LANES), f32),
            pltpu.SemaphoreType.DMA((2,)),
        ],
        anywhere=(12,),
        out_any={1: pl.ANY},
        alias={12: 1},
    )
    return filled, basis_t.T


def solution(mesh):
    fine = Mesh(mesh.devices.reshape(SIZES), ("zlo", "y", "core", "x", "zhi"))
    return jax.shard_map(
        per_device,
        mesh=fine,
        in_specs=(
            P(DAY, PIX, None),
            P(DAY, PIX, None),
            P(PIX, None),
            P(DAY, None),
            P(DAY, None),
        ),
        out_specs=(P(DAY, PIX, None), P(DAY, None)),
        check_vma=False,
    )
```

```python
import jax
import jax.numpy as jnp
from jax import lax
from jax.experimental import pallas as pl
from jax.experimental.pallas import tpu as pltpu
from jax.sharding import Mesh, PartitionSpec as P

RADIUS = 3
K = 32
LANES = 128
HALO = 8 * RADIUS

PIX = ("zlo", "y", "core")
DAY = ("x", "zhi")
NEAR = ("zlo", "core")
SIZES = (4, 8, 2, 4, 2)

exact = lax.Precision.HIGHEST
smoothing = 0.2
f32 = jnp.float32
bf16 = jnp.bfloat16


def mul(a, b):
    return lax.dot_general(
        a, b, (((1,), (0,)), ((), ())), precision=exact, preferred_element_type=f32
    )


def mul_t(a, b):
    return lax.dot_general(
        a, b, (((1,), (1,)), ((), ())), precision=exact, preferred_element_type=f32
    )


def split(x):
    high = x.astype(bf16)
    rest = x - high.astype(f32)
    middle = rest.astype(bf16)
    return high, middle, (rest - middle.astype(f32)).astype(bf16)


def parts_of(a):
    return jnp.concatenate(split(a), axis=0)


def mul_few(stack, b, over=0):
    rows = stack.shape[0] // 3
    total = None
    for i, part in enumerate(split(b)):
        found = lax.dot_general(
            stack[: rows * (3 - i)],
            part,
            (((1,), (over,)), ((), ())),
            preferred_element_type=f32,
        )
        for j in range(3 - i):
            piece = found[rows * j : rows * j + rows]
            total = piece if total is None else total + piece
    return total


def deep_parts_of(a):
    high, middle, low = split(a)
    return jnp.concatenate([low, middle, high, middle, high, high], axis=1)


def mul_deep(stack, b):
    high, middle, low = split(b)
    right = jnp.concatenate([high, middle, low, high, middle, high], axis=0)
    return lax.dot_general(
        stack, right, (((1,), (0,)), ((), ())), preferred_element_type=f32
    )


def inverse_factor(wide):
    row = lax.broadcasted_iota(jnp.int32, (K, LANES), 0)
    lane = lax.broadcasted_iota(jnp.int32, (K, LANES), 1)
    work = jnp.where(lane < K, wide, jnp.where(lane == row + K, f32(1.0), f32(0.0)))
    done = []
    for start in range(0, K, 8):
        size = K - start
        at = lax.broadcasted_iota(jnp.int32, (size, LANES), 0)
        spread = [
            jnp.broadcast_to(work[:, start + j : start + j + 1], (size, LANES))
            for j in range(8)
        ]
        for j in range(8):
            inverse = 1.0 / spread[j][j : j + 1, :]
            column = jnp.where(at > j, spread[j], f32(0.0))
            for l in range(j + 1, 8):
                spread[l] = spread[l] - column * (spread[l][j : j + 1, :] * inverse)
            work = work - column * (work[j : j + 1, :] * inverse)
        done.append(work[:8])
        work = work[8:]
    work = jnp.concatenate(done, axis=0)
    pivots = jnp.sum(jnp.where(lane == row, work, f32(0.0)), axis=1, keepdims=True)
    work = work * (1.0 / jnp.sqrt(pivots))
    return pltpu.roll(work, LANES - K, 1)[:, :K]


def unpack_gram(packed):
    return jnp.concatenate(
        [packed] + [pltpu.roll(packed, LANES - K * a, 1) for a in range(1, 4)], axis=0
    )


def pack_rows(wide):
    packed = wide[:8]
    for a in range(1, 4):
        packed = packed + pltpu.roll(wide[8 * a : 8 * a + 8], K * a, 1)
    return packed


def pack_gram(weights_t):
    rest = jnp.zeros((LANES - K, LANES), f32)
    return pack_rows(mul_t(weights_t, jnp.concatenate([weights_t, rest], axis=0)))


def total_of(arrived):
    total = arrived[0]
    for j in range(1, arrived.shape[0]):
        total = total + arrived[j]
    return total


def call(body, outs, args, scratch=(), limit=8, anywhere=(), still=(), alias=None, out_any={}):
    specs = []
    for i, a in enumerate(args):
        space = pltpu.SMEM if a.ndim == 1 else pltpu.VMEM
        space = pl.ANY if i in anywhere else pltpu.HBM if i in still else space
        specs.append(pl.BlockSpec(memory_space=space))
    many = isinstance(outs, list)
    shapes = [
        jax.ShapeDtypeStruct(s, f32) if isinstance(s, tuple) else s
        for s in (outs if many else [outs])
    ]
    out_specs = [
        pl.BlockSpec(memory_space=out_any.get(i, pltpu.VMEM))
        for i in range(len(shapes))
    ]
    return pl.pallas_call(
        body,
        out_shape=shapes if many else shapes[0],
        in_specs=specs,
        out_specs=out_specs if many else out_specs[0],
        scratch_shapes=list(scratch),
        input_output_aliases=alias or {},
        compiler_params=pltpu.CompilerParams(vmem_limit_bytes=limit * 1024 * 1024),
        cost_estimate=pl.CostEstimate(
            flops=1_000_000, bytes_accessed=1_000_000, transcendentals=0
        ),
    )(*args)


def rows_of(halves, start, size):
    return jnp.concatenate(
        [half[pl.ds(start, size, stride=8), :] for half in halves], axis=1
    )


def start_body(
    day,
    observed_hbm,
    missing_hbm,
    land_hbm,
    basis_hbm,
    out_hbm,
    observed,
    missing,
    land,
    basis_t,
    half_0,
    half_1,
    out,
    arrivals,
    sent,
):
    parts = 4
    days = observed.shape[0]
    size = days // parts
    small = [
        pltpu.make_async_copy(land_hbm, land, arrivals.at[2 * parts]),
        pltpu.make_async_copy(basis_hbm, basis_t, arrivals.at[2 * parts + 1]),
    ]
    for copy in small:
        copy.start()
    copies = []
    for i in range(parts):
        at = pl.ds(size * i, size)
        for c, (source, target) in enumerate(
            ((missing_hbm, missing), (observed_hbm, observed))
        ):
            copies.append(
                pltpu.make_async_copy(
                    source.at[at], target.at[at], arrivals.at[2 * i + c]
                )
            )
            copies[-1].start()
    d = day[0]
    halves = (half_0, half_1)
    out[:, K:, :] = jnp.zeros((8, HALO, out.shape[2]), f32)
    for copy in small:
        copy.wait()
    ocean = 1.0 - land[...].astype(f32)
    for i in range(parts):
        copies[2 * i].wait()
        copies[2 * i + 1].wait()
        now = slice(size * i, size * i + size)
        for c, half in enumerate(halves):
            at = slice(LANES * c, LANES * c + LANES)
            tile = jnp.where(missing[now, :, at] == 1, f32(0.0), observed[now, :, at])
            tile = tile * ocean[None, :, at]
            half[8 * size * i : 8 * size * (i + 1), :] = tile.reshape(8 * size, LANES)
    low, high = jnp.maximum(d - 1, 0), jnp.minimum(d + 1, 7)
    for t in range(RADIUS):
        for target, source in ((low, t), (high, days - RADIUS + t)):
            tile = [half[8 * source : 8 * source + 8, :] for half in halves]
            out[target, K + 8 * t : K + 8 * t + 8, :] = jnp.concatenate(tile, axis=1)
    weights = parts_of(basis_t[...])
    copies = []
    for r in range(8):
        out[r, :K, :] = mul_few(weights, rows_of(halves, r, days))
        copies.append(pltpu.make_async_copy(out.at[r], out_hbm.at[r], sent.at[r]))
        copies[-1].start()
    for copy in copies:
        copy.wait()


def turn_body(
    observed_hbm,
    missing_hbm,
    land,
    first_hbm,
    gap_hbm,
    observed,
    missing,
    half_0,
    half_1,
    mask_0,
    mask_1,
    first,
    gap,
    arrivals,
    sent,
):
    pairs = ((missing_hbm, missing), (observed_hbm, observed))
    copies = [
        pltpu.make_async_copy(source, target, arrivals.at[i])
        for i, (source, target) in enumerate(pairs)
    ]
    for copy in copies:
        copy.start()
    for copy in copies:
        copy.wait()
    days = missing.shape[0]
    ocean = 1.0 - land[...].astype(f32)
    halves, masks = (half_0, half_1), (mask_0, mask_1)
    for c in range(2):
        at = slice(LANES * c, LANES * c + LANES)
        absent = missing[:, :, at] == 1
        tile = jnp.where(absent, f32(0.0), observed[:, :, at]) * ocean[None, :, at]
        halves[c][...] = tile.reshape(8 * days, LANES)
        masks[c][...] = absent.astype(f32).reshape(8 * days, LANES)
    for r in range(8):
        first[r] = rows_of(halves, r, days)
        gap[r] = rows_of(masks, r, days).astype(bf16)
    copies = [
        pltpu.make_async_copy(first, first_hbm, sent.at[0]),
        pltpu.make_async_copy(gap, gap_hbm, sent.at[1]),
    ]
    for copy in copies:
        copy.start()
    for copy in copies:
        copy.wait()


def add_rows_body(arrived, out):
    total = arrived[0, :K, :]
    for j in range(1, arrived.shape[0]):
        total = total + arrived[j, :K, :]
    for j in range(out.shape[0]):
        out[j] = total


def add_rows_again_body(arrived, filled, out):
    del filled
    add_rows_body(arrived, out)


def add_all_body(arrived, out):
    total = total_of(arrived)
    for j in range(out.shape[0]):
        out[j] = total


def add_last_body(arrived, out, extra):
    total = total_of(arrived)
    for j in range(out.shape[0]):
        out[j] = total[:K]
    extra[...] = total[K:]


def factor_body(arrived, out):
    packed = arrived[0, K:, :LANES]
    for j in range(1, arrived.shape[0]):
        packed = packed + arrived[j, K:, :LANES]
    out[:, :K] = inverse_factor(unpack_gram(packed))
    out[:, K:] = jnp.zeros((K, LANES - K), f32)


def edges_of(modes, land, edge_low, edge_high):
    ocean = 1.0 - land[...].astype(f32)
    for edge, r in ((edge_low, 0), (edge_high, 7)):
        edge[:K, :] = modes[r]
        edge[K:, :] = jnp.broadcast_to(ocean[r : r + 1], (8, ocean.shape[1]))


class Products:
    def __init__(self, count):
        self.count = count
        self.totals = [jnp.zeros((count, K * (3 - i)), f32) for i in range(3)]

    def add(self, few, many):
        stack = parts_of(few)
        for i, part in enumerate(split(many)):
            self.totals[i] = self.totals[i] + lax.dot_general(
                part,
                stack[: K * (3 - i)],
                (((1,), (1,)), ((), ())),
                preferred_element_type=f32,
            )

    def result(self):
        found = None
        for i, total in enumerate(self.totals):
            tall = ((0, 2 * LANES - self.count), (0, LANES - total.shape[1]))
            total = jnp.pad(total, tall).T
            for j in range(3 - i):
                piece = total[K * j : K * j + K]
                found = piece if found is None else found + piece
        return found


def project_again_body(modes, filled, land, factor, out, edge_low, edge_high):
    cols = modes.shape[2]
    wide = jnp.concatenate([modes[r] for r in range(8)], axis=1)
    wide = mul_deep(deep_parts_of(factor[:, :K]), wide)
    products = Products(LANES + K)
    for r in range(8):
        modes_u = wide[:, cols * r : cols * r + cols]
        products.add(modes_u, jnp.concatenate([filled[r], modes_u], axis=0))
    total = products.result()
    packed = pack_rows(total[:, LANES:])
    for j in range(out.shape[0]):
        out[j, :K, :] = total[:, :LANES]
        out[j, K:, :] = packed
    edges_of(modes, land, edge_low, edge_high)


def project_body(
    day, arrived, modes, filled, land, out, edge_low, edge_high, halo_0, halo_1
):
    d = day[0]
    low = arrived[jnp.maximum(d - 1, 0), K : K + HALO, :]
    high = arrived[jnp.minimum(d + 1, 7), K : K + HALO, :]
    low = jnp.where(d > 0, low, f32(0.0))
    high = jnp.where(d < 7, high, f32(0.0))
    cols = modes.shape[2]
    for c, halo in enumerate((halo_0, halo_1)):
        halo[:HALO, :] = low[:, LANES * c : LANES * c + LANES]
        halo[HALO : 2 * HALO, :] = high[:, LANES * c : LANES * c + LANES]
        halo[2 * HALO :, :] = jnp.zeros((64 - 2 * HALO, LANES), f32)
    pad = jnp.zeros((8, cols), f32)
    products = Products(LANES + K + 16)
    for r in range(8):
        modes_u = modes[r]
        days_near = rows_of((halo_0, halo_1), r, 8)
        right = jnp.concatenate([filled[r], modes_u, days_near, pad], axis=0)
        products.add(modes_u, right)
    total = products.result()
    extra = total[:, LANES:]
    packed = extra[:16] + pltpu.roll(extra[16:], 64, 1)
    for j in range(out.shape[0]):
        out[j, :K, :] = total[:, :LANES]
        out[j, K:, :] = packed
    edges_of(modes, land, edge_low, edge_high)


def smooth_body(modes, above, below, land, out):
    cols = out.shape[2]
    lane = lax.broadcasted_iota(jnp.int32, (1, cols), 1)
    ocean = 1.0 - land[...].astype(f32)
    rows = [above[:K, :]] + [modes[r] for r in range(8)] + [below[:K, :]]
    flags = (
        [above[K : K + 1, :]]
        + [ocean[r : r + 1] for r in range(8)]
        + [below[K : K + 1, :]]
    )
    for r in range(8):
        here, flag = rows[r + 1], flags[r + 1]
        left = jnp.where(lane > 0, pltpu.roll(flag, 1, 1), f32(0.0))
        right = jnp.where(lane < cols - 1, pltpu.roll(flag, cols - 1, 1), f32(0.0))
        up, down = flags[r], flags[r + 2]
        centre = 1.0 - smoothing * (up + down + left + right)
        spread = (
            up * rows[r]
            + down * rows[r + 2]
            + left * pltpu.roll(here, 1, 1)
            + right * pltpu.roll(here, cols - 1, 1)
        )
        out[r] = centre * here + smoothing * spread


def refill_body(
    day,
    arrived,
    band,
    smooth_hbm,
    first,
    gap,
    land,
    filled_hbm,
    out,
    smooth,
    filled,
    arrivals,
    sent,
):
    def start(source, target, semaphore):
        copy = pltpu.make_async_copy(source, target, semaphore)
        copy.start()
        return copy

    waits = [start(smooth_hbm, smooth, arrivals.at[0])]
    total = total_of(arrived)
    extra = jnp.concatenate([total[K:], pltpu.roll(total[K:], 64, 1)], axis=0)
    raw = jnp.concatenate([total[:K], extra], axis=1)
    tempered_t = mul(raw, band[: 2 * LANES, :]).T
    factor = inverse_factor(extra)
    weights_t = mul(factor, total[:K])
    mixed = deep_parts_of(mul(tempered_t, mul(factor.T, factor)))
    weights = parts_of(weights_t)
    cols = filled.shape[2]
    packed = pack_gram(weights_t)
    for j in range(8):
        out[j, K:, :LANES] = packed
        out[j, K:, LANES:] = jnp.zeros((8, cols - LANES), f32)
    ocean = 1.0 - land[...].astype(f32)
    for copy in waits:
        copy.wait()
    sends = []
    for r in range(0, 8, 2):
        for q in (r, r + 1):
            surface = mul_deep(mixed, smooth[q])
            absent = gap[q].astype(f32) == 1
            now = jnp.where(absent, surface * ocean[q : q + 1], first[q])
            filled[q] = now
            out[q, :K, :] = mul_few(weights, now)
        for q in (r, r + 1):
            sends.append(start(filled.at[q], filled_hbm.at[q], sent.at[q]))
    for copy in sends:
        copy.wait()


def last_weights_body(raw, extra, band, scale, mixed, right, factor):
    tempered_t = mul(raw[0], band[:LANES, :]).T
    found = inverse_factor(unpack_gram(extra[...]))
    inner = mul(found.T, mul(found, scale[:, :K]))
    mixed[...] = mul(tempered_t, inner)
    right[...] = inner
    factor[...] = found


def last_fill_body(mixed, smooth, observed, missing, land, out, *halves):
    days = observed.shape[0]
    ocean = 1.0 - land[...].astype(f32)
    mix = deep_parts_of(mixed[...])
    for r in range(8):
        surface = mul_deep(mix, smooth[r])
        for c, half in enumerate(halves):
            half[pl.ds(r, days, stride=8), :] = surface[:, LANES * c : LANES * c + LANES]
    for c, half in enumerate(halves):
        at = slice(LANES * c, LANES * c + LANES)
        surface = half[...].reshape(days, 8, LANES)
        value = jnp.where(missing[:, :, at] == 1, surface, observed[:, :, at])
        out[:, :, at] = value * ocean[None, :, at]


def finish_body(
    day,
    arrived,
    band,
    factor,
    right,
    mixed,
    smooth,
    observed_low,
    observed_high,
    missing_low,
    missing_high,
    land,
    filled_in,
    basis_t,
    filled,
    edges,
    halves,
    sent,
):
    del filled_in
    d = day[0]
    low = arrived[jnp.maximum(d - 1, 0)]
    high = arrived[jnp.minimum(d + 1, 7)]
    low = jnp.where(d > 0, low, f32(0.0))
    high = jnp.where(d < 7, high, f32(0.0))
    near = mul(jnp.concatenate([low, high], axis=1), band[2 * LANES :, :]).T
    near = mixed[...] + mul(near, right[...])
    days = near.shape[0]
    near = jnp.concatenate([near[:8], near[days - 8 :]], axis=0)
    near = deep_parts_of(near)
    for r in range(8):
        surface = mul_deep(near, smooth[r])
        for c in range(2):
            halves[c, pl.ds(r, 16, stride=8), :] = surface[:, LANES * c : LANES * c + LANES]
    ocean = 1.0 - land[...].astype(f32)
    sides = ((observed_low, missing_low), (observed_high, missing_high))
    copies = []
    for e, (observed, missing) in enumerate(sides):
        for c in range(2):
            at = slice(LANES * c, LANES * c + LANES)
            surface = halves[c, 64 * e : 64 * e + 64, :].reshape(8, 8, LANES)
            value = jnp.where(missing[:, :, at] == 1, surface, observed[:, :, at])
            edges[e, :, :, at] = value * ocean[None, :, at]
        copy = pltpu.make_async_copy(
            edges.at[e], filled.at[pl.ds((days - 8) * e, 8)], sent.at[e]
        )
        copy.start()
        copies.append(copy)
    found = factor[...]
    raw = [arrived[j] for j in range(arrived.shape[0])]
    weights_t = mul(found, jnp.concatenate(raw, axis=1))
    rest = jnp.zeros((LANES - K, weights_t.shape[1]), f32)
    gram = mul_few(
        parts_of(weights_t), jnp.concatenate([weights_t, rest], axis=0), 1
    )
    basis_t[...] = mul(inverse_factor(gram), mul(found, arrived[d]))
    for copy in copies:
        copy.wait()


def swap(blocks, axes):
    return lax.all_to_all(blocks, axes, 0, 0)


def near_rows(edge_low, edge_high):
    count = lax.axis_size(PIX)
    up = [(i, i + 1) for i in range(count - 1)]
    down = [(i + 1, i) for i in range(count - 1)]
    return lax.ppermute(edge_high, PIX, up), lax.ppermute(edge_low, PIX, down)


def band_of(day_weights):
    days = day_weights.shape[0]
    slot = lax.broadcasted_iota(jnp.int32, (4 * LANES, days), 0)
    target = lax.broadcasted_iota(jnp.int32, (4 * LANES, days), 1)
    first = LANES + K
    source = jnp.where(slot < days, slot, 4 * days)
    source = jnp.where((slot >= first) & (slot < first + 3), slot - first - 3, source)
    source = jnp.where(
        (slot >= first + 3) & (slot < first + 6), slot - first - 3 + days, source
    )
    source = jnp.where(slot >= 2 * LANES, slot - 3 * LANES, source)
    source = jnp.where(slot >= 3 * LANES, slot - 3 * LANES + days, source)
    taps = day_weights.T
    return sum(
        jnp.where(source - target + RADIUS == j, taps[j : j + 1], f32(0.0))
        for j in range(2 * RADIUS + 1)
    )


def per_device(observed, missing, land, basis_start, day_weights):
    days, rows, cols = observed.shape
    day = lax.axis_index(DAY).reshape(1)
    near, far = lax.axis_size(NEAR), lax.axis_size("y")
    halo = [pltpu.VMEM((64, LANES), f32)] * 2
    halves = [pltpu.VMEM((days * rows, LANES), f32)] * 2
    edge = (K + 8, cols)
    block = (rows, K, cols)

    def add_near(joint, edges):
        joint = call(add_all_body, (far,) + joint.shape[1:], (swap(joint, NEAR),))
        return lax.optimization_barrier((joint, *edges))

    def smooth_beside(joint, low, high, modes):
        above, below = near_rows(low, high)
        joint = swap(joint, "y")
        smooth = call(smooth_body, block, (modes, above, below, land))
        return lax.optimization_barrier((joint, smooth))

    slab = pltpu.VMEM((days, rows, cols), f32)
    turned = pltpu.VMEM((rows, days, cols), f32)
    mask = pltpu.VMEM((days, rows, cols), jnp.int32)

    part = call(
        start_body,
        (rows, K + HALO, cols),
        (day, observed, missing, land, basis_start.T),
        [
            slab,
            mask,
            pltpu.VMEM((rows, cols), jnp.int32),
            pltpu.VMEM((K, days), f32),
            *halves,
            pltpu.VMEM((rows, K + HALO, cols), f32),
            pltpu.SemaphoreType.DMA((10,)),
            pltpu.SemaphoreType.DMA((8,)),
        ],
        limit=56,
        anywhere=(1, 2, 3, 4),
        out_any={0: pl.ANY},
    )
    later, taps, part = lax.optimization_barrier((missing, day_weights, part))
    band = band_of(taps)
    first, gap = call(
        turn_body,
        [(rows, days, cols), jax.ShapeDtypeStruct((rows, days, cols), bf16)],
        (observed, later, land),
        [slab, mask, *halves, *halves, turned, pltpu.VMEM((rows, days, cols), bf16)]
        + [pltpu.SemaphoreType.DMA((2,))] * 2,
        limit=56,
        anywhere=(0, 1),
        out_any={0: pl.ANY, 1: pl.ANY},
    )
    arrived, first, gap, band = lax.optimization_barrier(
        (swap(part, DAY), first, gap, band)
    )
    modes = swap(call(add_rows_body, block, (arrived,)), DAY)
    joint, *edges = call(
        project_body,
        [(near, K + 16, LANES), edge, edge],
        (day, arrived, modes, first, land),
        halo,
    )
    above, below = near_rows(*edges)
    joint = swap(joint, NEAR)
    smooth = call(smooth_body, block, (modes, above, below, land))
    joint, smooth = lax.optimization_barrier((joint, smooth))
    joint = swap(call(add_all_body, (far,) + joint.shape[1:], (joint,)), "y")
    filled, part = call(
        refill_body,
        [pltpu.HBM((rows, days, cols), f32), (rows, K + 8, cols)],
        (day, joint, band, smooth, first, gap, land),
        [
            pltpu.VMEM(block, f32),
            turned,
            pltpu.SemaphoreType.DMA((1,)),
            pltpu.SemaphoreType.DMA((8,)),
        ],
        limit=12,
        anywhere=(3,),
        out_any={0: pltpu.HBM},
    )
    arrived = swap(part, DAY)
    modes = call(add_rows_again_body, block, (arrived, filled), still=(1,), limit=53)
    modes = swap(modes, DAY)
    factor = call(factor_body, (K, LANES), (arrived,))
    joint, *edges = call(
        project_again_body,
        [(near, K + 8, LANES), edge, edge],
        (modes, filled, land, factor),
    )
    joint, low, high = add_near(joint, edges)
    joint, smooth = smooth_beside(joint, low, high, modes)
    raw, extra = call(add_last_body, [(8, K, LANES), (8, LANES)], (joint,))
    arrived = swap(raw, DAY)
    mixed, right, found = call(
        last_weights_body,
        [(days, K), (K, K), (K, K)],
        (raw, extra, band, factor),
    )
    filled = call(
        last_fill_body,
        (days, rows, cols),
        (mixed, smooth, observed, missing, land),
        halves,
    )
    ends = (slice(0, 8), slice(days - 8, days))
    basis_t, filled = call(
        finish_body,
        [(K, days), (days, rows, cols)],
        (day, arrived, band, found, right, mixed, smooth)
        + tuple(observed[e] for e in ends)
        + tuple(missing[e] for e in ends)
        + (land, filled),
        [
            pltpu.VMEM((2, 8, rows, cols), f32),
            pltpu.VMEM((2, 128, LANES), f32),
            pltpu.SemaphoreType.DMA((2,)),
        ],
        anywhere=(12,),
        out_any={1: pl.ANY},
        alias={12: 1},
    )
    return filled, basis_t.T


def solution(mesh):
    fine = Mesh(mesh.devices.reshape(SIZES), ("zlo", "y", "core", "x", "zhi"))
    return jax.shard_map(
        per_device,
        mesh=fine,
        in_specs=(
            P(DAY, PIX, None),
            P(DAY, PIX, None),
            P(PIX, None),
            P(DAY, None),
            P(DAY, None),
        ),
        out_specs=(P(DAY, PIX, None), P(DAY, None)),
        check_vma=False,
    )
```

```python
import jax
import jax.numpy as jnp
from jax import lax
from jax.experimental import pallas as pl
from jax.experimental.pallas import tpu as pltpu
from jax.sharding import Mesh, PartitionSpec as P

RADIUS = 3
K = 32
LANES = 128
HALO = 8 * RADIUS

PIX = ("zlo", "y", "core")
DAY = ("x", "zhi")
NEAR = ("zlo", "core")
SIZES = (4, 8, 2, 4, 2)

exact = lax.Precision.HIGHEST
smoothing = 0.2
f32 = jnp.float32
bf16 = jnp.bfloat16


def mul(a, b):
    return lax.dot_general(
        a, b, (((1,), (0,)), ((), ())), precision=exact, preferred_element_type=f32
    )


def mul_t(a, b):
    return lax.dot_general(
        a, b, (((1,), (1,)), ((), ())), precision=exact, preferred_element_type=f32
    )


def split(x):
    high = x.astype(bf16)
    rest = x - high.astype(f32)
    middle = rest.astype(bf16)
    return high, middle, (rest - middle.astype(f32)).astype(bf16)


def parts_of(a):
    return jnp.concatenate(split(a), axis=0)


def mul_few(stack, b, over=0):
    rows = stack.shape[0] // 3
    total = None
    for i, part in enumerate(split(b)):
        found = lax.dot_general(
            stack[: rows * (3 - i)],
            part,
            (((1,), (over,)), ((), ())),
            preferred_element_type=f32,
        )
        for j in range(3 - i):
            piece = found[rows * j : rows * j + rows]
            total = piece if total is None else total + piece
    return total


def deep_parts_of(a):
    high, middle, low = split(a)
    return jnp.concatenate([low, middle, high, middle, high, high], axis=1)


def mul_deep(stack, b):
    high, middle, low = split(b)
    right = jnp.concatenate([high, middle, low, high, middle, high], axis=0)
    return lax.dot_general(
        stack, right, (((1,), (0,)), ((), ())), preferred_element_type=f32
    )


def inverse_factor(wide):
    row = lax.broadcasted_iota(jnp.int32, (K, LANES), 0)
    lane = lax.broadcasted_iota(jnp.int32, (K, LANES), 1)
    work = jnp.where(lane < K, wide, jnp.where(lane == row + K, f32(1.0), f32(0.0)))
    done = []
    for start in range(0, K, 8):
        size = K - start
        at = lax.broadcasted_iota(jnp.int32, (size, LANES), 0)
        spread = [
            jnp.broadcast_to(work[:, start + j : start + j + 1], (size, LANES))
            for j in range(8)
        ]
        for j in range(8):
            inverse = 1.0 / spread[j][j : j + 1, :]
            column = jnp.where(at > j, spread[j], f32(0.0))
            for l in range(j + 1, 8):
                spread[l] = spread[l] - column * (spread[l][j : j + 1, :] * inverse)
            work = work - column * (work[j : j + 1, :] * inverse)
        done.append(work[:8])
        work = work[8:]
    work = jnp.concatenate(done, axis=0)
    pivots = jnp.sum(jnp.where(lane == row, work, f32(0.0)), axis=1, keepdims=True)
    work = work * (1.0 / jnp.sqrt(pivots))
    return pltpu.roll(work, LANES - K, 1)[:, :K]


def unpack_gram(packed):
    return jnp.concatenate(
        [packed] + [pltpu.roll(packed, LANES - K * a, 1) for a in range(1, 4)], axis=0
    )


def pack_rows(wide):
    packed = wide[:8]
    for a in range(1, 4):
        packed = packed + pltpu.roll(wide[8 * a : 8 * a + 8], K * a, 1)
    return packed


def pack_gram(weights_t):
    rest = jnp.zeros((LANES - K, LANES), f32)
    return pack_rows(mul_t(weights_t, jnp.concatenate([weights_t, rest], axis=0)))


def total_of(arrived):
    total = arrived[0]
    for j in range(1, arrived.shape[0]):
        total = total + arrived[j]
    return total


def call(body, outs, args, scratch=(), limit=8, anywhere=(), still=(), alias=None, out_any={}):
    specs = []
    for i, a in enumerate(args):
        space = pltpu.SMEM if a.ndim == 1 else pltpu.VMEM
        space = pl.ANY if i in anywhere else pltpu.HBM if i in still else space
        specs.append(pl.BlockSpec(memory_space=space))
    many = isinstance(outs, list)
    shapes = [
        jax.ShapeDtypeStruct(s, f32) if isinstance(s, tuple) else s
        for s in (outs if many else [outs])
    ]
    out_specs = [
        pl.BlockSpec(memory_space=out_any.get(i, pltpu.VMEM))
        for i in range(len(shapes))
    ]
    return pl.pallas_call(
        body,
        out_shape=shapes if many else shapes[0],
        in_specs=specs,
        out_specs=out_specs if many else out_specs[0],
        scratch_shapes=list(scratch),
        input_output_aliases=alias or {},
        compiler_params=pltpu.CompilerParams(vmem_limit_bytes=limit * 1024 * 1024),
        cost_estimate=pl.CostEstimate(
            flops=1_000_000, bytes_accessed=1_000_000, transcendentals=0
        ),
    )(*args)


def rows_of(halves, start, size):
    return jnp.concatenate(
        [half[pl.ds(start, size, stride=8), :] for half in halves], axis=1
    )


def start_body(
    day,
    observed_hbm,
    missing_hbm,
    land_hbm,
    basis_hbm,
    out_hbm,
    observed,
    missing,
    land,
    basis_t,
    half_0,
    half_1,
    out,
    arrivals,
    sent,
):
    parts = 4
    days = observed.shape[0]
    size = days // parts
    small = [
        pltpu.make_async_copy(land_hbm, land, arrivals.at[2 * parts]),
        pltpu.make_async_copy(basis_hbm, basis_t, arrivals.at[2 * parts + 1]),
    ]
    for copy in small:
        copy.start()
    copies = []
    for i in range(parts):
        at = pl.ds(size * i, size)
        for c, (source, target) in enumerate(
            ((missing_hbm, missing), (observed_hbm, observed))
        ):
            copies.append(
                pltpu.make_async_copy(
                    source.at[at], target.at[at], arrivals.at[2 * i + c]
                )
            )
            copies[-1].start()
    d = day[0]
    halves = (half_0, half_1)
    out[:, K:, :] = jnp.zeros((8, HALO, out.shape[2]), f32)
    for copy in small:
        copy.wait()
    ocean = 1.0 - land[...].astype(f32)
    for i in range(parts):
        copies[2 * i].wait()
        copies[2 * i + 1].wait()
        now = slice(size * i, size * i + size)
        for c, half in enumerate(halves):
            at = slice(LANES * c, LANES * c + LANES)
            tile = jnp.where(missing[now, :, at] == 1, f32(0.0), observed[now, :, at])
            tile = tile * ocean[None, :, at]
            half[8 * size * i : 8 * size * (i + 1), :] = tile.reshape(8 * size, LANES)
    low, high = jnp.maximum(d - 1, 0), jnp.minimum(d + 1, 7)
    for t in range(RADIUS):
        for target, source in ((low, t), (high, days - RADIUS + t)):
            tile = [half[8 * source : 8 * source + 8, :] for half in halves]
            out[target, K + 8 * t : K + 8 * t + 8, :] = jnp.concatenate(tile, axis=1)
    weights = parts_of(basis_t[...])
    copies = []
    for r in range(8):
        out[r, :K, :] = mul_few(weights, rows_of(halves, r, days))
        copies.append(pltpu.make_async_copy(out.at[r], out_hbm.at[r], sent.at[r]))
        copies[-1].start()
    for copy in copies:
        copy.wait()


def turn_body(
    observed_hbm,
    missing_hbm,
    land,
    first_hbm,
    gap_hbm,
    observed,
    missing,
    half_0,
    half_1,
    mask_0,
    mask_1,
    first,
    gap,
    arrivals,
    sent,
):
    pairs = ((missing_hbm, missing), (observed_hbm, observed))
    copies = [
        pltpu.make_async_copy(source, target, arrivals.at[i])
        for i, (source, target) in enumerate(pairs)
    ]
    for copy in copies:
        copy.start()
    for copy in copies:
        copy.wait()
    days = missing.shape[0]
    ocean = 1.0 - land[...].astype(f32)
    halves, masks = (half_0, half_1), (mask_0, mask_1)
    for c in range(2):
        at = slice(LANES * c, LANES * c + LANES)
        absent = missing[:, :, at] == 1
        tile = jnp.where(absent, f32(0.0), observed[:, :, at]) * ocean[None, :, at]
        halves[c][...] = tile.reshape(8 * days, LANES)
        masks[c][...] = absent.astype(f32).reshape(8 * days, LANES)
    for r in range(8):
        first[r] = rows_of(halves, r, days)
        gap[r] = rows_of(masks, r, days).astype(bf16)
    copies = [
        pltpu.make_async_copy(first, first_hbm, sent.at[0]),
        pltpu.make_async_copy(gap, gap_hbm, sent.at[1]),
    ]
    for copy in copies:
        copy.start()
    for copy in copies:
        copy.wait()


def add_rows_body(arrived, out):
    total = arrived[0, :K, :]
    for j in range(1, arrived.shape[0]):
        total = total + arrived[j, :K, :]
    for j in range(out.shape[0]):
        out[j] = total


def add_rows_again_body(arrived, filled, out):
    del filled
    add_rows_body(arrived, out)


def add_all_body(arrived, out):
    total = total_of(arrived)
    for j in range(out.shape[0]):
        out[j] = total


def add_last_body(arrived, out, extra):
    total = total_of(arrived)
    for j in range(out.shape[0]):
        out[j] = total[:K]
    extra[...] = total[K:]


def factor_body(arrived, out):
    packed = arrived[0, K:, :LANES]
    for j in range(1, arrived.shape[0]):
        packed = packed + arrived[j, K:, :LANES]
    out[:, :K] = inverse_factor(unpack_gram(packed))
    out[:, K:] = jnp.zeros((K, LANES - K), f32)


def edges_of(modes, land, edge_low, edge_high):
    ocean = 1.0 - land[...].astype(f32)
    for edge, r in ((edge_low, 0), (edge_high, 7)):
        edge[:K, :] = modes[r]
        edge[K:, :] = jnp.broadcast_to(ocean[r : r + 1], (8, ocean.shape[1]))


class Products:
    def __init__(self, count):
        self.count = count
        self.totals = [jnp.zeros((count, K * (3 - i)), f32) for i in range(3)]

    def add(self, few, many):
        stack = parts_of(few)
        for i, part in enumerate(split(many)):
            self.totals[i] = self.totals[i] + lax.dot_general(
                part,
                stack[: K * (3 - i)],
                (((1,), (1,)), ((), ())),
                preferred_element_type=f32,
            )

    def result(self):
        found = None
        for i, total in enumerate(self.totals):
            tall = ((0, 2 * LANES - self.count), (0, LANES - total.shape[1]))
            total = jnp.pad(total, tall).T
            for j in range(3 - i):
                piece = total[K * j : K * j + K]
                found = piece if found is None else found + piece
        return found


def project_again_body(modes, filled, land, factor, out, edge_low, edge_high):
    cols = modes.shape[2]
    wide = jnp.concatenate([modes[r] for r in range(8)], axis=1)
    wide = mul_deep(deep_parts_of(factor[:, :K]), wide)
    products = Products(LANES + K)
    for r in range(8):
        modes_u = wide[:, cols * r : cols * r + cols]
        products.add(modes_u, jnp.concatenate([filled[r], modes_u], axis=0))
    total = products.result()
    packed = pack_rows(total[:, LANES:])
    for j in range(out.shape[0]):
        out[j, :K, :] = total[:, :LANES]
        out[j, K:, :] = packed
    edges_of(modes, land, edge_low, edge_high)


def project_body(
    day, arrived, modes, filled, land, out, edge_low, edge_high, halo_0, halo_1
):
    d = day[0]
    low = arrived[jnp.maximum(d - 1, 0), K : K + HALO, :]
    high = arrived[jnp.minimum(d + 1, 7), K : K + HALO, :]
    low = jnp.where(d > 0, low, f32(0.0))
    high = jnp.where(d < 7, high, f32(0.0))
    cols = modes.shape[2]
    for c, halo in enumerate((halo_0, halo_1)):
        halo[:HALO, :] = low[:, LANES * c : LANES * c + LANES]
        halo[HALO : 2 * HALO, :] = high[:, LANES * c : LANES * c + LANES]
        halo[2 * HALO :, :] = jnp.zeros((64 - 2 * HALO, LANES), f32)
    pad = jnp.zeros((8, cols), f32)
    products = Products(LANES + K + 16)
    for r in range(8):
        modes_u = modes[r]
        days_near = rows_of((halo_0, halo_1), r, 8)
        right = jnp.concatenate([filled[r], modes_u, days_near, pad], axis=0)
        products.add(modes_u, right)
    total = products.result()
    extra = total[:, LANES:]
    packed = extra[:16] + pltpu.roll(extra[16:], 64, 1)
    for j in range(out.shape[0]):
        out[j, :K, :] = total[:, :LANES]
        out[j, K:, :] = packed
    edges_of(modes, land, edge_low, edge_high)


def smooth_body(modes, above, below, land, out):
    cols = out.shape[2]
    lane = lax.broadcasted_iota(jnp.int32, (1, cols), 1)
    ocean = 1.0 - land[...].astype(f32)
    rows = [above[:K, :]] + [modes[r] for r in range(8)] + [below[:K, :]]
    flags = (
        [above[K : K + 1, :]]
        + [ocean[r : r + 1] for r in range(8)]
        + [below[K : K + 1, :]]
    )
    for r in range(8):
        here, flag = rows[r + 1], flags[r + 1]
        left = jnp.where(lane > 0, pltpu.roll(flag, 1, 1), f32(0.0))
        right = jnp.where(lane < cols - 1, pltpu.roll(flag, cols - 1, 1), f32(0.0))
        up, down = flags[r], flags[r + 2]
        centre = 1.0 - smoothing * (up + down + left + right)
        spread = (
            up * rows[r]
            + down * rows[r + 2]
            + left * pltpu.roll(here, 1, 1)
            + right * pltpu.roll(here, cols - 1, 1)
        )
        out[r] = centre * here + smoothing * spread


def refill_body(
    day,
    arrived,
    band,
    smooth_hbm,
    first,
    gap,
    land,
    filled_hbm,
    out,
    smooth,
    filled,
    arrivals,
    sent,
):
    def start(source, target, semaphore):
        copy = pltpu.make_async_copy(source, target, semaphore)
        copy.start()
        return copy

    waits = [start(smooth_hbm, smooth, arrivals.at[0])]
    total = total_of(arrived)
    extra = jnp.concatenate([total[K:], pltpu.roll(total[K:], 64, 1)], axis=0)
    raw = jnp.concatenate([total[:K], extra], axis=1)
    tempered_t = mul(raw, band[: 2 * LANES, :]).T
    factor = inverse_factor(extra)
    weights_t = mul(factor, total[:K])
    mixed = deep_parts_of(mul(tempered_t, mul(factor.T, factor)))
    weights = parts_of(weights_t)
    cols = filled.shape[2]
    packed = pack_gram(weights_t)
    for j in range(8):
        out[j, K:, :LANES] = packed
        out[j, K:, LANES:] = jnp.zeros((8, cols - LANES), f32)
    ocean = 1.0 - land[...].astype(f32)
    for copy in waits:
        copy.wait()
    sends = []
    for r in range(0, 8, 2):
        for q in (r, r + 1):
            surface = mul_deep(mixed, smooth[q])
            absent = gap[q].astype(f32) == 1
            now = jnp.where(absent, surface * ocean[q : q + 1], first[q])
            filled[q] = now
            out[q, :K, :] = mul_few(weights, now)
        for q in (r, r + 1):
            sends.append(start(filled.at[q], filled_hbm.at[q], sent.at[q]))
    for copy in sends:
        copy.wait()


def last_weights_body(raw, extra, band, scale, mixed, right, factor):
    tempered_t = mul(raw[0], band[:LANES, :]).T
    found = inverse_factor(unpack_gram(extra[...]))
    inner = mul(found.T, mul(found, scale[:, :K]))
    mixed[...] = mul(tempered_t, inner)
    right[...] = inner
    factor[...] = found


def last_fill_body(mixed, smooth, observed, missing, land, out, *halves):
    days = observed.shape[0]
    ocean = 1.0 - land[...].astype(f32)
    mix = deep_parts_of(mixed[...])
    for r in range(8):
        surface = mul_deep(mix, smooth[r])
        for c, half in enumerate(halves):
            half[pl.ds(r, days, stride=8), :] = surface[:, LANES * c : LANES * c + LANES]
    for c, half in enumerate(halves):
        at = slice(LANES * c, LANES * c + LANES)
        surface = half[...].reshape(days, 8, LANES)
        value = jnp.where(missing[:, :, at] == 1, surface, observed[:, :, at])
        out[:, :, at] = value * ocean[None, :, at]


def finish_body(
    day,
    arrived,
    band,
    factor,
    right,
    mixed,
    smooth,
    observed_low,
    observed_high,
    missing_low,
    missing_high,
    land,
    filled_in,
    basis_t,
    filled,
    edges,
    halves,
    sent,
):
    del filled_in
    d = day[0]
    low = arrived[jnp.maximum(d - 1, 0)]
    high = arrived[jnp.minimum(d + 1, 7)]
    low = jnp.where(d > 0, low, f32(0.0))
    high = jnp.where(d < 7, high, f32(0.0))
    near = mul(jnp.concatenate([low, high], axis=1), band[2 * LANES :, :]).T
    near = mixed[...] + mul(near, right[...])
    days = near.shape[0]
    near = jnp.concatenate([near[:8], near[days - 8 :]], axis=0)
    near = deep_parts_of(near)
    for r in range(8):
        surface = mul_deep(near, smooth[r])
        for c in range(2):
            halves[c, pl.ds(r, 16, stride=8), :] = surface[:, LANES * c : LANES * c + LANES]
    ocean = 1.0 - land[...].astype(f32)
    sides = ((observed_low, missing_low), (observed_high, missing_high))
    copies = []
    for e, (observed, missing) in enumerate(sides):
        for c in range(2):
            at = slice(LANES * c, LANES * c + LANES)
            surface = halves[c, 64 * e : 64 * e + 64, :].reshape(8, 8, LANES)
            value = jnp.where(missing[:, :, at] == 1, surface, observed[:, :, at])
            edges[e, :, :, at] = value * ocean[None, :, at]
        copy = pltpu.make_async_copy(
            edges.at[e], filled.at[pl.ds((days - 8) * e, 8)], sent.at[e]
        )
        copy.start()
        copies.append(copy)
    found = factor[...]
    raw = [arrived[j] for j in range(arrived.shape[0])]
    weights_t = mul(found, jnp.concatenate(raw, axis=1))
    rest = jnp.zeros((LANES - K, weights_t.shape[1]), f32)
    gram = mul_few(
        parts_of(weights_t), jnp.concatenate([weights_t, rest], axis=0), 1
    )
    basis_t[...] = mul(inverse_factor(gram), mul(found, arrived[d]))
    for copy in copies:
        copy.wait()


def swap(blocks, axes):
    return lax.all_to_all(blocks, axes, 0, 0)


def near_rows(edge_low, edge_high):
    count = lax.axis_size(PIX)
    up = [(i, i + 1) for i in range(count - 1)]
    down = [(i + 1, i) for i in range(count - 1)]
    return lax.ppermute(edge_high, PIX, up), lax.ppermute(edge_low, PIX, down)


def band_of(day_weights):
    days = day_weights.shape[0]
    slot = lax.broadcasted_iota(jnp.int32, (4 * LANES, days), 0)
    target = lax.broadcasted_iota(jnp.int32, (4 * LANES, days), 1)
    first = LANES + K
    source = jnp.where(slot < days, slot, 4 * days)
    source = jnp.where((slot >= first) & (slot < first + 3), slot - first - 3, source)
    source = jnp.where(
        (slot >= first + 3) & (slot < first + 6), slot - first - 3 + days, source
    )
    source = jnp.where(slot >= 2 * LANES, slot - 3 * LANES, source)
    source = jnp.where(slot >= 3 * LANES, slot - 3 * LANES + days, source)
    taps = day_weights.T
    return sum(
        jnp.where(source - target + RADIUS == j, taps[j : j + 1], f32(0.0))
        for j in range(2 * RADIUS + 1)
    )


def per_device(observed, missing, land, basis_start, day_weights):
    days, rows, cols = observed.shape
    day = lax.axis_index(DAY).reshape(1)
    near, far = lax.axis_size(NEAR), lax.axis_size("y")
    halo = [pltpu.VMEM((64, LANES), f32)] * 2
    halves = [pltpu.VMEM((days * rows, LANES), f32)] * 2
    edge = (K + 8, cols)
    block = (rows, K, cols)

    def add_near(joint, edges):
        joint = call(add_all_body, (far,) + joint.shape[1:], (swap(joint, NEAR),))
        return lax.optimization_barrier((joint, *edges))

    def smooth_beside(joint, low, high, modes):
        above, below = near_rows(low, high)
        joint = swap(joint, "y")
        smooth = call(smooth_body, block, (modes, above, below, land))
        return lax.optimization_barrier((joint, smooth))

    slab = pltpu.VMEM((days, rows, cols), f32)
    turned = pltpu.VMEM((rows, days, cols), f32)
    mask = pltpu.VMEM((days, rows, cols), jnp.int32)

    part = call(
        start_body,
        (rows, K + HALO, cols),
        (day, observed, missing, land, basis_start.T),
        [
            slab,
            mask,
            pltpu.VMEM((rows, cols), jnp.int32),
            pltpu.VMEM((K, days), f32),
            *halves,
            pltpu.VMEM((rows, K + HALO, cols), f32),
            pltpu.SemaphoreType.DMA((10,)),
            pltpu.SemaphoreType.DMA((8,)),
        ],
        limit=56,
        anywhere=(1, 2, 3, 4),
        out_any={0: pl.ANY},
    )
    later, taps, part = lax.optimization_barrier((missing, day_weights, part))
    band = band_of(taps)
    first, gap = call(
        turn_body,
        [(rows, days, cols), jax.ShapeDtypeStruct((rows, days, cols), bf16)],
        (observed, later, land),
        [slab, mask, *halves, *halves, turned, pltpu.VMEM((rows, days, cols), bf16)]
        + [pltpu.SemaphoreType.DMA((2,))] * 2,
        limit=56,
        anywhere=(0, 1),
        out_any={0: pl.ANY, 1: pl.ANY},
    )
    arrived, first, gap, band = lax.optimization_barrier(
        (swap(part, DAY), first, gap, band)
    )
    modes = swap(call(add_rows_body, block, (arrived,)), DAY)
    joint, *edges = call(
        project_body,
        [(near, K + 16, LANES), edge, edge],
        (day, arrived, modes, first, land),
        halo,
    )
    joint, low, high = add_near(joint, edges)
    joint, smooth = smooth_beside(joint, low, high, modes)
    filled, part = call(
        refill_body,
        [pltpu.HBM((rows, days, cols), f32), (rows, K + 8, cols)],
        (day, joint, band, smooth, first, gap, land),
        [
            pltpu.VMEM(block, f32),
            turned,
            pltpu.SemaphoreType.DMA((1,)),
            pltpu.SemaphoreType.DMA((8,)),
        ],
        limit=12,
        anywhere=(3,),
        out_any={0: pltpu.HBM},
    )
    arrived = swap(part, DAY)
    modes = call(add_rows_again_body, block, (arrived, filled), still=(1,), limit=53)
    modes = swap(modes, DAY)
    factor = call(factor_body, (K, LANES), (arrived,))
    joint, *edges = call(
        project_again_body,
        [(near, K + 8, LANES), edge, edge],
        (modes, filled, land, factor),
    )
    joint, low, high = add_near(joint, edges)
    joint = swap(joint, "y")
    raw, extra = call(add_last_body, [(8, K, LANES), (8, LANES)], (joint,))
    arrived = swap(raw, DAY)
    above, below = near_rows(low, high)
    smooth = call(smooth_body, block, (modes, above, below, land))
    mixed, right, found = call(
        last_weights_body,
        [(days, K), (K, K), (K, K)],
        (raw, extra, band, factor),
    )
    filled = call(
        last_fill_body,
        (days, rows, cols),
        (mixed, smooth, observed, missing, land),
        halves,
    )
    ends = (slice(0, 8), slice(days - 8, days))
    basis_t, filled = call(
        finish_body,
        [(K, days), (days, rows, cols)],
        (day, arrived, band, found, right, mixed, smooth)
        + tuple(observed[e] for e in ends)
        + tuple(missing[e] for e in ends)
        + (land, filled),
        [
            pltpu.VMEM((2, 8, rows, cols), f32),
            pltpu.VMEM((2, 128, LANES), f32),
            pltpu.SemaphoreType.DMA((2,)),
        ],
        anywhere=(12,),
        out_any={1: pl.ANY},
        alias={12: 1},
    )
    return filled, basis_t.T


def solution(mesh):
    fine = Mesh(mesh.devices.reshape(SIZES), ("zlo", "y", "core", "x", "zhi"))
    return jax.shard_map(
        per_device,
        mesh=fine,
        in_specs=(
            P(DAY, PIX, None),
            P(DAY, PIX, None),
            P(PIX, None),
            P(DAY, None),
            P(DAY, None),
        ),
        out_specs=(P(DAY, PIX, None), P(DAY, None)),
        check_vma=False,
    )
```
